32 devices in a mesh: groups: 2 (over y), zone: 4 (over z), scen: 2 (over x), hour: 2 (over core).
Axes of the slice: x: 2, y: 2, z: 4, core: 2. Of those that a mesh axis runs over, the one named last changes fastest.
Arguments:
- forcing: bfloat16 [1024, 48, 64], P(('groups', 'zone', 'scen', 'hour')), parts along dimension 0, may hold values from -3 to 3
- response: bfloat16 [48, 64, 8192], P('hour', None, ('groups', 'zone')), parts along dimension 2, may hold values from -0.75 to 0.75
- window_params: float32 [128, 64], P('groups'), parts along dimension 0, may hold values from 0.5 to 1.5
- building_map: int32 [8192], P(('groups', 'zone')), parts along dimension 0, may hold values from 0 to 1023
- owner_ids: int32 [2048], P('groups'), parts along dimension 0, may hold values from 0 to 63
- band_ids: int32 [48, 8192], P('hour', ('groups', 'zone')), parts along dimension 1, may hold values from 0 to 7
- floor_area: float32 [8192], P(('groups', 'zone')), parts along dimension 0, may hold values from 0.5 to 18, as said below
Outputs:
- sensitivity: float32 [128, 64], P(('groups', 'zone', 'scen', 'hour')), parts along dimension 0
- objective: float32 [2], P('groups'), parts along dimension 0
The draws below stay inside these ranges and needn't reach their ends.
There are 2 independent parts, one for each index of `groups`. The reference program is written for one: setup_inputs(seed, part) draws one part's arguments, and reference() takes and returns one part's arrays. A program takes and returns all parts, laid end to end along the dimension named above; each array names one. Nothing has to cross between parts.
Inputs may be any that keep to these rules, and one draw needn't show every extreme that they name: `floor_area`: floor areas are positive.
All inputs are finite; a program needn't handle non-finite values.
Results may differ from the reference program's by a relative error of at most 0.0006.
Values may be sent and summed in bfloat16 or wider, within the bound.
No kernel may reach another device: no remote copies, remote signals or barrier semaphores. Data moves between devices by JAX's collectives and lax.ppermute only.
A program may use at most 128 MiB of HBM per device.

```python
import math
import jax
import jax.numpy as jnp
from jax import lax

WINDOW_COUNT = 64
BANDS = 8
HOURS = 48
SCENARIOS = 512
ZONES = 4096
DESIGNS = 64
BUILDINGS = 1024


def draw_floor_area(key, part):
    position = jnp.arange(ZONES).astype(jnp.float32) / (ZONES - 1)
    trend = jnp.exp(math.log(3.0) * position)
    noise = jnp.exp(jax.random.uniform(key, (ZONES,), jnp.float32, math.log(0.5), math.log(2.0)))
    return (trend * noise).astype(jnp.float32)


def set_ends(drawn, key, low, largest):
    longest = drawn.shape.index(max(drawn.shape))
    spots = []
    for shift in (0, 1):
        where = [jax.random.randint(jax.random.fold_in(key, axis), (), 0, length) for axis, length in enumerate(drawn.shape)]
        where[longest] = (where[longest] + shift) % drawn.shape[longest]
        spots.append(tuple(where))
    return drawn.at[spots[0]].set(low).at[spots[1]].set(largest)


def block_levels(own_key, extent, pieces, low, top_value):
    factor_of = 1.0
    for dim, blocks in pieces:
        heights = jax.random.uniform(jax.random.fold_in(jax.random.fold_in(own_key, 6), dim), (blocks,), jnp.float32, low / len(pieces), top_value / len(pieces))
        factor_of = factor_of * jnp.repeat(jnp.exp(heights), extent[dim] // blocks).reshape((-1,) + (1,) * (len(extent) - 1 - dim))
    return factor_of


def gaussian(key, shape, deviation, bound, shards=(), kind=jnp.bfloat16):
    array = deviation * jax.random.normal(key, shape, jnp.float32)
    if shards:
        array = array * block_levels(key, shape, shards, -0.22, 0.18)
    return jnp.clip(array, -bound, bound).astype(kind)


def setup_inputs(seed: int = 0, part: int = 0) -> dict:
    seeds = jax.random.split(jax.random.key(seed), 8)
    own_keys = jax.random.split(jax.random.fold_in(seeds[7], part), 8)
    forcing = gaussian(own_keys[0], (SCENARIOS, HOURS, WINDOW_COUNT), 0.5, 3.0, ((0, 16),))
    response = gaussian(own_keys[1], (HOURS, WINDOW_COUNT, ZONES), WINDOW_COUNT ** -0.5, 0.75, ((0, 2), (2, 4)))
    window_params = jnp.clip(jax.random.uniform(own_keys[2], (DESIGNS, WINDOW_COUNT), jnp.float32, 0.5, 1.5), 0.5, 1.5)
    building_map = set_ends(jax.random.randint(own_keys[3], (ZONES,), 0, BUILDINGS), jax.random.fold_in(own_keys[3], 1), 0, BUILDINGS - 1).astype(jnp.int32)
    owner_ids = set_ends(jax.random.randint(own_keys[4], (BUILDINGS,), 0, DESIGNS), jax.random.fold_in(own_keys[4], 1), 0, DESIGNS - 1).astype(jnp.int32)
    band_ids = set_ends(jax.random.randint(own_keys[5], (HOURS, ZONES), 0, BANDS), jax.random.fold_in(own_keys[5], 1), 0, BANDS - 1).astype(jnp.int32)
    floor_area = draw_floor_area(jax.random.fold_in(jax.random.fold_in(seeds[7], part), 71), part)
    return dict(forcing=forcing, response=response, window_params=window_params, building_map=building_map, owner_ids=owner_ids, band_ids=band_ids, floor_area=floor_area)


SHARPNESS = 200.0

def reference(forcing, response, window_params, building_map, owner_ids, band_ids, floor_area):
    candidate_plan = owner_ids[building_map].astype(jnp.int32)
    zone_parameters = window_params[candidate_plan]
    lower_factor = lax.optimization_barrier((response.astype(jnp.float32) * zone_parameters.T[None, :, :]).astype(jnp.bfloat16))
    coeff_full = lower_factor.astype(jnp.float32)
    positions = jnp.arange(HOURS).astype(jnp.float32)
    occupant_level = 1.0 + 2.0 * positions / (HOURS - 1)
    zone_weight = occupant_level[:, None] * floor_area[None, :]
    weight_total = jnp.sum(floor_area) * jnp.sum(occupant_level)
    band_low = 0.25 * (band_ids.astype(jnp.float32) - 3.5) - 0.5
    band_high = band_low + 1.0
    blocks = forcing.reshape(SCENARIOS // 16, 16, HOURS, WINDOW_COUNT)
    response_full = response.astype(jnp.float32)

    def heat_of(record_elements):
        return jnp.einsum('shp,hpz->shz', record_elements.astype(jnp.float32), coeff_full)

    def loss_block(record_elements):
        thermal_demand = heat_of(record_elements)
        penalty = jax.nn.softplus(thermal_demand - band_high[None]) + jax.nn.softplus(band_low[None] - thermal_demand)
        return lax.optimization_barrier(jnp.sum(penalty * zone_weight[None], axis=(1, 2)))
    losses = lax.map(loss_block, blocks).reshape(SCENARIOS)
    scores = SHARPNESS * losses / weight_total
    peak_score = jnp.max(scores)
    exp_total = jnp.sum(jnp.exp(scores - peak_score))
    objective = ((peak_score + jnp.log(exp_total)) / SHARPNESS).reshape(1)
    scen_weight = jnp.exp(scores - peak_score) / exp_total / weight_total

    def grad_step(accumulated, inputs):
        record_elements, row_weight = inputs
        thermal_demand = heat_of(record_elements)
        slope = jax.nn.sigmoid(thermal_demand - band_high[None]) - jax.nn.sigmoid(band_low[None] - thermal_demand)
        adjoint = slope * row_weight[:, None, None] * zone_weight[None]
        adjoint = lax.optimization_barrier(adjoint.astype(jnp.bfloat16)).astype(jnp.float32)
        mixed = jnp.einsum('shp,shz->hpz', record_elements.astype(jnp.float32), adjoint)
        return (accumulated + lax.optimization_barrier(jnp.sum(response_full * mixed, axis=0)), None)
    zone_grad, unused = lax.scan(grad_step, jnp.zeros((WINDOW_COUNT, ZONES), jnp.float32), (blocks, scen_weight.reshape(SCENARIOS // 16, 16)))
    gain = math.sqrt(WINDOW_COUNT * ZONES * HOURS * DESIGNS)
    sensitivity = jax.ops.segment_sum(zone_grad.T, candidate_plan, num_segments=DESIGNS) * gain
    return (sensitivity, objective)
```

```python
import functools
import math

import jax
import jax.numpy as jnp
from jax import lax
from jax.experimental import pallas as pl
from jax.experimental.pallas import tpu as pltpu
from jax.sharding import PartitionSpec as P

SHARPNESS = 200.0
MINUS_LOG2_E = -1.0 / math.log(2.0)
EDGE = 2.0 * math.cosh(0.5)
LANES = 128
DEPTH = 128
ZONE_TILE = 256
VMEM = pl.BlockSpec(memory_space=pltpu.VMEM)
SMEM = pl.BlockSpec(memory_space=pltpu.SMEM)
F32 = jnp.float32
BF16 = jnp.bfloat16


def params(**kw):
    return pltpu.CompilerParams(vmem_limit_bytes=56 * 2**20, **kw)


def coeff_kernel(map_ref, owner_ref, wp_ref, band_ref, resp_ref, rhs_ref, plan_ref, zp_ref):
    width = wp_ref.shape[1]
    zones = resp_ref.shape[2]

    @pl.when(pl.program_id(0) == 0)
    def _():
        place = map_ref[...]
        row, lane = place // LANES, place % LANES

        def look(i, found):
            table = jnp.broadcast_to(owner_ref[pl.ds(i, 1), :], place.shape)
            here = jnp.take_along_axis(table, lane, axis=1, mode="promise_in_bounds")
            return jnp.where(row == i, here, found)

        plan = lax.fori_loop(0, owner_ref.shape[0], look, jnp.zeros_like(place))
        for r in range(plan.shape[0]):
            plan_ref[:, r * LANES : (r + 1) * LANES] = plan[r : r + 1, :]
        designs = wp_ref.shape[0]
        onehot = (
            lax.broadcasted_iota(jnp.int32, (designs, zones), 0) == plan_ref[...]
        ).astype(F32).astype(BF16)
        rest = wp_ref[...]
        total = jnp.zeros((width, zones), F32)
        for _ in range(3):
            part = rest.astype(BF16)
            rest = rest - part.astype(F32)
            total = total + lax.dot_general(
                part, onehot, (((0,), (0,)), ((), ())), preferred_element_type=F32
            )
        zp_ref[...] = total

    extra = lax.broadcasted_iota(jnp.int32, (DEPTH - width, zones), 0)
    for h in range(resp_ref.shape[0]):
        rhs_ref[h, :width, :] = (resp_ref[h].astype(F32) * zp_ref[...]).astype(BF16)
        middle = 0.25 * (band_ref[h].astype(F32) - 3.5)
        tail = jnp.where(extra == 0, -middle, jnp.where(extra == 1, 1.0, 0.0))
        rhs_ref[h, width:, :] = tail.astype(BF16)


def coefficients(building_map, owner_ids, window_params, band_ids, response):
    hours, width, zones = response.shape
    step = 6
    return pl.pallas_call(
        coeff_kernel,
        grid=(hours // step,),
        in_specs=[
            VMEM,
            VMEM,
            VMEM,
            pl.BlockSpec((step, 1, zones), lambda i: (i, 0, 0)),
            pl.BlockSpec((step, width, zones), lambda i: (i, 0, 0)),
        ],
        out_specs=[
            pl.BlockSpec((step, DEPTH, zones), lambda i: (i, 0, 0)),
            pl.BlockSpec((1, zones), lambda i: (0, 0)),
        ],
        out_shape=[
            jax.ShapeDtypeStruct((hours, DEPTH, zones), BF16),
            jax.ShapeDtypeStruct((1, zones), jnp.int32),
        ],
        scratch_shapes=[pltpu.VMEM((width, zones), F32)],
        compiler_params=params(),
        name="coefficients",
    )(
        building_map.reshape(-1, LANES),
        owner_ids.reshape(-1, LANES),
        window_params,
        band_ids.reshape(hours, 1, zones),
        response,
    )


def drivers(pair, second, fill):
    half = pair.shape[1] // 2
    lane = lax.broadcasted_iota(jnp.int32, pair.shape, 1)
    if second:
        pair = pltpu.roll(pair.astype(F32), half, 1).astype(BF16)
    rest = jnp.zeros(pair.shape, F32)
    for spot, value in enumerate(fill):
        rest = jnp.where(lane == half + spot, value, rest)
    return jnp.where(lane < half, pair, rest.astype(BF16))


def occupancy(hour, hours_total):
    return 1.0 + 2.0 * hour.astype(F32) / (hours_total - 1)


def loss_kernel(hours_total, last, core_ref, f_ref, rhs_ref, area_ref, *rest):
    if last:
        prior_ref, out_ref, acc_ref = rest
    else:
        out_ref, acc_ref = rest
    step = pl.program_id(0)
    hours_step = rhs_ref.shape[0]
    zones = rhs_ref.shape[2]
    hours_local = hours_step * pl.num_programs(0)
    core = core_ref[0]

    @pl.when(step == 0)
    def _():
        acc_ref[...] = jnp.zeros_like(acc_ref)

    def pair_step(j, carry):
        pair = f_ref[:, pl.ds(pl.multiple_of(j * LANES, LANES), LANES)]
        for k in range(2):
            h = 2 * j + k
            lhs = drivers(pair, k == 1, (1.0,))
            occ = occupancy(core * hours_local + step * hours_step + h, hours_total)
            for z in range(0, zones, ZONE_TILE):
                v = jnp.dot(lhs, rhs_ref[h, :, z : z + ZONE_TILE], preferred_element_type=F32)
                a = jnp.abs(v) * MINUS_LOG2_E
                q = jnp.exp2(a)
                pen = jnp.log2((q + EDGE) * q + 1.0) - a
                pen = pen * (area_ref[:, z : z + ZONE_TILE] * occ)
                part = pen[:, :LANES]
                for c in range(LANES, ZONE_TILE, LANES):
                    part = part + pen[:, c : c + LANES]
                acc_ref[...] += part
        return carry

    lax.fori_loop(0, hours_step // 2, pair_step, 0)

    @pl.when(step == pl.num_programs(0) - 1)
    def _():
        row = jnp.sum(acc_ref[...].T, axis=0, keepdims=True)
        if not last:
            out_ref[...] = jnp.broadcast_to(row, out_ref.shape)
        else:
            index = lax.broadcasted_iota(jnp.int32, out_ref.shape[1:], 0)
            first_hour = core * hours_local
            occ_sum = hours_local * 1.0 + (
                2.0 * (first_hour * hours_local + hours_local * (hours_local - 1) // 2)
            ).astype(F32) / (hours_total - 1)
            weight = jnp.sum(area_ref[...]) * occ_sum
            message = jnp.where(
                index == core,
                prior_ref[0:1, :],
                jnp.where(index == 1 - core, row, jnp.where(index == 2, weight, 0.0)),
            )
            for d in range(out_ref.shape[0]):
                out_ref[d] = message


def losses(core, f, offset, rhs, area, hours_total, prior=None, copies=0):
    hours, _, zones = rhs.shape
    step = 6
    rows = f.shape[0]
    last = prior is not None
    if last:
        out_shape = jax.ShapeDtypeStruct((copies, 8, rows), F32)
        out_spec = pl.BlockSpec((copies, 8, rows), lambda i, *_: (0, 0, 0))
    else:
        out_shape = jax.ShapeDtypeStruct((8, rows), F32)
        out_spec = pl.BlockSpec((8, rows), lambda i, *_: (0, 0))
    steps = hours // step
    return pl.pallas_call(
        functools.partial(loss_kernel, hours_total, last),
        grid_spec=pltpu.PrefetchScalarGridSpec(
            num_scalar_prefetch=1,
            grid=(steps,),
            in_specs=[
                pl.BlockSpec((rows, step * 64), lambda i, c: (0, c[0] * steps * offset + i)),
                pl.BlockSpec((step, DEPTH, zones), lambda i, c: (i, 0, 0)),
                pl.BlockSpec((1, zones), lambda i, c: (0, 0)),
            ]
            + ([pl.BlockSpec((8, rows), lambda i, c: (0, 0))] if last else []),
            out_specs=out_spec,
            scratch_shapes=[pltpu.VMEM((rows, LANES), F32)],
        ),
        out_shape=out_shape,
        compiler_params=params(),
        name="losses",
    )(core, f, rhs, area, *((prior,) if last else ()))


def slope_kernel(core_ref, f0_ref, f1_ref, rhs_ref, slope_ref, ft_ref):
    zones = rhs_ref.shape[2]
    rows = f0_ref.shape[0]
    for j in range(rhs_ref.shape[0] // 2):
        for b, f_ref in enumerate((f0_ref, f1_ref)):
            pair = f_ref[:, j * LANES : (j + 1) * LANES]
            ft_ref[j * LANES : (j + 1) * LANES, b * rows : (b + 1) * rows] = pair.T

    def pair_step(j, carry):
        at = pl.ds(pl.multiple_of(j * LANES, LANES), LANES)
        pair = jnp.concatenate([f0_ref[:, at], f1_ref[:, at]], axis=0)
        for k in range(2):
            h = 2 * j + k
            lhs = drivers((pair.astype(F32) * 0.5).astype(BF16), k == 1, (0.5, 0.25))
            for z in range(0, zones, ZONE_TILE):
                v = jnp.dot(lhs, rhs_ref[h, :, z : z + ZONE_TILE], preferred_element_type=F32)
                slope = jnp.tanh(v) + jnp.tanh(v - 0.5)
                slope_ref[h, :, z : z + ZONE_TILE] = slope.astype(BF16)
        return carry

    lax.fori_loop(0, rhs_ref.shape[0] // 2, pair_step, 0)


def slopes(core, straight, crossed, rhs):
    hours, _, zones = rhs.shape
    step = 4
    steps = hours // step
    rows = straight.shape[0]
    return pl.pallas_call(
        slope_kernel,
        grid_spec=pltpu.PrefetchScalarGridSpec(
            num_scalar_prefetch=1,
            grid=(steps,),
            in_specs=[
                pl.BlockSpec((rows, step * 64), lambda i, c: (0, c[0] * steps + i)),
                pl.BlockSpec((rows, step * 64), lambda i, c: (0, i)),
                pl.BlockSpec((step, DEPTH, zones), lambda i, c: (i, 0, 0)),
            ],
            out_specs=[
                pl.BlockSpec((step, 2 * rows, zones), lambda i, c: (i, 0, 0)),
                pl.BlockSpec((step * 64, 2 * rows), lambda i, c: (i, 0)),
            ],
        ),
        out_shape=[
            jax.ShapeDtypeStruct((hours, 2 * rows, zones), BF16),
            jax.ShapeDtypeStruct((hours * 64, 2 * rows), BF16),
        ],
        compiler_params=params(),
        name="slopes",
    )(core, straight, crossed, rhs)


def gradient_kernel(
    hours_total, gain, owners, core_ref, msg_ref, ft_ref, slope_ref, resp_ref, area_ref, plan_ref,
    out_ref, acc_ref, e_ref, scale_ref,
):
    step = pl.program_id(0)
    hours_step, width, zones = resp_ref.shape
    hours_local = hours_step * pl.num_programs(0)
    core = core_ref[0]

    @pl.when(step == 0)
    def _():
        acc_ref[...] = jnp.zeros_like(acc_ref)
        total = jnp.sum(msg_ref[...], axis=0)
        weight = jnp.max(total[2:3, :])
        score = total[0:2, :] * (SHARPNESS * math.log(2.0) / weight)
        peak = jnp.max(score)
        e = jnp.exp(score - peak)
        rows = e.shape[1]
        e_ref[:, :rows] = jnp.where(core == 0, e[0:1, :], e[1:2, :])
        e_ref[:, rows:] = jnp.where(core == 0, e[1:2, :], e[0:1, :])
        scale_ref[0] = peak
        scale_ref[1] = jnp.sum(e)
        scale_ref[2] = weight

    def hour_step(h, carry):
        occ = occupancy(core * hours_local + step * hours_step + h, hours_total)
        ft = ft_ref[pl.ds(pl.multiple_of(h * width, width), width), :].astype(F32)
        ft = ft * (e_ref[...] * occ)
        high = ft.astype(BF16)
        low = (ft - high.astype(F32)).astype(BF16)
        both = jnp.concatenate([high, low], axis=0)
        for z in range(0, zones, ZONE_TILE):
            at = slice(z, z + ZONE_TILE)
            mixed = jnp.dot(both, slope_ref[h, :, at], preferred_element_type=F32)
            mixed = mixed[:width] + mixed[width:]
            acc_ref[:, at] += resp_ref[h, :, at].astype(F32) * mixed
        return carry

    lax.fori_loop(0, hours_step, hour_step, 0)

    @pl.when(step == pl.num_programs(0) - 1)
    def _():
        grad = acc_ref[...] * area_ref[...]
        blocks = out_ref.shape[0]
        pad = out_ref.shape[1]
        index = lax.broadcasted_iota(jnp.int32, (blocks * pad, zones), 0)
        within = index % pad
        design = jnp.where(within < owners, (index // pad) * owners + within, -1)
        onehot = (design == plan_ref[...]).astype(F32)
        sens = lax.dot_general(
            onehot,
            grad,
            (((1,), (1,)), ((), ())),
            precision=lax.Precision.HIGHEST,
            preferred_element_type=F32,
        )
        sens = sens * (0.5 * gain / scale_ref[2])
        out_ref[:, :, :width] = sens.reshape(blocks, pad, width)
        lane = lax.broadcasted_iota(jnp.int32, (blocks, pad, LANES - width), 2)
        out_ref[:, :, width:] = jnp.where(lane == 0, scale_ref[0], scale_ref[1])


def gradient(core, msg, ft, slope, response, area, plan, hours_total, gain, devices, owners):
    hours, width, zones = response.shape
    step = 4
    scen = slope.shape[1]
    pad = -(-owners // 8) * 8
    return pl.pallas_call(
        functools.partial(gradient_kernel, hours_total, gain, owners),
        grid_spec=pltpu.PrefetchScalarGridSpec(
            num_scalar_prefetch=1,
            grid=(hours // step,),
            in_specs=[
                pl.BlockSpec(msg.shape, lambda i, c: (0, 0, 0)),
                pl.BlockSpec((step * width, scen), lambda i, c: (i, 0)),
                pl.BlockSpec((step, scen, zones), lambda i, c: (i, 0, 0)),
                pl.BlockSpec((step, width, zones), lambda i, c: (i, 0, 0)),
                pl.BlockSpec((1, zones), lambda i, c: (0, 0)),
                pl.BlockSpec((1, zones), lambda i, c: (0, 0)),
            ],
            out_specs=pl.BlockSpec((devices, pad, LANES), lambda i, c: (0, 0, 0)),
            scratch_shapes=[
                pltpu.VMEM((width, zones), F32),
                pltpu.VMEM((1, scen), F32),
                pltpu.SMEM((4,), F32),
            ],
        ),
        out_shape=jax.ShapeDtypeStruct((devices, pad, LANES), F32),
        compiler_params=params(),
        name="gradient",
    )(core, msg, ft, slope, response, area, plan)


def finish_kernel(scen_parts, width, parts_ref, sens_ref, objective_ref):
    parts = parts_ref[...]
    devices = parts.shape[0]
    peaks = parts[:, :, width : width + 1]
    totals = parts[:, :, width + 1 : width + 2]
    peak = jnp.max(peaks)
    scale = jnp.exp(peaks - peak)
    total = jnp.sum((scale * totals)[:, 0:1, :]) * (scen_parts / devices)
    summed = jnp.sum(parts[:, :, :width] * scale, axis=0) / total
    sens_ref[...] = summed[: sens_ref.shape[0]]
    log_total = jnp.max(jnp.log(jnp.full((8, LANES), total, F32)))
    objective_ref[0] = (peak + log_total) / SHARPNESS - 0.5


def on_device(forcing, response, window_params, building_map, owner_ids, band_ids, floor_area):
    hours, width, zones = response.shape
    hour_parts = lax.axis_size("hour")
    zone_parts = lax.axis_size("zone")
    scen_parts = lax.axis_size("scen")
    hours_total = hours * hour_parts
    core = lax.axis_index("hour").astype(jnp.int32).reshape(1)
    area = floor_area.reshape(1, zones)

    everyone = forcing.reshape(forcing.shape[0], hours_total * width)
    gathered = lax.all_gather(everyone, "zone", axis=0, tiled=True)
    half = hours * width
    leaving = lax.dynamic_slice_in_dim(gathered, (1 - core[0]) * half, half, axis=1)
    crossed = lax.ppermute(leaving, "hour", [(0, 1), (1, 0)])

    rhs, plan = coefficients(building_map, owner_ids, window_params, band_ids, response)
    first = losses(core, gathered, 1, rhs, area, hours_total)
    message = losses(
        core, crossed, 0, rhs, area, hours_total, prior=first, copies=zone_parts * hour_parts
    )
    slope, ft = slopes(core, gathered, crossed, rhs)
    shared = lax.all_to_all(message, ("zone", "hour"), split_axis=0, concat_axis=0, tiled=True)

    designs = window_params.shape[0]
    devices = zone_parts * scen_parts * hour_parts
    owners = designs // devices
    gain = math.sqrt(width * zones * zone_parts * hours_total * designs)
    parts = gradient(
        core, shared, ft, slope, response, area, plan, hours_total, gain, devices, owners
    )
    parts = lax.all_to_all(
        parts, ("zone", "scen", "hour"), split_axis=0, concat_axis=0, tiled=True
    )
    sensitivity, objective = pl.pallas_call(
        functools.partial(finish_kernel, scen_parts, width),
        in_specs=[VMEM],
        out_specs=[VMEM, SMEM],
        out_shape=[
            jax.ShapeDtypeStruct((owners, width), F32),
            jax.ShapeDtypeStruct((1,), F32),
        ],
        compiler_params=params(),
        name="finish",
    )(parts)
    return (sensitivity, objective)


def solution(mesh):
    in_specs = (
        P(("groups", "zone", "scen", "hour"), None, None),
        P("hour", None, ("groups", "zone")),
        P("groups", None),
        P(("groups", "zone")),
        P("groups"),
        P("hour", ("groups", "zone")),
        P(("groups", "zone")),
    )
    out_specs = (P(("groups", "zone", "scen", "hour"), None), P("groups"))
    return jax.shard_map(
        on_device, mesh=mesh, in_specs=in_specs, out_specs=out_specs, check_vma=False
    )
```

```python
import functools
import math

import jax
import jax.numpy as jnp
from jax import lax
from jax.experimental import pallas as pl
from jax.experimental.pallas import tpu as pltpu
from jax.sharding import PartitionSpec as P

SHARPNESS = 200.0
MINUS_LOG2_E = -1.0 / math.log(2.0)
EDGE = 2.0 * math.cosh(0.5)
LANES = 128
DEPTH = 128
ZONE_TILE = 256
VMEM = pl.BlockSpec(memory_space=pltpu.VMEM)
SMEM = pl.BlockSpec(memory_space=pltpu.SMEM)
F32 = jnp.float32
BF16 = jnp.bfloat16


def params():
    return pltpu.CompilerParams(vmem_limit_bytes=20 * 2**20)


def near(x):
    return pltpu.with_memory_space_constraint(x, pltpu.VMEM)


def call(kernel, name, outs, args, scratch=()):
    return pl.pallas_call(
        kernel,
        in_specs=[SMEM] + [VMEM] * (len(args) - 1),
        out_specs=[VMEM] * len(outs),
        out_shape=[pltpu.MemorySpace.VMEM(shape, kind) for shape, kind in outs],
        scratch_shapes=list(scratch),
        compiler_params=params(),
        name=name,
    )(args[0], *[near(a) for a in args[1:]])


def coeff_kernel(place_ref, map_ref, owner_ref, wp_ref, band_ref, resp_ref, rhs_ref, plan_ref, zp_ref):
    hours, width, zones = resp_ref.shape
    place = map_ref[...]
    row, lane = place // LANES, place % LANES

    def look(i, found):
        table = jnp.broadcast_to(owner_ref[pl.ds(i, 1), :], place.shape)
        here = jnp.take_along_axis(table, lane, axis=1, mode="promise_in_bounds")
        return jnp.where(row == i, here, found)

    plan = lax.fori_loop(0, owner_ref.shape[0], look, jnp.zeros_like(place))
    for r in range(plan.shape[0]):
        plan_ref[:, r * LANES : (r + 1) * LANES] = plan[r : r + 1, :]
    designs = wp_ref.shape[0]
    onehot = (
        lax.broadcasted_iota(jnp.int32, (designs, zones), 0) == plan_ref[...]
    ).astype(F32).astype(BF16)
    rest = wp_ref[...]
    total = jnp.zeros((width, zones), F32)
    for _ in range(3):
        part = rest.astype(BF16)
        rest = rest - part.astype(F32)
        total = total + lax.dot_general(
            part, onehot, (((0,), (0,)), ((), ())), preferred_element_type=F32
        )
    zp_ref[...] = total
    extra = lax.broadcasted_iota(jnp.int32, (16, zones), 0)
    blank = jnp.zeros((DEPTH - width - 16, zones), BF16)

    def hour_step(h, carry):
        rhs_ref[h, :width, :] = (resp_ref[h].astype(F32) * zp_ref[...]).astype(BF16)
        middle = 0.25 * (band_ref[pl.ds(h, 1), :].astype(F32) - 3.5)
        tail = jnp.where(extra == 0, -middle, jnp.where(extra == 1, 1.0, 0.0))
        rhs_ref[h, width : width + 16, :] = tail.astype(BF16)
        rhs_ref[h, width + 16 :, :] = blank
        return carry

    lax.fori_loop(0, hours, hour_step, 0)


def coefficients(place, building_map, owner_ids, window_params, band_ids, response):
    hours, width, zones = response.shape
    return call(
        coeff_kernel,
        "coefficients",
        [((hours, DEPTH, zones), BF16), ((1, zones), jnp.int32)],
        [
            place,
            building_map.reshape(-1, LANES),
            owner_ids.reshape(-1, LANES),
            window_params,
            band_ids,
            response,
        ],
        [pltpu.VMEM((width, zones), F32)],
    )


def drivers(pair, second, fill):
    half = pair.shape[1] // 2
    lane = lax.broadcasted_iota(jnp.int32, pair.shape, 1)
    if second:
        pair = pltpu.roll(pair.astype(F32), half, 1).astype(BF16)
    rest = jnp.zeros(pair.shape, F32)
    for spot, value in enumerate(fill):
        rest = jnp.where(lane == half + spot, value, rest)
    return jnp.where(lane < half, pair, rest.astype(BF16))


def occupancy(hour, hours_total):
    return 1.0 + 2.0 * hour.astype(F32) / (hours_total - 1)


def scan_kernel(kind, hours_total, chunks, zone_parts, copies, place_ref, *refs):
    with_loss, with_slope = "loss" in kind, "slope" in kind
    f_refs, refs = refs[:chunks], refs[chunks:]
    rhs_ref, area_ref, refs = refs[0], refs[1], refs[2:]
    if copies:
        prior_ref, refs = refs[0], refs[1:]
    if with_loss:
        out_ref, refs = refs[0], refs[1:]
    if with_slope:
        slope_ref, ft_ref, refs = refs[0], refs[1], refs[2:]
    if with_loss:
        acc_ref = refs[0]
        acc_ref[...] = jnp.zeros_like(acc_ref)
    hours, _, zones = rhs_ref.shape
    core = place_ref[0]

    def pair_step(j, carry):
        at = pl.ds(pl.multiple_of(j * LANES, LANES), LANES)
        pair = [f_ref[:, at] for f_ref in f_refs]
        pair = pair[0] if chunks == 1 else jnp.concatenate(pair, axis=0)
        if with_slope:
            ft_ref[at, :] = pair.T
        gathered = None
        for k in range(2):
            h = 2 * j + k
            if with_loss:
                lhs = drivers(pair, k == 1, (1.0,))
                occ = occupancy(core * hours + h, hours_total)
            else:
                lhs = drivers((pair.astype(F32) * 0.5).astype(BF16), k == 1, (0.5, 0.25))
            summed = None
            for z in range(0, zones, ZONE_TILE):
                v = jnp.dot(lhs, rhs_ref[h, :, z : z + ZONE_TILE], preferred_element_type=F32)
                if with_loss:
                    a = jnp.abs(v) * MINUS_LOG2_E
                    q = jnp.exp2(a)
                    pen = jnp.log2((q + EDGE) * q + 1.0) - a
                    pen = pen * area_ref[:, z : z + ZONE_TILE]
                    for c in range(0, ZONE_TILE, LANES):
                        piece = pen[:, c : c + LANES]
                        summed = piece if summed is None else summed + piece
                if with_slope:
                    x = v * 0.5 + 0.25 if with_loss else v
                    slope = jnp.tanh(x) + jnp.tanh(x - 0.5)
                    slope_ref[h, :, z : z + ZONE_TILE] = slope.astype(BF16)
            if with_loss:
                summed = summed * occ
                gathered = summed if gathered is None else gathered + summed
        if with_loss:
            acc_ref[...] += gathered
        return carry

    lax.fori_loop(0, hours // 2, pair_step, 0, unroll=2)

    if with_loss:
        row = jnp.sum(acc_ref[...].T, axis=0, keepdims=True)
        if not copies:
            out_ref[...] = jnp.broadcast_to(row, out_ref.shape)
        else:
            zone = place_ref[1]
            half_zones = zone_parts // 2
            chunk = row.shape[1] // half_zones
            occ_sum = hours * 1.0 + (
                2.0 * (core * hours * hours + hours * (hours - 1) // 2)
            ).astype(F32) / (hours_total - 1)
            weight = jnp.sum(area_ref[...]) * occ_sum
            message = jnp.zeros(out_ref.shape[1:], F32) + weight
            index = lax.broadcasted_iota(jnp.int32, message.shape, 0)
            blank = jnp.zeros((1, LANES - chunk), F32)
            for k in range(zone_parts):
                source = prior_ref[0:1, :] if k < half_zones else row
                first = (k % half_zones) * chunk
                piece = jnp.concatenate([source[:, first : first + chunk], blank], axis=1)
                message = jnp.where(index == (zone ^ k), piece, message)
            for d in range(copies):
                out_ref[d] = message


def scan(kind, place, drivers_in, rhs, area, hours_total, zone_parts, prior=None, copies=0):
    hours, _, zones = rhs.shape
    rows = sum(f.shape[0] for f in drivers_in)
    outs = []
    scratch = []
    if "loss" in kind:
        sublanes = -(-(zone_parts + 1) // 8) * 8
        outs.append(((copies, sublanes, LANES) if copies else (8, rows), F32))
        scratch.append(pltpu.VMEM((rows, LANES), F32))
    if "slope" in kind:
        outs.append(((hours, rows, zones), BF16))
        outs.append(((drivers_in[0].shape[1], rows), BF16))
    return call(
        functools.partial(scan_kernel, kind, hours_total, len(drivers_in), zone_parts, copies),
        kind,
        outs,
        [place, *drivers_in, rhs, area] + ([prior] if copies else []),
        scratch,
    )


def gradient_kernel(
    hours_total, gain, owners, zone_parts, place_ref, msg_ref, ft0_ref, ft1_ref, slope0_ref, slope1_ref,
    resp_ref, area_ref, plan_ref, out_ref, acc_ref, score_ref, e_ref,
):
    hours, width, zones = resp_ref.shape
    core, zone = place_ref[0], place_ref[1]
    chunk = e_ref.shape[1] // zone_parts
    total = jnp.sum(msg_ref[...], axis=0)
    weight = jnp.max(total[zone_parts : zone_parts + 1, :])
    score = total * (SHARPNESS * math.log(2.0) / weight)
    rows = lax.broadcasted_iota(jnp.int32, score.shape, 0)
    lanes = lax.broadcasted_iota(jnp.int32, score.shape, 1)
    valid = (rows < zone_parts) & (lanes < chunk)
    peak = jnp.max(jnp.where(valid, score, -jnp.inf))
    e = jnp.where(valid, jnp.exp(jnp.where(valid, score - peak, 0.0)), 0.0)
    exp_total = jnp.sum(e)
    score_ref[...] = e
    for k in range(zone_parts):
        piece = score_ref[pl.ds(zone ^ k, 1), :]
        e_ref[:, k * chunk : (k + 1) * chunk] = piece[:, :chunk]
    acc_ref[...] = jnp.zeros_like(acc_ref)

    def hour_step(h, carry):
        occ = occupancy(core * hours + h, hours_total)
        at = pl.ds(pl.multiple_of(h * width, width), width)
        ft = jnp.concatenate([ft0_ref[at, :], ft1_ref[at, :]], axis=1).astype(F32)
        ft = ft * (e_ref[...] * occ)
        high = ft.astype(BF16)
        low = (ft - high.astype(F32)).astype(BF16)
        both = jnp.concatenate([high, low], axis=0)
        for z in range(0, zones, ZONE_TILE):
            at = slice(z, z + ZONE_TILE)
            kept = jnp.concatenate([slope0_ref[h, :, at], slope1_ref[h, :, at]], axis=0)
            mixed = jnp.dot(both, kept, preferred_element_type=F32)
            mixed = mixed[:width] + mixed[width:]
            acc_ref[:, at] += resp_ref[h, :, at].astype(F32) * mixed
        return carry

    lax.fori_loop(0, hours, hour_step, 0, unroll=2)

    grad = acc_ref[...] * area_ref[...]
    blocks, pad, _ = out_ref.shape
    index = lax.broadcasted_iota(jnp.int32, (blocks * pad, zones), 0)
    within = index % pad
    design = jnp.where(within < owners, (index // pad) * owners + within, -1)
    onehot = (design == plan_ref[...]).astype(F32).astype(BF16)
    sens = jnp.zeros((blocks * pad, width), F32)
    for _ in range(3):
        part = grad.astype(BF16)
        grad = grad - part.astype(F32)
        sens = sens + lax.dot_general(
            onehot, part, (((1,), (1,)), ((), ())), preferred_element_type=F32
        )
    sens = sens * (0.5 * gain / weight)
    out_ref[:, :, :width] = sens.reshape(blocks, pad, width)
    lane = lax.broadcasted_iota(jnp.int32, (blocks, pad, LANES - width), 2)
    out_ref[:, :, width:] = jnp.where(lane == 0, peak, exp_total)


def finish_kernel(scen_parts, width, parts_ref, sens_ref, objective_ref):
    parts = parts_ref[...]
    devices = parts.shape[0]
    peaks = parts[:, :, width : width + 1]
    totals = parts[:, :, width + 1 : width + 2]
    peak = jnp.max(peaks)
    scale = jnp.exp(peaks - peak)
    total = jnp.sum((scale * totals)[:, 0:1, :]) * (scen_parts / devices)
    summed = jnp.sum(parts[:, :, :width] * scale, axis=0) / total
    sens_ref[...] = summed[: sens_ref.shape[0]]
    log_total = jnp.max(jnp.log(jnp.full((8, LANES), total, F32)))
    objective_ref[0] = (peak + log_total) / SHARPNESS - 0.5


def swapped(x, axis, size, step):
    return lax.ppermute(x, axis, [(i, i ^ step) for i in range(size)])


def on_device(forcing, response, window_params, building_map, owner_ids, band_ids, floor_area):
    hours, width, zones = response.shape
    hour_parts = lax.axis_size("hour")
    zone_parts = lax.axis_size("zone")
    scen_parts = lax.axis_size("scen")
    hours_total = hours * hour_parts
    core, zone = lax.axis_index("hour"), lax.axis_index("zone")
    place = jnp.stack([core, zone]).astype(jnp.int32)
    area = floor_area.reshape(1, zones)

    half = hours * width
    everyone = forcing.reshape(forcing.shape[0], hours_total * width)
    keep = lax.dynamic_slice_in_dim(everyone, core * half, half, axis=1)
    leave = lax.dynamic_slice_in_dim(everyone, (1 - core) * half, half, axis=1)
    came = swapped(leave, "hour", hour_parts, 1)
    mine = jnp.concatenate(
        [jnp.where(core == 0, keep, came), jnp.where(core == 0, came, keep)], axis=0
    )
    if zone_parts == 4:
        halves = (
            [mine, swapped(mine, "zone", 4, 1)],
            [swapped(mine, "zone", 4, 2), swapped(mine, "zone", 4, 3)],
        )
    else:
        gathered = lax.all_gather(mine, "zone", axis=0)
        ordered = jnp.take(gathered, zone ^ jnp.arange(zone_parts), axis=0).reshape(2, -1, half)
        halves = ([ordered[0]], [ordered[1]])

    rhs, plan = coefficients(place, building_map, owner_ids, window_params, band_ids, response)
    common = (rhs, area, hours_total, zone_parts)
    first, slope0, ft0 = scan("loss_slope", place, halves[0], *common)
    (message,) = scan(
        "loss", place, halves[1], *common, prior=first, copies=zone_parts * hour_parts
    )
    shared = lax.all_to_all(message, ("zone", "hour"), split_axis=0, concat_axis=0, tiled=True)
    slope1, ft1 = scan("slope", place, halves[1], *common)

    designs = window_params.shape[0]
    devices = zone_parts * scen_parts * hour_parts
    owners = designs // devices
    pad = -(-owners // 8) * 8
    gain = math.sqrt(width * zones * zone_parts * hours_total * designs)
    (parts,) = call(
        functools.partial(gradient_kernel, hours_total, gain, owners, zone_parts),
        "gradient",
        [((devices, pad, LANES), F32)],
        [place, shared, ft0, ft1, slope0, slope1, response, area, plan],
        [
            pltpu.VMEM((width, zones), F32),
            pltpu.VMEM(shared.shape[1:], F32),
            pltpu.VMEM((1, ft0.shape[1] + ft1.shape[1]), F32),
        ],
    )
    parts = lax.all_to_all(
        parts, ("zone", "scen", "hour"), split_axis=0, concat_axis=0, tiled=True
    )
    sensitivity, objective = pl.pallas_call(
        functools.partial(finish_kernel, scen_parts, width),
        in_specs=[VMEM],
        out_specs=[VMEM, SMEM],
        out_shape=[
            jax.ShapeDtypeStruct((owners, width), F32),
            jax.ShapeDtypeStruct((1,), F32),
        ],
        compiler_params=params(),
        name="finish",
    )(near(parts))
    return (sensitivity, objective)


def solution(mesh):
    in_specs = (
        P(("groups", "zone", "scen", "hour"), None, None),
        P("hour", None, ("groups", "zone")),
        P("groups", None),
        P(("groups", "zone")),
        P("groups"),
        P("hour", ("groups", "zone")),
        P(("groups", "zone")),
    )
    out_specs = (P(("groups", "zone", "scen", "hour"), None), P("groups"))
    return jax.shard_map(
        on_device, mesh=mesh, in_specs=in_specs, out_specs=out_specs, check_vma=False
    )
```

```python
import functools
import math

import jax
import jax.numpy as jnp
from jax import lax
from jax.experimental import pallas as pl
from jax.experimental.pallas import tpu as pltpu
from jax.sharding import PartitionSpec as P

SHARPNESS = 200.0
MINUS_LOG2_E = -1.0 / math.log(2.0)
EDGE = 2.0 * math.cosh(0.5)
LANES = 128
DEPTH = 128
ZONE_TILE = 256
VMEM = pl.BlockSpec(memory_space=pltpu.VMEM)
SMEM = pl.BlockSpec(memory_space=pltpu.SMEM)
F32 = jnp.float32
BF16 = jnp.bfloat16


def params():
    return pltpu.CompilerParams(vmem_limit_bytes=20 * 2**20)


def near(x):
    return pltpu.with_memory_space_constraint(x, pltpu.VMEM)


def call(kernel, name, outs, args, scratch=()):
    return pl.pallas_call(
        kernel,
        in_specs=[SMEM] + [VMEM] * (len(args) - 1),
        out_specs=[VMEM] * len(outs),
        out_shape=[pltpu.MemorySpace.VMEM(shape, kind) for shape, kind in outs],
        scratch_shapes=list(scratch),
        compiler_params=params(),
        name=name,
    )(args[0], *[near(a) for a in args[1:]])


def coeff_kernel(
    map_hbm, owner_hbm, wp_hbm, band_hbm, area_hbm, resp_hbm, rhs_ref, plan_ref, area_ref, resp_ref,
    map_ref, owner_ref, wp_ref, band_ref, zp_ref, sems, resp_sems,
):
    hours, width, zones = resp_ref.shape
    pieces = resp_sems.shape[0]
    span = hours // pieces
    small = [
        pltpu.make_async_copy(source, target, sems.at[i])
        for i, (source, target) in enumerate(
            (
                (map_hbm, map_ref),
                (owner_hbm, owner_ref),
                (wp_hbm, wp_ref),
                (band_hbm, band_ref),
                (area_hbm, area_ref),
            )
        )
    ]
    for copy in small:
        copy.start()
    large = []
    for i in range(pieces):
        part = pl.ds(i * span, span)
        large.append(
            pltpu.make_async_copy(resp_hbm.at[part], resp_ref.at[part], resp_sems.at[i])
        )
        large[-1].start()
    for copy in small:
        copy.wait()
    place = map_ref[...]
    row, lane = place // LANES, place % LANES

    def look(i, found):
        table = jnp.broadcast_to(owner_ref[pl.ds(i, 1), :], place.shape)
        here = jnp.take_along_axis(table, lane, axis=1, mode="promise_in_bounds")
        return jnp.where(row == i, here, found)

    plan = lax.fori_loop(0, owner_ref.shape[0], look, jnp.zeros_like(place))
    for r in range(plan.shape[0]):
        plan_ref[:, r * LANES : (r + 1) * LANES] = plan[r : r + 1, :]
    designs = wp_ref.shape[0]
    onehot = (
        lax.broadcasted_iota(jnp.int32, (designs, zones), 0) == plan_ref[...]
    ).astype(F32).astype(BF16)
    rest = wp_ref[...]
    total = jnp.zeros((width, zones), F32)
    for _ in range(3):
        part = rest.astype(BF16)
        rest = rest - part.astype(F32)
        total = total + lax.dot_general(
            part, onehot, (((0,), (0,)), ((), ())), preferred_element_type=F32
        )
    zp_ref[...] = total
    extra = lax.broadcasted_iota(jnp.int32, (16, zones), 0)
    blank = jnp.zeros((DEPTH - width - 16, zones), BF16)

    def hour_step(h, carry):
        rhs_ref[h, :width, :] = (resp_ref[h].astype(F32) * zp_ref[...]).astype(BF16)
        middle = 0.25 * (band_ref[pl.ds(h, 1), :].astype(F32) - 3.5)
        tail = jnp.where(extra == 0, -middle, jnp.where(extra == 1, 1.0, 0.0))
        rhs_ref[h, width : width + 16, :] = tail.astype(BF16)
        rhs_ref[h, width + 16 :, :] = blank
        return carry

    for i in range(pieces):
        large[i].wait()
        lax.fori_loop(i * span, (i + 1) * span, hour_step, 0)


def coefficients(building_map, owner_ids, window_params, band_ids, floor_area, response):
    hours, width, zones = response.shape
    args = [
        building_map.reshape(-1, LANES),
        owner_ids.reshape(-1, LANES),
        window_params,
        band_ids,
        floor_area.reshape(1, zones),
        response,
    ]
    outs = [
        ((hours, DEPTH, zones), BF16),
        ((1, zones), jnp.int32),
        ((1, zones), F32),
        (response.shape, BF16),
    ]
    return pl.pallas_call(
        coeff_kernel,
        in_specs=[pl.BlockSpec(memory_space=pl.ANY)] * len(args),
        out_specs=[VMEM] * len(outs),
        out_shape=[pltpu.MemorySpace.VMEM(shape, kind) for shape, kind in outs],
        scratch_shapes=[pltpu.VMEM(a.shape, a.dtype) for a in args[:4]]
        + [
            pltpu.VMEM((width, zones), F32),
            pltpu.SemaphoreType.DMA((5,)),
            pltpu.SemaphoreType.DMA((4,)),
        ],
        compiler_params=params(),
        name="coefficients",
    )(*[pltpu.with_memory_space_constraint(a, pltpu.HBM) for a in args])


def drivers(pair, second, fill):
    half = pair.shape[1] // 2
    lane = lax.broadcasted_iota(jnp.int32, pair.shape, 1)
    if second:
        pair = pltpu.roll(pair.astype(F32), half, 1).astype(BF16)
    rest = jnp.zeros(pair.shape, F32)
    for spot, value in enumerate(fill):
        rest = jnp.where(lane == half + spot, value, rest)
    return jnp.where(lane < half, pair, rest.astype(BF16))


def occupancy(hour, hours_total):
    return 1.0 + 2.0 * hour.astype(F32) / (hours_total - 1)


def scan_kernel(kind, hours_total, chunks, sources, last, place_ref, *refs):
    with_loss, with_slope = "loss" in kind, "slope" in kind
    f_refs, refs = refs[:chunks], refs[chunks:]
    rhs_ref, area_ref, refs = refs[0], refs[1], refs[2:]
    if last:
        prior_ref, refs = refs[0], refs[1:]
    if with_loss:
        out_ref, refs = refs[0], refs[1:]
    if with_slope:
        slope_ref, ft_ref, refs = refs[0], refs[1], refs[2:]
    if with_loss:
        acc_ref = refs[0]
        acc_ref[...] = jnp.zeros_like(acc_ref)
    hours, _, zones = rhs_ref.shape
    core = place_ref[0]

    def pair_step(j, carry):
        at = pl.ds(pl.multiple_of(j * LANES, LANES), LANES)
        pair = [f_ref[:, at] for f_ref in f_refs]
        pair = pair[0] if chunks == 1 else jnp.concatenate(pair, axis=0)
        if with_slope:
            ft_ref[at, :] = pair.T
        gathered = None
        for k in range(2):
            h = 2 * j + k
            if with_loss:
                lhs = drivers(pair, k == 1, (1.0,))
                occ = occupancy(core * hours + h, hours_total)
            else:
                lhs = drivers((pair.astype(F32) * 0.5).astype(BF16), k == 1, (0.5, 0.25))
            summed = None
            for z in range(0, zones, ZONE_TILE):
                v = jnp.dot(lhs, rhs_ref[h, :, z : z + ZONE_TILE], preferred_element_type=F32)
                if with_loss:
                    a = jnp.abs(v) * MINUS_LOG2_E
                    q = jnp.exp2(a)
                    pen = jnp.log2((q + EDGE) * q + 1.0) - a
                    pen = pen * area_ref[:, z : z + ZONE_TILE]
                    for c in range(0, ZONE_TILE, LANES):
                        piece = pen[:, c : c + LANES]
                        summed = piece if summed is None else summed + piece
                if with_slope:
                    x = v * 0.5 + 0.25 if with_loss else v
                    slope = jnp.tanh(x) + jnp.tanh(x - 0.5)
                    slope_ref[h, :, z : z + ZONE_TILE] = slope.astype(BF16)
            if with_loss:
                summed = summed * occ
                gathered = summed if gathered is None else gathered + summed
        if with_loss:
            acc_ref[...] += gathered
        return carry

    lax.fori_loop(0, hours // 2, pair_step, 0, unroll=2)

    if with_loss:
        row = jnp.sum(acc_ref[...].T, axis=0, keepdims=True)
        if not last:
            out_ref[...] = jnp.broadcast_to(row, out_ref.shape)
        else:
            me = place_ref[1]
            per_half = sources // 2
            chunk = row.shape[1] // per_half
            occ_sum = hours * 1.0 + (
                2.0 * (core * hours * hours + hours * (hours - 1) // 2)
            ).astype(F32) / (hours_total - 1)
            weight = jnp.sum(area_ref[...]) * occ_sum
            message = jnp.zeros(out_ref.shape, F32) + weight
            index = lax.broadcasted_iota(jnp.int32, message.shape, 0)
            blank = jnp.zeros((1, LANES - chunk), F32)
            for m in range(sources):
                source = prior_ref[0:1, :] if m < per_half else row
                first = (m % per_half) * chunk
                piece = jnp.concatenate([source[:, first : first + chunk], blank], axis=1)
                message = jnp.where(index == (me ^ m), piece, message)
            out_ref[...] = message


def scan(kind, place, drivers_in, rhs, area, hours_total, sources, prior=None):
    hours, _, zones = rhs.shape
    rows = sum(f.shape[0] for f in drivers_in)
    outs = []
    scratch = []
    if "loss" in kind:
        sublanes = -(-(sources + 1) // 8) * 8
        outs.append(((8, rows) if prior is None else (sublanes, LANES), F32))
        scratch.append(pltpu.VMEM((rows, LANES), F32))
    if "slope" in kind:
        outs.append(((hours, rows, zones), BF16))
        outs.append(((drivers_in[0].shape[1], rows), BF16))
    return call(
        functools.partial(
            scan_kernel, kind, hours_total, len(drivers_in), sources, prior is not None
        ),
        kind,
        outs,
        [place, *drivers_in, rhs, area] + ([] if prior is None else [prior]),
        scratch,
    )


def gradient_kernel(
    hours_total, gain, owners, sources, messages, place_ref, *refs
):
    msg_refs, refs = refs[:messages], refs[messages:]
    (
        ft0_ref, ft1_ref, slope0_ref, slope1_ref, resp_ref, area_ref, plan_ref,
        out_ref, acc_ref, score_ref, e_ref,
    ) = refs
    hours, width, zones = resp_ref.shape
    core, me = place_ref[0], place_ref[1]
    chunk = e_ref.shape[1] // sources
    total = [msg_ref[...] for msg_ref in msg_refs]
    while len(total) > 1:
        total = [first + second for first, second in zip(total[::2], total[1::2])]
    total = total[0]
    weight = jnp.max(total[sources : sources + 1, :])
    score = total * (SHARPNESS * math.log(2.0) / weight)
    rows = lax.broadcasted_iota(jnp.int32, score.shape, 0)
    lanes = lax.broadcasted_iota(jnp.int32, score.shape, 1)
    valid = (rows < sources) & (lanes < chunk)
    peak = jnp.max(jnp.where(valid, score, -jnp.inf))
    e = jnp.where(valid, jnp.exp(jnp.where(valid, score - peak, 0.0)), 0.0)
    exp_total = jnp.sum(e)
    score_ref[...] = e
    for m in range(sources):
        piece = score_ref[pl.ds(me ^ m, 1), :]
        e_ref[:, m * chunk : (m + 1) * chunk] = piece[:, :chunk]
    acc_ref[...] = jnp.zeros_like(acc_ref)

    def hour_step(h, carry):
        occ = occupancy(core * hours + h, hours_total)
        at = pl.ds(pl.multiple_of(h * width, width), width)
        ft = jnp.concatenate([ft0_ref[at, :], ft1_ref[at, :]], axis=1).astype(F32)
        ft = ft * (e_ref[...] * occ)
        high = ft.astype(BF16)
        low = (ft - high.astype(F32)).astype(BF16)
        both = jnp.concatenate([high, low], axis=0)
        for z in range(0, zones, ZONE_TILE):
            at = slice(z, z + ZONE_TILE)
            kept = jnp.concatenate([slope0_ref[h, :, at], slope1_ref[h, :, at]], axis=0)
            mixed = jnp.dot(both, kept, preferred_element_type=F32)
            mixed = mixed[:width] + mixed[width:]
            acc_ref[:, at] += resp_ref[h, :, at].astype(F32) * mixed
        return carry

    lax.fori_loop(0, hours, hour_step, 0, unroll=2)

    grad = acc_ref[...] * area_ref[...]
    blocks, pad, _ = out_ref.shape
    index = lax.broadcasted_iota(jnp.int32, (blocks * pad, zones), 0)
    within = index % pad
    design = jnp.where(within < owners, (index // pad) * owners + within, -1)
    onehot = (design == plan_ref[...]).astype(F32).astype(BF16)
    sens = jnp.zeros((blocks * pad, width), F32)
    for _ in range(3):
        part = grad.astype(BF16)
        grad = grad - part.astype(F32)
        sens = sens + lax.dot_general(
            onehot, part, (((1,), (1,)), ((), ())), preferred_element_type=F32
        )
    sens = sens * (0.5 * gain / weight)
    out_ref[:, :, :width] = sens.reshape(blocks, pad, width)
    lane = lax.broadcasted_iota(jnp.int32, (blocks, pad, LANES - width), 2)
    out_ref[:, :, width:] = jnp.where(lane == 0, peak, exp_total)


def finish_kernel(scen_parts, width, parts_ref, sens_ref, objective_ref):
    parts = parts_ref[...]
    devices = parts.shape[0]
    peaks = parts[:, :, width : width + 1]
    totals = parts[:, :, width + 1 : width + 2]
    peak = jnp.max(peaks)
    scale = jnp.exp(peaks - peak)
    total = jnp.sum((scale * totals)[:, 0:1, :]) * (scen_parts / devices)
    summed = jnp.sum(parts[:, :, :width] * scale, axis=0) / total
    sens_ref[...] = summed[: sens_ref.shape[0]]
    log_total = jnp.max(jnp.log(jnp.full((8, LANES), total, F32)))
    objective_ref[0] = (peak + log_total) / SHARPNESS - 0.5


def on_device(forcing, response, window_params, building_map, owner_ids, band_ids, floor_area):
    hours, width, zones = response.shape
    hour_parts = lax.axis_size("hour")
    zone_parts = lax.axis_size("zone")
    scen_parts = lax.axis_size("scen")
    hours_total = hours * hour_parts
    core = lax.axis_index("hour")
    me = lax.axis_index(("zone", "hour"))
    sources = zone_parts * hour_parts
    place = jnp.stack([core, me]).astype(jnp.int32)

    half = hours * width
    everyone = forcing.reshape(forcing.shape[0], hours_total * width)
    keep = lax.dynamic_slice_in_dim(everyone, core * half, half, axis=1)
    leave = lax.dynamic_slice_in_dim(everyone, (1 - core) * half, half, axis=1)
    pairs = [[(i, i ^ m) for i in range(sources)] for m in range(sources)]
    if sources == 8:
        came = {
            m: lax.ppermute(leave if m % 2 else keep, ("zone", "hour"), pairs[m])
            for m in (4, 5, 6, 7, 1, 2, 3)
        }
        came[0] = keep
        halves = ([came[m] for m in range(4)], [came[m] for m in range(4, 8)])
    else:
        other = lax.ppermute(leave, "hour", [(0, 1), (1, 0)])
        both = jnp.where(core == 0, jnp.stack([keep, other]), jnp.stack([other, keep]))
        gathered = lax.all_gather(both, "zone", axis=0, tiled=True)
        ordered = jnp.take(gathered, me ^ jnp.arange(sources), axis=0).reshape(2, -1, half)
        halves = ([ordered[0]], [ordered[1]])

    rhs, plan, area, near_response = coefficients(
        building_map, owner_ids, window_params, band_ids, floor_area, response
    )
    common = (rhs, area, hours_total, sources)
    first, slope0, ft0 = scan("loss_slope", place, halves[0], *common)
    (message,) = scan("loss", place, halves[1], *common, prior=first)
    message = message + lax.ppermute(message, "hour", [(0, 1), (1, 0)])
    if zone_parts == 4:
        messages = [message] + [
            lax.ppermute(message, "zone", [(i, i ^ k) for i in range(4)]) for k in (1, 2, 3)
        ]
    else:
        messages = [lax.psum(message, "zone")]
    slope1, ft1 = scan("slope", place, halves[1], *common)

    designs = window_params.shape[0]
    devices = zone_parts * scen_parts * hour_parts
    owners = designs // devices
    pad = -(-owners // 8) * 8
    gain = math.sqrt(width * zones * zone_parts * hours_total * designs)
    (parts,) = call(
        functools.partial(gradient_kernel, hours_total, gain, owners, sources, len(messages)),
        "gradient",
        [((devices, pad, LANES), F32)],
        [place, *messages, ft0, ft1, slope0, slope1, near_response, area, plan],
        [
            pltpu.VMEM((width, zones), F32),
            pltpu.VMEM(message.shape, F32),
            pltpu.VMEM((1, ft0.shape[1] + ft1.shape[1]), F32),
        ],
    )
    parts = lax.all_to_all(
        parts, ("zone", "scen", "hour"), split_axis=0, concat_axis=0, tiled=True
    )
    sensitivity, objective = pl.pallas_call(
        functools.partial(finish_kernel, scen_parts, width),
        in_specs=[VMEM],
        out_specs=[VMEM, SMEM],
        out_shape=[
            jax.ShapeDtypeStruct((owners, width), F32),
            jax.ShapeDtypeStruct((1,), F32),
        ],
        compiler_params=params(),
        name="finish",
    )(near(parts))
    return (sensitivity, objective)


def solution(mesh):
    in_specs = (
        P(("groups", "zone", "scen", "hour"), None, None),
        P("hour", None, ("groups", "zone")),
        P("groups", None),
        P(("groups", "zone")),
        P("groups"),
        P("hour", ("groups", "zone")),
        P(("groups", "zone")),
    )
    out_specs = (P(("groups", "zone", "scen", "hour"), None), P("groups"))
    return jax.shard_map(
        on_device, mesh=mesh, in_specs=in_specs, out_specs=out_specs, check_vma=False
    )
```

```python
import functools
import math

import jax
import jax.numpy as jnp
from jax import lax
from jax.experimental import pallas as pl
from jax.experimental.pallas import tpu as pltpu
from jax.sharding import PartitionSpec as P

SHARPNESS = 200.0
MINUS_LOG2_E = -1.0 / math.log(2.0)
EDGE = 2.0 * math.cosh(0.5)
LANES = 128
DEPTH = 128
ZONE_TILE = 256
SHORT = pl.CostEstimate(flops=1, bytes_accessed=1, transcendentals=0)
VMEM = pl.BlockSpec(memory_space=pltpu.VMEM)
SMEM = pl.BlockSpec(memory_space=pltpu.SMEM)
F32 = jnp.float32
BF16 = jnp.bfloat16


def params():
    return pltpu.CompilerParams(vmem_limit_bytes=20 * 2**20)


def near(x):
    return pltpu.with_memory_space_constraint(x, pltpu.VMEM)


def call(kernel, name, outs, args, scratch=(), cost=None):
    return pl.pallas_call(
        kernel,
        in_specs=[VMEM] * len(args),
        out_specs=[VMEM] * len(outs),
        out_shape=[pltpu.MemorySpace.VMEM(shape, kind) for shape, kind in outs],
        scratch_shapes=list(scratch),
        compiler_params=params(),
        cost_estimate=cost,
        name=name,
    )(*[near(a) for a in args])


def coeff_kernel(
    map_hbm, owner_hbm, wp_hbm, band_hbm, area_hbm, resp_hbm, rhs_ref, plan_ref, area_ref, resp_ref,
    map_ref, owner_ref, wp_ref, band_ref, zp_ref, sems, resp_sems,
):
    hours, width, zones = resp_ref.shape
    pieces = resp_sems.shape[0]
    span = hours // pieces
    small = [
        pltpu.make_async_copy(source, target, sems.at[i])
        for i, (source, target) in enumerate(
            (
                (map_hbm, map_ref),
                (owner_hbm, owner_ref),
                (wp_hbm, wp_ref),
                (band_hbm, band_ref),
                (area_hbm, area_ref),
            )
        )
    ]
    for copy in small:
        copy.start()
    large = []
    for i in range(pieces):
        part = pl.ds(i * span, span)
        large.append(
            pltpu.make_async_copy(resp_hbm.at[part], resp_ref.at[part], resp_sems.at[i])
        )
        large[-1].start()
    for copy in small:
        copy.wait()
    place = map_ref[...]
    row, lane = place // LANES, place % LANES

    def look(i, found):
        table = jnp.broadcast_to(owner_ref[pl.ds(i, 1), :], place.shape)
        here = jnp.take_along_axis(table, lane, axis=1, mode="promise_in_bounds")
        return jnp.where(row == i, here, found)

    plan = lax.fori_loop(0, owner_ref.shape[0], look, jnp.zeros_like(place))
    for r in range(plan.shape[0]):
        plan_ref[:, r * LANES : (r + 1) * LANES] = plan[r : r + 1, :]
    designs = wp_ref.shape[0]
    onehot = (
        lax.broadcasted_iota(jnp.int32, (designs, zones), 0) == plan_ref[...]
    ).astype(F32).astype(BF16)
    rest = wp_ref[...]
    total = jnp.zeros((width, zones), F32)
    for _ in range(3):
        part = rest.astype(BF16)
        rest = rest - part.astype(F32)
        total = total + lax.dot_general(
            part, onehot, (((0,), (0,)), ((), ())), preferred_element_type=F32
        )
    zp_ref[...] = total
    extra = lax.broadcasted_iota(jnp.int32, (16, zones), 0)
    blank = jnp.zeros((DEPTH - width - 16, zones), BF16)

    def hour_step(h, carry):
        rhs_ref[h, :width, :] = (resp_ref[h].astype(F32) * zp_ref[...]).astype(BF16)
        middle = 0.25 * (band_ref[pl.ds(h, 1), :].astype(F32) - 3.5)
        tail = jnp.where(extra == 0, -middle, jnp.where(extra == 1, 1.0, 0.0))
        rhs_ref[h, width : width + 16, :] = tail.astype(BF16)
        rhs_ref[h, width + 16 :, :] = blank
        return carry

    for i in range(pieces):
        large[i].wait()
        lax.fori_loop(i * span, (i + 1) * span, hour_step, 0)


def coefficients(building_map, owner_ids, window_params, band_ids, floor_area, response):
    hours, width, zones = response.shape
    args = [
        building_map.reshape(-1, LANES),
        owner_ids.reshape(-1, LANES),
        window_params,
        band_ids,
        floor_area.reshape(1, zones),
        response,
    ]
    outs = [
        ((hours, DEPTH, zones), BF16),
        ((1, zones), jnp.int32),
        ((1, zones), F32),
        (response.shape, BF16),
    ]
    return pl.pallas_call(
        coeff_kernel,
        in_specs=[pl.BlockSpec(memory_space=pl.ANY)] * len(args),
        out_specs=[VMEM] * len(outs),
        out_shape=[pltpu.MemorySpace.VMEM(shape, kind) for shape, kind in outs],
        scratch_shapes=[pltpu.VMEM(a.shape, a.dtype) for a in args[:4]]
        + [
            pltpu.VMEM((width, zones), F32),
            pltpu.SemaphoreType.DMA((5,)),
            pltpu.SemaphoreType.DMA((4,)),
        ],
        compiler_params=params(),
        cost_estimate=SHORT,
        name="coefficients",
    )(*[pltpu.with_memory_space_constraint(a, pltpu.HBM) for a in args])


def drivers(pair, second, fill):
    half = pair.shape[1] // 2
    lane = lax.broadcasted_iota(jnp.int32, pair.shape, 1)
    if second:
        pair = pltpu.roll(pair.astype(F32), half, 1).astype(BF16)
    rest = jnp.zeros(pair.shape, F32)
    for spot, value in enumerate(fill):
        rest = jnp.where(lane == half + spot, value, rest)
    return jnp.where(lane < half, pair, rest.astype(BF16))


def here():
    core = lax.axis_index("hour")
    return core, lax.axis_index("zone") * lax.axis_size("hour") + core


def occupancy(hour, hours_total):
    return 1.0 + 2.0 * hour.astype(F32) / (hours_total - 1)


def scan_kernel(kind, hours_total, chunks, extra, sources, priors, unroll, *refs):
    with_loss, with_slope, with_turn = "loss" in kind, "slope" in kind, "turn" in kind
    f_refs, refs = refs[:chunks], refs[chunks:]
    turn_refs, refs = [*refs[:extra], *f_refs], refs[extra:]
    rhs_ref, area_ref, refs = refs[0], refs[1], refs[2:]
    prior_refs, refs = refs[:priors], refs[priors:]
    if with_loss:
        out_ref, refs = refs[0], refs[1:]
    if with_slope:
        slope_ref, refs = refs[0], refs[1:]
    if with_turn:
        ft_ref, refs = refs[0], refs[1:]
    if with_loss:
        acc_ref = refs[0]
        acc_ref[...] = jnp.zeros_like(acc_ref)
    hours, _, zones = rhs_ref.shape
    core, me = here()

    def rows_of(parts, at):
        parts = [part[:, at] for part in parts]
        return parts[0] if len(parts) == 1 else jnp.concatenate(parts, axis=0)

    def pair_step(j, carry):
        at = pl.ds(pl.multiple_of(j * LANES, LANES), LANES)
        pair = rows_of(f_refs, at)
        if with_turn:
            ft_ref[at, :] = rows_of(turn_refs, at).T
        gathered = None
        for k in range(2):
            h = 2 * j + k
            if with_loss:
                lhs = drivers(pair, k == 1, (1.0,))
                occ = occupancy(core * hours + h, hours_total)
            else:
                lhs = drivers((pair.astype(F32) * 0.5).astype(BF16), k == 1, (0.5, 0.25))
            summed = None
            for z in range(0, zones, ZONE_TILE):
                v = jnp.dot(lhs, rhs_ref[h, :, z : z + ZONE_TILE], preferred_element_type=F32)
                if with_loss:
                    a = jnp.abs(v) * MINUS_LOG2_E
                    q = jnp.exp2(a)
                    pen = jnp.log2((q + EDGE) * q + 1.0) - a
                    pen = pen * area_ref[:, z : z + ZONE_TILE]
                    for c in range(0, ZONE_TILE, LANES):
                        piece = pen[:, c : c + LANES]
                        summed = piece if summed is None else summed + piece
                if with_slope:
                    x = v * 0.5 + 0.25 if with_loss else v
                    slope = jnp.tanh(x) + jnp.tanh(x - 0.5)
                    slope_ref[h, :, z : z + ZONE_TILE] = slope.astype(BF16)
            if with_loss:
                summed = summed * occ
                gathered = summed if gathered is None else gathered + summed
        if with_loss:
            acc_ref[...] += gathered
        return carry

    lax.fori_loop(0, hours // 2, pair_step, 0, unroll=unroll)

    if with_loss:
        row = jnp.sum(acc_ref[...].T, axis=0, keepdims=True)
        if not priors:
            out_ref[...] = jnp.broadcast_to(row, out_ref.shape)
        else:
            known = [ref[0:1, :] for ref in prior_refs] + [row]
            chunk = sum(part.shape[1] for part in known) // sources
            pieces = [
                part[:, first : first + chunk]
                for part in known
                for first in range(0, part.shape[1], chunk)
            ]
            occ_sum = hours * 1.0 + (
                2.0 * (core * hours * hours + hours * (hours - 1) // 2)
            ).astype(F32) / (hours_total - 1)
            weight = jnp.sum(area_ref[...]) * occ_sum
            message = jnp.zeros(out_ref.shape, F32) + weight
            index = lax.broadcasted_iota(jnp.int32, message.shape, 0)
            blank = jnp.zeros((1, LANES - chunk), F32)
            for m, piece in enumerate(pieces):
                piece = jnp.concatenate([piece, blank], axis=1)
                message = jnp.where(index == (me ^ m), piece, message)
            out_ref[...] = message


def scan(kind, rows_in, rhs, area, hours_total, sources, extra=(), priors=(), unroll=4, cost=None):
    hours, _, zones = rhs.shape
    rows = sum(f.shape[0] for f in rows_in)
    outs = []
    scratch = []
    if "loss" in kind:
        sublanes = -(-(sources + 1) // 8) * 8
        outs.append(((sublanes, LANES) if priors else (8, rows), F32))
        scratch.append(pltpu.VMEM((rows, LANES), F32))
    if "slope" in kind:
        outs.append(((hours, rows, zones), BF16))
    if "turn" in kind:
        outs.append(((rows_in[0].shape[1], rows + sum(f.shape[0] for f in extra)), BF16))
    return call(
        functools.partial(
            scan_kernel, kind, hours_total, len(rows_in), len(extra), sources, len(priors), unroll
        ),
        kind,
        outs,
        [*rows_in, *extra, rhs, area, *priors],
        scratch,
        cost,
    )


def gradient_kernel(
    hours_total, gain, owners, sources, messages, *refs
):
    msg_refs, refs = refs[:messages], refs[messages:]
    ft_refs, slope_refs, refs = refs[:2], refs[2:5], refs[5:]
    resp_ref, area_ref, plan_ref, out_ref, acc_ref, score_ref, e_ref = refs
    hours, width, zones = resp_ref.shape
    core, me = here()
    chunk = e_ref.shape[1] // sources
    total = [msg_ref[...] for msg_ref in msg_refs]
    while len(total) > 1:
        total = [first + second for first, second in zip(total[::2], total[1::2])]
    total = total[0]
    weight = jnp.max(total[sources : sources + 1, :])
    score = total * (SHARPNESS * math.log(2.0) / weight)
    rows = lax.broadcasted_iota(jnp.int32, score.shape, 0)
    lanes = lax.broadcasted_iota(jnp.int32, score.shape, 1)
    valid = (rows < sources) & (lanes < chunk)
    peak = jnp.max(jnp.where(valid, score, -jnp.inf))
    e = jnp.where(valid, jnp.exp(jnp.where(valid, score - peak, 0.0)), 0.0)
    exp_total = jnp.sum(e)
    score_ref[...] = e
    for m in range(sources):
        piece = score_ref[pl.ds(me ^ m, 1), :]
        e_ref[:, m * chunk : (m + 1) * chunk] = piece[:, :chunk]
    acc_ref[...] = jnp.zeros_like(acc_ref)

    def hour_step(h, carry):
        occ = occupancy(core * hours + h, hours_total)
        at = pl.ds(pl.multiple_of(h * width, width), width)
        ft = jnp.concatenate([ref[at, :] for ref in ft_refs], axis=1).astype(F32)
        ft = ft * (e_ref[...] * occ)
        high = ft.astype(BF16)
        low = (ft - high.astype(F32)).astype(BF16)
        both = jnp.concatenate([high, low], axis=0)
        for z in range(0, zones, ZONE_TILE):
            at = slice(z, z + ZONE_TILE)
            kept = jnp.concatenate([ref[h, :, at] for ref in slope_refs], axis=0)
            mixed = jnp.dot(both, kept, preferred_element_type=F32)
            mixed = mixed[:width] + mixed[width:]
            acc_ref[:, at] += resp_ref[h, :, at].astype(F32) * mixed
        return carry

    lax.fori_loop(0, hours, hour_step, 0, unroll=4)

    grad = acc_ref[...] * area_ref[...]
    blocks, pad, _ = out_ref.shape
    index = lax.broadcasted_iota(jnp.int32, (blocks * pad, zones), 0)
    within = index % pad
    design = jnp.where(within < owners, (index // pad) * owners + within, -1)
    onehot = (design == plan_ref[...]).astype(F32).astype(BF16)
    sens = jnp.zeros((blocks * pad, width), F32)
    for _ in range(3):
        part = grad.astype(BF16)
        grad = grad - part.astype(F32)
        sens = sens + lax.dot_general(
            onehot, part, (((1,), (1,)), ((), ())), preferred_element_type=F32
        )
    sens = sens * (0.5 * gain / weight)
    out_ref[:, :, :width] = sens.reshape(blocks, pad, width)
    lane = lax.broadcasted_iota(jnp.int32, (blocks, pad, LANES - width), 2)
    out_ref[:, :, width:] = jnp.where(lane == 0, peak, exp_total)


def finish_kernel(scen_parts, width, parts_ref, sens_ref, objective_ref):
    parts = parts_ref[...]
    devices = parts.shape[0]
    peaks = parts[:, :, width : width + 1]
    totals = parts[:, :, width + 1 : width + 2]
    peak = jnp.max(peaks)
    scale = jnp.exp(peaks - peak)
    total = jnp.sum((scale * totals)[:, 0:1, :]) * (scen_parts / devices)
    summed = jnp.sum(parts[:, :, :width] * scale, axis=0) / total
    sens_ref[...] = summed[: sens_ref.shape[0]]
    log_total = jnp.max(jnp.log(jnp.full((8, LANES), total, F32)))
    objective_ref[0] = (peak + log_total) / SHARPNESS - 0.5


def on_device(forcing, response, window_params, building_map, owner_ids, band_ids, floor_area):
    hours, width, zones = response.shape
    hour_parts = lax.axis_size("hour")
    zone_parts = lax.axis_size("zone")
    scen_parts = lax.axis_size("scen")
    hours_total = hours * hour_parts
    core = lax.axis_index("hour")
    sources = zone_parts * hour_parts

    half = hours * width
    everyone = forcing.reshape(forcing.shape[0], hours_total * width)
    keep = lax.dynamic_slice_in_dim(everyone, core * half, half, axis=1)
    leave = lax.dynamic_slice_in_dim(everyone, (1 - core) * half, half, axis=1)
    came = lax.ppermute(leave, "hour", [(0, 1), (1, 0)])
    mine = jnp.concatenate([keep, came], axis=0)

    def swap(x, step):
        return lax.ppermute(x, "zone", [(i, i ^ step) for i in range(zone_parts)])

    rhs, plan, area, near_response = coefficients(
        building_map, owner_ids, window_params, band_ids, floor_area, response
    )
    common = (rhs, area, hours_total, sources)
    if zone_parts == 4:
        far = swap(mine, 2)
        beside = swap(mine, 1)
        loss0, slope0 = scan("loss_slope", [mine], *common, cost=SHORT)
        far, loss0 = lax.optimization_barrier((far, loss0))
        last = [far, swap(far, 1)]
    else:
        me = lax.axis_index(("zone", "hour"))
        both = jnp.where(core == 0, jnp.stack([keep, came]), jnp.stack([came, keep]))
        gathered = lax.all_gather(both, "zone", axis=0, tiled=True)
        ordered = jnp.take(gathered, me ^ jnp.arange(sources), axis=0).reshape(4, -1, half)
        mine, beside, last = ordered[0], ordered[1], [ordered[2], ordered[3]]
        loss0, slope0 = scan("loss_slope", [mine], *common)
    loss1, slope1, ft0 = scan("loss_slope_turn", [beside], *common, extra=[mine])
    (message,) = scan("loss", last, *common, priors=[loss0, loss1], unroll=6)
    message = message + lax.ppermute(message, "hour", [(0, 1), (1, 0)])
    if zone_parts == 4:
        messages = [message] + [swap(message, k) for k in (1, 2, 3)]
    else:
        messages = [lax.psum(message, "zone")]
    slope2, ft1 = scan("slope_turn", last, *common)

    designs = window_params.shape[0]
    devices = zone_parts * scen_parts * hour_parts
    owners = designs // devices
    pad = -(-owners // 8) * 8
    gain = math.sqrt(width * zones * zone_parts * hours_total * designs)
    (parts,) = call(
        functools.partial(gradient_kernel, hours_total, gain, owners, sources, len(messages)),
        "gradient",
        [((devices, pad, LANES), F32)],
        [*messages, ft0, ft1, slope0, slope1, slope2, near_response, area, plan],
        [
            pltpu.VMEM((width, zones), F32),
            pltpu.VMEM(message.shape, F32),
            pltpu.VMEM((1, ft0.shape[1] + ft1.shape[1]), F32),
        ],
    )
    parts = lax.all_to_all(
        parts, ("zone", "scen", "hour"), split_axis=0, concat_axis=0, tiled=True
    )
    sensitivity, objective = pl.pallas_call(
        functools.partial(finish_kernel, scen_parts, width),
        in_specs=[VMEM],
        out_specs=[VMEM, SMEM],
        out_shape=[
            jax.ShapeDtypeStruct((owners, width), F32),
            jax.ShapeDtypeStruct((1,), F32),
        ],
        compiler_params=params(),
        name="finish",
    )(near(parts))
    return (sensitivity, objective)


def solution(mesh):
    in_specs = (
        P(("groups", "zone", "scen", "hour"), None, None),
        P("hour", None, ("groups", "zone")),
        P("groups", None),
        P(("groups", "zone")),
        P("groups"),
        P("hour", ("groups", "zone")),
        P(("groups", "zone")),
    )
    out_specs = (P(("groups", "zone", "scen", "hour"), None), P("groups"))
    return jax.shard_map(
        on_device, mesh=mesh, in_specs=in_specs, out_specs=out_specs, check_vma=False
    )
```

```python
import functools
import math

import jax
import jax.numpy as jnp
from jax import lax
from jax.experimental import pallas as pl
from jax.experimental.pallas import tpu as pltpu
from jax.sharding import PartitionSpec as P

SHARPNESS = 200.0
MINUS_LOG2_E = -1.0 / math.log(2.0)
EDGE = 2.0 * math.cosh(0.5)
LANES = 128
DEPTH = 128
ZONE_TILE = 256
SHORT = pl.CostEstimate(flops=1, bytes_accessed=1, transcendentals=0)
VMEM = pl.BlockSpec(memory_space=pltpu.VMEM)
SMEM = pl.BlockSpec(memory_space=pltpu.SMEM)
F32 = jnp.float32
BF16 = jnp.bfloat16


def params():
    return pltpu.CompilerParams(vmem_limit_bytes=20 * 2**20)


def near(x):
    return pltpu.with_memory_space_constraint(x, pltpu.VMEM)


def call(kernel, name, outs, args, scratch=(), cost=None):
    return pl.pallas_call(
        kernel,
        in_specs=[VMEM] * len(args),
        out_specs=[VMEM] * len(outs),
        out_shape=[pltpu.MemorySpace.VMEM(shape, kind) for shape, kind in outs],
        scratch_shapes=list(scratch),
        compiler_params=params(),
        cost_estimate=cost,
        name=name,
    )(*[near(a) for a in args])


def coeff_kernel(
    map_hbm, owner_hbm, wp_hbm, band_hbm, area_hbm, resp_hbm, rhs_ref, plan_ref, area_ref, resp_ref,
    map_ref, owner_ref, wp_ref, band_ref, zp_ref, sems, resp_sems,
):
    hours, width, zones = resp_ref.shape
    pieces = resp_sems.shape[0]
    span = hours // pieces
    small = [
        pltpu.make_async_copy(source, target, sems.at[i])
        for i, (source, target) in enumerate(
            (
                (map_hbm, map_ref),
                (owner_hbm, owner_ref),
                (wp_hbm, wp_ref),
                (band_hbm, band_ref),
                (area_hbm, area_ref),
            )
        )
    ]
    for copy in small:
        copy.start()
    large = []
    for i in range(pieces):
        part = pl.ds(i * span, span)
        large.append(
            pltpu.make_async_copy(resp_hbm.at[part], resp_ref.at[part], resp_sems.at[i])
        )
        large[-1].start()
    for copy in small:
        copy.wait()
    place = map_ref[...]
    row, lane = place // LANES, place % LANES

    def look(i, found):
        table = jnp.broadcast_to(owner_ref[pl.ds(i, 1), :], place.shape)
        here = jnp.take_along_axis(table, lane, axis=1, mode="promise_in_bounds")
        return jnp.where(row == i, here, found)

    plan = lax.fori_loop(0, owner_ref.shape[0], look, jnp.zeros_like(place))
    for r in range(plan.shape[0]):
        plan_ref[:, r * LANES : (r + 1) * LANES] = plan[r : r + 1, :]
    designs = wp_ref.shape[0]
    onehot = (
        lax.broadcasted_iota(jnp.int32, (designs, zones), 0) == plan_ref[...]
    ).astype(F32).astype(BF16)
    rest = wp_ref[...]
    total = jnp.zeros((width, zones), F32)
    for _ in range(3):
        part = rest.astype(BF16)
        rest = rest - part.astype(F32)
        total = total + lax.dot_general(
            part, onehot, (((0,), (0,)), ((), ())), preferred_element_type=F32
        )
    zp_ref[...] = total
    extra = lax.broadcasted_iota(jnp.int32, (16, zones), 0)
    blank = jnp.zeros((DEPTH - width - 16, zones), BF16)

    def pair_step(j, carry):
        for k in range(2):
            h = 2 * j + k
            at = k * DEPTH
            coeff = resp_ref[h].astype(F32) * zp_ref[...]
            rhs_ref[j, at : at + width, :] = coeff.astype(BF16)
            middle = 0.25 * (band_ref[pl.ds(h, 1), :].astype(F32) - 3.5)
            tail = jnp.where(extra == 0, -middle, jnp.where(extra == 1, 1.0, 0.0))
            rhs_ref[j, at + width : at + width + 16, :] = tail.astype(BF16)
            rhs_ref[j, at + width + 16 : at + DEPTH, :] = blank
        return carry

    for i in range(pieces):
        large[i].wait()
        lax.fori_loop(i * span // 2, (i + 1) * span // 2, pair_step, 0)


def coefficients(building_map, owner_ids, window_params, band_ids, floor_area, response):
    hours, width, zones = response.shape
    args = [
        building_map.reshape(-1, LANES),
        owner_ids.reshape(-1, LANES),
        window_params,
        band_ids,
        floor_area.reshape(1, zones),
        response,
    ]
    outs = [
        ((hours // 2, 2 * DEPTH, zones), BF16),
        ((1, zones), jnp.int32),
        ((1, zones), F32),
        (response.shape, BF16),
    ]
    return pl.pallas_call(
        coeff_kernel,
        in_specs=[pl.BlockSpec(memory_space=pl.ANY)] * len(args),
        out_specs=[VMEM] * len(outs),
        out_shape=[pltpu.MemorySpace.VMEM(shape, kind) for shape, kind in outs],
        scratch_shapes=[pltpu.VMEM(a.shape, a.dtype) for a in args[:4]]
        + [
            pltpu.VMEM((width, zones), F32),
            pltpu.SemaphoreType.DMA((5,)),
            pltpu.SemaphoreType.DMA((4,)),
        ],
        compiler_params=params(),
        cost_estimate=SHORT,
        name="coefficients",
    )(*[pltpu.with_memory_space_constraint(a, pltpu.HBM) for a in args])


def drivers(pair, second, fill):
    half = pair.shape[1] // 2
    lane = lax.broadcasted_iota(jnp.int32, pair.shape, 1)
    if second:
        pair = pltpu.roll(pair.astype(F32), half, 1).astype(BF16)
    rest = jnp.zeros(pair.shape, F32)
    for spot, value in enumerate(fill):
        rest = jnp.where(lane == half + spot, value, rest)
    return jnp.where(lane < half, pair, rest.astype(BF16))


def here():
    core = lax.axis_index("hour")
    return core, lax.axis_index("zone") * lax.axis_size("hour") + core


def occupancy(hour, hours_total):
    return 1.0 + 2.0 * hour.astype(F32) / (hours_total - 1)


def scan_kernel(kind, hours_total, chunks, extra, sources, priors, unroll, *refs):
    with_loss, with_slope, with_turn = "loss" in kind, "slope" in kind, "turn" in kind
    f_refs, refs = refs[:chunks], refs[chunks:]
    turn_refs, refs = [*refs[:extra], *f_refs], refs[extra:]
    rhs_ref, area_ref, refs = refs[0], refs[1], refs[2:]
    prior_refs, refs = refs[:priors], refs[priors:]
    if with_loss:
        out_ref, refs = refs[0], refs[1:]
    if with_slope:
        slope_ref, refs = refs[0], refs[1:]
    if with_turn:
        ft_ref, refs = refs[0], refs[1:]
    if with_loss:
        acc_ref = refs[0]
        acc_ref[...] = jnp.zeros_like(acc_ref)
    pairs, _, zones = rhs_ref.shape
    hours = 2 * pairs
    core, me = here()

    def rows_of(parts, at):
        parts = [part[:, at] for part in parts]
        return parts[0] if len(parts) == 1 else jnp.concatenate(parts, axis=0)

    def pair_step(j, carry):
        at = pl.ds(pl.multiple_of(j * LANES, LANES), LANES)
        pair = rows_of(f_refs, at)
        if with_turn:
            ft_ref[at, :] = rows_of(turn_refs, at).T
        rows = pair.shape[0]
        fill = (1.0,) if with_loss else (0.5, 0.25)
        if not with_loss:
            pair = (pair.astype(F32) * 0.5).astype(BF16)
        none = jnp.zeros(pair.shape, BF16)
        lhs = jnp.concatenate(
            [
                jnp.concatenate([drivers(pair, False, fill), none], axis=1),
                jnp.concatenate([none, drivers(pair, True, fill)], axis=1),
            ],
            axis=0,
        )
        summed = None
        for z in range(0, zones, ZONE_TILE):
            v = jnp.dot(lhs, rhs_ref[j, :, z : z + ZONE_TILE], preferred_element_type=F32)
            if with_loss:
                a = jnp.abs(v) * MINUS_LOG2_E
                q = jnp.exp2(a)
                pen = jnp.log2((q + EDGE) * q + 1.0) - a
                pen = pen * area_ref[:, z : z + ZONE_TILE]
                for c in range(0, ZONE_TILE, LANES):
                    piece = pen[:, c : c + LANES]
                    summed = piece if summed is None else summed + piece
            if with_slope:
                x = v * 0.5 + 0.25 if with_loss else v
                slope = (jnp.tanh(x) + jnp.tanh(x - 0.5)).astype(BF16)
                slope_ref[2 * j, :, z : z + ZONE_TILE] = slope[:rows]
                slope_ref[2 * j + 1, :, z : z + ZONE_TILE] = slope[rows:]
        if with_loss:
            first = core * hours + 2 * j
            acc_ref[...] += summed[:rows] * occupancy(first, hours_total) + summed[
                rows:
            ] * occupancy(first + 1, hours_total)
        return carry

    lax.fori_loop(0, pairs, pair_step, 0, unroll=unroll)

    if with_loss:
        row = jnp.sum(acc_ref[...].T, axis=0, keepdims=True)
        if not priors:
            out_ref[...] = jnp.broadcast_to(row, out_ref.shape)
        else:
            known = [ref[0:1, :] for ref in prior_refs] + [row]
            chunk = sum(part.shape[1] for part in known) // sources
            pieces = [
                part[:, first : first + chunk]
                for part in known
                for first in range(0, part.shape[1], chunk)
            ]
            occ_sum = hours * 1.0 + (
                2.0 * (core * hours * hours + hours * (hours - 1) // 2)
            ).astype(F32) / (hours_total - 1)
            weight = jnp.sum(area_ref[...]) * occ_sum
            message = jnp.zeros(out_ref.shape, F32) + weight
            index = lax.broadcasted_iota(jnp.int32, message.shape, 0)
            blank = jnp.zeros((1, LANES - chunk), F32)
            for m, piece in enumerate(pieces):
                piece = jnp.concatenate([piece, blank], axis=1)
                message = jnp.where(index == (me ^ m), piece, message)
            out_ref[...] = message


def scan(kind, rows_in, rhs, area, hours_total, sources, extra=(), priors=(), unroll=4, cost=None):
    hours, zones = 2 * rhs.shape[0], rhs.shape[2]
    rows = sum(f.shape[0] for f in rows_in)
    outs = []
    scratch = []
    if "loss" in kind:
        sublanes = -(-(sources + 1) // 8) * 8
        outs.append(((sublanes, LANES) if priors else (8, rows), F32))
        scratch.append(pltpu.VMEM((rows, LANES), F32))
    if "slope" in kind:
        outs.append(((hours, rows, zones), BF16))
    if "turn" in kind:
        outs.append(((rows_in[0].shape[1], rows + sum(f.shape[0] for f in extra)), BF16))
    return call(
        functools.partial(
            scan_kernel, kind, hours_total, len(rows_in), len(extra), sources, len(priors), unroll
        ),
        kind,
        outs,
        [*rows_in, *extra, rhs, area, *priors],
        scratch,
        cost,
    )


def gradient_kernel(
    hours_total, gain, owners, sources, messages, *refs
):
    msg_refs, refs = refs[:messages], refs[messages:]
    ft_refs, slope_refs, refs = refs[:2], refs[2:5], refs[5:]
    resp_ref, area_ref, plan_ref, out_ref, acc_ref, score_ref, e_ref = refs
    hours, width, zones = resp_ref.shape
    core, me = here()
    chunk = e_ref.shape[1] // sources
    total = [msg_ref[...] for msg_ref in msg_refs]
    while len(total) > 1:
        total = [first + second for first, second in zip(total[::2], total[1::2])]
    total = total[0]
    weight = jnp.max(total[sources : sources + 1, :])
    score = total * (SHARPNESS * math.log(2.0) / weight)
    rows = lax.broadcasted_iota(jnp.int32, score.shape, 0)
    lanes = lax.broadcasted_iota(jnp.int32, score.shape, 1)
    valid = (rows < sources) & (lanes < chunk)
    peak = jnp.max(jnp.where(valid, score, -jnp.inf))
    e = jnp.where(valid, jnp.exp(jnp.where(valid, score - peak, 0.0)), 0.0)
    exp_total = jnp.sum(e)
    score_ref[...] = e
    quarter = sources // 4
    order = [q * quarter + m for q in (1, 2, 0, 3) for m in range(quarter)]
    for spot, m in enumerate(order):
        piece = score_ref[pl.ds(me ^ m, 1), :]
        e_ref[:, spot * chunk : (spot + 1) * chunk] = piece[:, :chunk]
    acc_ref[...] = jnp.zeros_like(acc_ref)

    def hour_step(h, carry):
        occ = occupancy(core * hours + h, hours_total)
        at = pl.ds(pl.multiple_of(h * width, width), width)
        ft = jnp.concatenate([ref[at, :] for ref in ft_refs], axis=1).astype(F32)
        ft = ft * (e_ref[...] * occ)
        high = ft.astype(BF16)
        low = (ft - high.astype(F32)).astype(BF16)
        both = jnp.concatenate([high, low], axis=0)
        for z in range(0, zones, ZONE_TILE):
            at = slice(z, z + ZONE_TILE)
            kept = jnp.concatenate([ref[h, :, at] for ref in slope_refs], axis=0)
            mixed = jnp.dot(both, kept, preferred_element_type=F32)
            mixed = mixed[:width] + mixed[width:]
            acc_ref[:, at] += resp_ref[h, :, at].astype(F32) * mixed
        return carry

    lax.fori_loop(0, hours, hour_step, 0, unroll=4)

    grad = acc_ref[...] * area_ref[...]
    blocks, pad, _ = out_ref.shape
    index = lax.broadcasted_iota(jnp.int32, (blocks * pad, zones), 0)
    within = index % pad
    design = jnp.where(within < owners, (index // pad) * owners + within, -1)
    onehot = (design == plan_ref[...]).astype(F32).astype(BF16)
    sens = jnp.zeros((blocks * pad, width), F32)
    for _ in range(3):
        part = grad.astype(BF16)
        grad = grad - part.astype(F32)
        sens = sens + lax.dot_general(
            onehot, part, (((1,), (1,)), ((), ())), preferred_element_type=F32
        )
    sens = sens * (0.5 * gain / weight)
    out_ref[:, :, :width] = sens.reshape(blocks, pad, width)
    lane = lax.broadcasted_iota(jnp.int32, (blocks, pad, LANES - width), 2)
    out_ref[:, :, width:] = jnp.where(lane == 0, peak, exp_total)


def finish_kernel(scen_parts, width, parts_ref, sens_ref, objective_ref):
    parts = parts_ref[...]
    devices = parts.shape[0]
    peaks = parts[:, :, width : width + 1]
    totals = parts[:, :, width + 1 : width + 2]
    peak = jnp.max(peaks)
    scale = jnp.exp(peaks - peak)
    total = jnp.sum((scale * totals)[:, 0:1, :]) * (scen_parts / devices)
    summed = jnp.sum(parts[:, :, :width] * scale, axis=0) / total
    sens_ref[...] = summed[: sens_ref.shape[0]]
    log_total = jnp.max(jnp.log(jnp.full((8, LANES), total, F32)))
    objective_ref[0] = (peak + log_total) / SHARPNESS - 0.5


def on_device(forcing, response, window_params, building_map, owner_ids, band_ids, floor_area):
    hours, width, zones = response.shape
    hour_parts = lax.axis_size("hour")
    zone_parts = lax.axis_size("zone")
    scen_parts = lax.axis_size("scen")
    hours_total = hours * hour_parts
    core = lax.axis_index("hour")
    sources = zone_parts * hour_parts

    half = hours * width
    everyone = forcing.reshape(forcing.shape[0], hours_total * width)
    keep = lax.dynamic_slice_in_dim(everyone, core * half, half, axis=1)
    leave = lax.dynamic_slice_in_dim(everyone, (1 - core) * half, half, axis=1)
    came = lax.ppermute(leave, "hour", [(0, 1), (1, 0)])

    def across(x, m):
        return lax.ppermute(x, ("zone", "hour"), [(i, i ^ m) for i in range(sources)])

    def swap(x, step):
        return lax.ppermute(x, "zone", [(i, i ^ step) for i in range(zone_parts)])

    came, building_map = lax.optimization_barrier((came, building_map))
    rhs, plan, area, near_response = coefficients(
        building_map, owner_ids, window_params, band_ids, floor_area, response
    )
    if zone_parts == 4:
        far0, far1 = across(keep, 4), across(leave, 5)
        near0, near1 = across(keep, 2), across(leave, 3)
        mine = [keep, came]
    else:
        me = lax.axis_index(("zone", "hour"))
        both = jnp.where(core == 0, jnp.stack([keep, came]), jnp.stack([came, keep]))
        gathered = lax.all_gather(both, "zone", axis=0, tiled=True)
        ordered = jnp.take(gathered, me ^ jnp.arange(sources), axis=0).reshape(4, -1, half)
        mine, beside, far, last = [ordered[0]], ordered[1], ordered[2], ordered[3]
    common = (rhs, area, hours_total, sources)
    loss0, slope0 = scan("loss_slope", mine, *common, cost=SHORT)
    if zone_parts == 4:
        near0, near1, far0, far1, loss0 = lax.optimization_barrier(
            (near0, near1, far0, far1, loss0)
        )
        beside = jnp.concatenate([near0, near1], axis=0)
        far = jnp.concatenate([far0, far1], axis=0)
        last = swap(far, 1)
    loss1, slope1, ft1 = scan("loss_slope_turn", [beside, far], *common)
    (message,) = scan("loss", [last], *common, priors=[loss0, loss1])
    message = message + lax.ppermute(message, "hour", [(0, 1), (1, 0)])
    slope2, ft2 = scan("slope_turn", [last], *common, extra=mine)
    if zone_parts == 4:
        others = [swap(message, k) for k in (1, 2, 3)]
        *others, slope2 = lax.optimization_barrier((*others, slope2))
        messages = [message, *others]
    else:
        messages = [lax.psum(message, "zone")]

    designs = window_params.shape[0]
    devices = zone_parts * scen_parts * hour_parts
    owners = designs // devices
    pad = -(-owners // 8) * 8
    gain = math.sqrt(width * zones * zone_parts * hours_total * designs)
    (parts,) = call(
        functools.partial(gradient_kernel, hours_total, gain, owners, sources, len(messages)),
        "gradient",
        [((devices, pad, LANES), F32)],
        [*messages, ft1, ft2, slope1, slope0, slope2, near_response, area, plan],
        [
            pltpu.VMEM((width, zones), F32),
            pltpu.VMEM(message.shape, F32),
            pltpu.VMEM((1, ft1.shape[1] + ft2.shape[1]), F32),
        ],
    )
    parts = lax.all_to_all(
        parts, ("zone", "scen", "hour"), split_axis=0, concat_axis=0, tiled=True
    )
    sensitivity, objective = pl.pallas_call(
        functools.partial(finish_kernel, scen_parts, width),
        in_specs=[VMEM],
        out_specs=[VMEM, SMEM],
        out_shape=[
            jax.ShapeDtypeStruct((owners, width), F32),
            jax.ShapeDtypeStruct((1,), F32),
        ],
        compiler_params=params(),
        name="finish",
    )(near(parts))
    return (sensitivity, objective)


def solution(mesh):
    in_specs = (
        P(("groups", "zone", "scen", "hour"), None, None),
        P("hour", None, ("groups", "zone")),
        P("groups", None),
        P(("groups", "zone")),
        P("groups"),
        P("hour", ("groups", "zone")),
        P(("groups", "zone")),
    )
    out_specs = (P(("groups", "zone", "scen", "hour"), None), P("groups"))
    return jax.shard_map(
        on_device, mesh=mesh, in_specs=in_specs, out_specs=out_specs, check_vma=False
    )
```

```python
import functools
import math

import jax
import jax.numpy as jnp
from jax import lax
from jax.experimental import pallas as pl
from jax.experimental.pallas import tpu as pltpu
from jax.sharding import PartitionSpec as P

SHARPNESS = 200.0
MINUS_LOG2_E = -1.0 / math.log(2.0)
EDGE = 2.0 * math.cosh(0.5)
LANES = 128
DEPTH = 128
ZONE_TILE = 256
SHORT = pl.CostEstimate(flops=1, bytes_accessed=1, transcendentals=0)
VMEM = pl.BlockSpec(memory_space=pltpu.VMEM)
SMEM = pl.BlockSpec(memory_space=pltpu.SMEM)
F32 = jnp.float32
BF16 = jnp.bfloat16


def params():
    return pltpu.CompilerParams(vmem_limit_bytes=20 * 2**20)


def near(x):
    return pltpu.with_memory_space_constraint(x, pltpu.VMEM)


def call(kernel, name, outs, args, scratch=(), cost=None):
    return pl.pallas_call(
        kernel,
        in_specs=[VMEM] * len(args),
        out_specs=[VMEM] * len(outs),
        out_shape=[pltpu.MemorySpace.VMEM(shape, kind) for shape, kind in outs],
        scratch_shapes=list(scratch),
        compiler_params=params(),
        cost_estimate=cost,
        name=name,
    )(*[near(a) for a in args])


def coeff_kernel(
    map_hbm, owner_hbm, wp_hbm, band_hbm, area_hbm, resp_hbm, rhs_ref, plan_ref, area_ref, resp_ref,
    map_ref, owner_ref, wp_ref, band_ref, zp_ref, sems, resp_sems,
):
    hours, width, zones = resp_ref.shape
    pieces = resp_sems.shape[0]
    span = hours // pieces
    small = [
        pltpu.make_async_copy(source, target, sems.at[i])
        for i, (source, target) in enumerate(
            (
                (map_hbm, map_ref),
                (owner_hbm, owner_ref),
                (wp_hbm, wp_ref),
                (band_hbm, band_ref),
                (area_hbm, area_ref),
            )
        )
    ]
    for copy in small:
        copy.start()
    large = []
    for i in range(pieces):
        part = pl.ds(i * span, span)
        large.append(
            pltpu.make_async_copy(resp_hbm.at[part], resp_ref.at[part], resp_sems.at[i])
        )
        large[-1].start()
    for copy in small:
        copy.wait()
    place = map_ref[...]
    row, lane = place // LANES, place % LANES

    def look(i, found):
        table = jnp.broadcast_to(owner_ref[pl.ds(i, 1), :], place.shape)
        here = jnp.take_along_axis(table, lane, axis=1, mode="promise_in_bounds")
        return jnp.where(row == i, here, found)

    plan = lax.fori_loop(0, owner_ref.shape[0], look, jnp.zeros_like(place))
    for r in range(plan.shape[0]):
        plan_ref[:, r * LANES : (r + 1) * LANES] = plan[r : r + 1, :]
    designs = wp_ref.shape[0]
    onehot = (
        lax.broadcasted_iota(jnp.int32, (designs, zones), 0) == plan_ref[...]
    ).astype(F32).astype(BF16)
    rest = wp_ref[...]
    total = jnp.zeros((width, zones), F32)
    for _ in range(3):
        part = rest.astype(BF16)
        rest = rest - part.astype(F32)
        total = total + lax.dot_general(
            part, onehot, (((0,), (0,)), ((), ())), preferred_element_type=F32
        )
    zp_ref[...] = total
    extra = lax.broadcasted_iota(jnp.int32, (16, zones), 0)
    blank = jnp.zeros((DEPTH - width - 16, zones), BF16)

    def pair_step(j, carry):
        for k in range(2):
            h = 2 * j + k
            at = k * DEPTH
            coeff = resp_ref[h].astype(F32) * zp_ref[...]
            rhs_ref[j, at : at + width, :] = coeff.astype(BF16)
            middle = 0.25 * (band_ref[pl.ds(h, 1), :].astype(F32) - 3.5)
            tail = jnp.where(extra == 0, -middle, jnp.where(extra == 1, 1.0, 0.0))
            rhs_ref[j, at + width : at + width + 16, :] = tail.astype(BF16)
            rhs_ref[j, at + width + 16 : at + DEPTH, :] = blank
        return carry

    for i in range(pieces):
        large[i].wait()
        lax.fori_loop(i * span // 2, (i + 1) * span // 2, pair_step, 0, unroll=span // 2)


def coefficients(building_map, owner_ids, window_params, band_ids, floor_area, response):
    hours, width, zones = response.shape
    args = [
        building_map.reshape(-1, LANES),
        owner_ids.reshape(-1, LANES),
        window_params,
        band_ids,
        floor_area.reshape(1, zones),
        response,
    ]
    outs = [
        ((hours // 2, 2 * DEPTH, zones), BF16),
        ((1, zones), jnp.int32),
        ((1, zones), F32),
        (response.shape, BF16),
    ]
    return pl.pallas_call(
        coeff_kernel,
        in_specs=[pl.BlockSpec(memory_space=pl.ANY)] * len(args),
        out_specs=[VMEM] * len(outs),
        out_shape=[pltpu.MemorySpace.VMEM(shape, kind) for shape, kind in outs],
        scratch_shapes=[pltpu.VMEM(a.shape, a.dtype) for a in args[:4]]
        + [
            pltpu.VMEM((width, zones), F32),
            pltpu.SemaphoreType.DMA((5,)),
            pltpu.SemaphoreType.DMA((4,)),
        ],
        compiler_params=params(),
        cost_estimate=SHORT,
        name="coefficients",
    )(*[pltpu.with_memory_space_constraint(a, pltpu.HBM) for a in args])


def drivers(pair, second, fill):
    half = pair.shape[1] // 2
    lane = lax.broadcasted_iota(jnp.int32, pair.shape, 1)
    if second:
        pair = pltpu.roll(pair.astype(F32), half, 1).astype(BF16)
    rest = jnp.zeros(pair.shape, F32)
    for spot, value in enumerate(fill):
        rest = jnp.where(lane == half + spot, value, rest)
    return jnp.where(lane < half, pair, rest.astype(BF16))


def here():
    core = lax.axis_index("hour")
    return core, lax.axis_index("zone") * lax.axis_size("hour") + core


def occupancy(hour, hours_total):
    return 1.0 + 2.0 * hour.astype(F32) / (hours_total - 1)


def scan_kernel(kind, hours_total, chunks, extra, sources, priors, unroll, *refs):
    with_loss, with_slope, with_turn = "loss" in kind, "slope" in kind, "turn" in kind
    f_refs, refs = refs[:chunks], refs[chunks:]
    turn_refs, refs = [*refs[:extra], *f_refs], refs[extra:]
    rhs_ref, area_ref, refs = refs[0], refs[1], refs[2:]
    prior_refs, refs = refs[:priors], refs[priors:]
    if with_loss:
        out_ref, refs = refs[0], refs[1:]
    if with_slope:
        slope_ref, refs = refs[0], refs[1:]
    if with_turn:
        ft_ref, refs = refs[0], refs[1:]
    if with_loss:
        acc_ref = refs[0]
        acc_ref[...] = jnp.zeros_like(acc_ref)
    pairs, _, zones = rhs_ref.shape
    hours = 2 * pairs
    core, me = here()

    def rows_of(parts, at):
        parts = [part[:, at] for part in parts]
        return parts[0] if len(parts) == 1 else jnp.concatenate(parts, axis=0)

    def pair_step(j, carry):
        at = pl.ds(pl.multiple_of(j * LANES, LANES), LANES)
        pair = rows_of(f_refs, at)
        if with_turn:
            ft_ref[at, :] = rows_of(turn_refs, at).T
        rows = pair.shape[0]
        fill = (0.5,) if with_loss else (0.5, 0.25)
        pair = (pair.astype(F32) * 0.5).astype(BF16)
        none = jnp.zeros(pair.shape, BF16)
        lhs = jnp.concatenate(
            [
                jnp.concatenate([drivers(pair, False, fill), none], axis=1),
                jnp.concatenate([none, drivers(pair, True, fill)], axis=1),
            ],
            axis=0,
        )
        summed = None
        for z in range(0, zones, ZONE_TILE):
            v = jnp.dot(lhs, rhs_ref[j, :, z : z + ZONE_TILE], preferred_element_type=F32)
            if with_loss:
                a = jnp.abs(v) * (2.0 * MINUS_LOG2_E)
                q = jnp.exp2(a)
                pen = jnp.log2((q + EDGE) * q + 1.0) - a
                pen = pen * area_ref[:, z : z + ZONE_TILE]
                for c in range(0, ZONE_TILE, LANES):
                    piece = pen[:, c : c + LANES]
                    summed = piece if summed is None else summed + piece
            if with_slope:
                if with_loss:
                    slope = jnp.tanh(v + 0.25) + jnp.tanh(v - 0.25)
                else:
                    slope = jnp.tanh(v) + jnp.tanh(v - 0.5)
                slope = slope.astype(BF16)
                slope_ref[2 * j, :, z : z + ZONE_TILE] = slope[:rows]
                slope_ref[2 * j + 1, :, z : z + ZONE_TILE] = slope[rows:]
        if with_loss:
            first = core * hours + 2 * j
            acc_ref[...] += summed[:rows] * occupancy(first, hours_total) + summed[
                rows:
            ] * occupancy(first + 1, hours_total)
        return carry

    lax.fori_loop(0, pairs, pair_step, 0, unroll=unroll)

    if with_loss:
        row = jnp.sum(acc_ref[...].T, axis=0, keepdims=True)
        if not priors:
            out_ref[...] = jnp.broadcast_to(row, out_ref.shape)
        else:
            known = [ref[0:1, :] for ref in prior_refs] + [row]
            chunk = sum(part.shape[1] for part in known) // sources
            pieces = [
                part[:, first : first + chunk]
                for part in known
                for first in range(0, part.shape[1], chunk)
            ]
            occ_sum = hours * 1.0 + (
                2.0 * (core * hours * hours + hours * (hours - 1) // 2)
            ).astype(F32) / (hours_total - 1)
            weight = jnp.sum(area_ref[...]) * occ_sum
            message = jnp.zeros(out_ref.shape, F32) + weight
            index = lax.broadcasted_iota(jnp.int32, message.shape, 0)
            blank = jnp.zeros((1, LANES - chunk), F32)
            for m, piece in enumerate(pieces):
                piece = jnp.concatenate([piece, blank], axis=1)
                message = jnp.where(index == (me ^ m), piece, message)
            out_ref[...] = message


def scan(kind, rows_in, rhs, area, hours_total, sources, extra=(), priors=(), unroll=6, cost=None):
    hours, zones = 2 * rhs.shape[0], rhs.shape[2]
    rows = sum(f.shape[0] for f in rows_in)
    outs = []
    scratch = []
    if "loss" in kind:
        sublanes = -(-(sources + 1) // 8) * 8
        outs.append(((sublanes, LANES) if priors else (8, rows), F32))
        scratch.append(pltpu.VMEM((rows, LANES), F32))
    if "slope" in kind:
        outs.append(((hours, rows, zones), BF16))
    if "turn" in kind:
        outs.append(((rows_in[0].shape[1], rows + sum(f.shape[0] for f in extra)), BF16))
    return call(
        functools.partial(
            scan_kernel, kind, hours_total, len(rows_in), len(extra), sources, len(priors), unroll
        ),
        kind,
        outs,
        [*rows_in, *extra, rhs, area, *priors],
        scratch,
        cost,
    )


def gradient_kernel(
    hours_total, gain, owners, sources, messages, *refs
):
    msg_refs, refs = refs[:messages], refs[messages:]
    ft_refs, slope_refs, refs = refs[:2], refs[2:5], refs[5:]
    resp_ref, area_ref, plan_ref, out_ref, acc_ref, score_ref, e_ref = refs
    hours, width, zones = resp_ref.shape
    core, me = here()
    chunk = e_ref.shape[1] // sources
    total = [msg_ref[...] for msg_ref in msg_refs]
    while len(total) > 1:
        total = [first + second for first, second in zip(total[::2], total[1::2])]
    total = total[0]
    weight = jnp.max(total[sources : sources + 1, :])
    score = total * (SHARPNESS * math.log(2.0) / weight)
    rows = lax.broadcasted_iota(jnp.int32, score.shape, 0)
    lanes = lax.broadcasted_iota(jnp.int32, score.shape, 1)
    valid = (rows < sources) & (lanes < chunk)
    peak = jnp.max(jnp.where(valid, score, -jnp.inf))
    e = jnp.where(valid, jnp.exp(jnp.where(valid, score - peak, 0.0)), 0.0)
    exp_total = jnp.sum(e)
    score_ref[...] = e
    quarter = sources // 4
    order = [q * quarter + m for q in (1, 2, 0, 3) for m in range(quarter)]
    for spot, m in enumerate(order):
        piece = score_ref[pl.ds(me ^ m, 1), :]
        e_ref[:, spot * chunk : (spot + 1) * chunk] = piece[:, :chunk]
    acc_ref[...] = jnp.zeros_like(acc_ref)

    def hour_step(h, carry):
        occ = occupancy(core * hours + h, hours_total)
        at = pl.ds(pl.multiple_of(h * width, width), width)
        ft = jnp.concatenate([ref[at, :] for ref in ft_refs], axis=1).astype(F32)
        ft = ft * (e_ref[...] * occ)
        high = ft.astype(BF16)
        low = (ft - high.astype(F32)).astype(BF16)
        both = jnp.concatenate([high, low], axis=0)
        for z in range(0, zones, ZONE_TILE):
            at = slice(z, z + ZONE_TILE)
            kept = jnp.concatenate([ref[h, :, at] for ref in slope_refs], axis=0)
            mixed = jnp.dot(both, kept, preferred_element_type=F32)
            mixed = mixed[:width] + mixed[width:]
            acc_ref[:, at] += resp_ref[h, :, at].astype(F32) * mixed
        return carry

    lax.fori_loop(0, hours, hour_step, 0, unroll=hours // 2)

    grad = acc_ref[...] * area_ref[...]
    blocks, pad, _ = out_ref.shape
    index = lax.broadcasted_iota(jnp.int32, (blocks * pad, zones), 0)
    within = index % pad
    design = jnp.where(within < owners, (index // pad) * owners + within, -1)
    onehot = (design == plan_ref[...]).astype(F32).astype(BF16)
    sens = jnp.zeros((blocks * pad, width), F32)
    for _ in range(3):
        part = grad.astype(BF16)
        grad = grad - part.astype(F32)
        sens = sens + lax.dot_general(
            onehot, part, (((1,), (1,)), ((), ())), preferred_element_type=F32
        )
    sens = sens * (0.5 * gain / weight)
    out_ref[:, :, :width] = sens.reshape(blocks, pad, width)
    lane = lax.broadcasted_iota(jnp.int32, (blocks, pad, LANES - width), 2)
    out_ref[:, :, width:] = jnp.where(lane == 0, peak, exp_total)


def finish_kernel(scen_parts, width, parts_ref, sens_ref, objective_ref):
    parts = parts_ref[...]
    devices = parts.shape[0]
    peaks = parts[:, :, width : width + 1]
    totals = parts[:, :, width + 1 : width + 2]
    peak = jnp.max(peaks)
    scale = jnp.exp(peaks - peak)
    total = jnp.sum((scale * totals)[:, 0:1, :]) * (scen_parts / devices)
    summed = jnp.sum(parts[:, :, :width] * scale, axis=0) / total
    sens_ref[...] = summed[: sens_ref.shape[0]]
    log_total = jnp.max(jnp.log(jnp.full((8, LANES), total, F32)))
    objective_ref[0] = (peak + log_total) / SHARPNESS - 0.5


def on_device(forcing, response, window_params, building_map, owner_ids, band_ids, floor_area):
    hours, width, zones = response.shape
    hour_parts = lax.axis_size("hour")
    zone_parts = lax.axis_size("zone")
    scen_parts = lax.axis_size("scen")
    hours_total = hours * hour_parts
    core = lax.axis_index("hour")
    sources = zone_parts * hour_parts

    half = hours * width
    everyone = forcing.reshape(forcing.shape[0], hours_total * width)
    keep = lax.dynamic_slice_in_dim(everyone, core * half, half, axis=1)
    leave = lax.dynamic_slice_in_dim(everyone, (1 - core) * half, half, axis=1)
    came = lax.ppermute(leave, "hour", [(0, 1), (1, 0)])

    def swap(x, step):
        return lax.ppermute(x, "zone", [(i, i ^ step) for i in range(zone_parts)])

    came, building_map = lax.optimization_barrier((came, building_map))
    rhs, plan, area, near_response = coefficients(
        building_map, owner_ids, window_params, band_ids, floor_area, response
    )
    if zone_parts == 4:
        mine = jnp.concatenate([keep, came], axis=0)
        far, beside = swap(mine, 2), swap(mine, 1)
        mine = [mine]
    else:
        me = lax.axis_index(("zone", "hour"))
        both = jnp.where(core == 0, jnp.stack([keep, came]), jnp.stack([came, keep]))
        gathered = lax.all_gather(both, "zone", axis=0, tiled=True)
        ordered = jnp.take(gathered, me ^ jnp.arange(sources), axis=0).reshape(4, -1, half)
        mine, beside, far, last = [ordered[0]], ordered[1], ordered[2], ordered[3]
    common = (rhs, area, hours_total, sources)
    loss0, slope0 = scan("loss_slope", mine, *common, cost=SHORT)
    if zone_parts == 4:
        beside, far, loss0 = lax.optimization_barrier((beside, far, loss0))
        last = swap(far, 1)
    loss1, slope1, ft1 = scan("loss_slope_turn", [beside, far], *common)
    (message,) = scan("loss", [last], *common, priors=[loss0, loss1])
    message = message + lax.ppermute(message, "hour", [(0, 1), (1, 0)])
    slope2, ft2 = scan("slope_turn", [last], *common, extra=mine)
    if zone_parts == 4:
        others = [swap(message, k) for k in (1, 2, 3)]
        *others, slope2 = lax.optimization_barrier((*others, slope2))
        messages = [message, *others]
    else:
        messages = [lax.psum(message, "zone")]

    designs = window_params.shape[0]
    devices = zone_parts * scen_parts * hour_parts
    owners = designs // devices
    pad = -(-owners // 8) * 8
    gain = math.sqrt(width * zones * zone_parts * hours_total * designs)
    (parts,) = call(
        functools.partial(gradient_kernel, hours_total, gain, owners, sources, len(messages)),
        "gradient",
        [((devices, pad, LANES), F32)],
        [*messages, ft1, ft2, slope1, slope0, slope2, near_response, area, plan],
        [
            pltpu.VMEM((width, zones), F32),
            pltpu.VMEM(message.shape, F32),
            pltpu.VMEM((1, ft1.shape[1] + ft2.shape[1]), F32),
        ],
    )
    parts = lax.all_to_all(
        parts, ("zone", "scen", "hour"), split_axis=0, concat_axis=0, tiled=True
    )
    sensitivity, objective = pl.pallas_call(
        functools.partial(finish_kernel, scen_parts, width),
        in_specs=[VMEM],
        out_specs=[VMEM, SMEM],
        out_shape=[
            jax.ShapeDtypeStruct((owners, width), F32),
            jax.ShapeDtypeStruct((1,), F32),
        ],
        compiler_params=params(),
        name="finish",
    )(near(parts))
    return (sensitivity, objective)


def solution(mesh):
    in_specs = (
        P(("groups", "zone", "scen", "hour"), None, None),
        P("hour", None, ("groups", "zone")),
        P("groups", None),
        P(("groups", "zone")),
        P("groups"),
        P("hour", ("groups", "zone")),
        P(("groups", "zone")),
    )
    out_specs = (P(("groups", "zone", "scen", "hour"), None), P("groups"))
    return jax.shard_map(
        on_device, mesh=mesh, in_specs=in_specs, out_specs=out_specs, check_vma=False
    )
```

```python
import functools
import math

import jax
import jax.numpy as jnp
from jax import lax
from jax.experimental import pallas as pl
from jax.experimental.pallas import tpu as pltpu
from jax.sharding import PartitionSpec as P

SHARPNESS = 200.0
MINUS_LOG2_E = -1.0 / math.log(2.0)
EDGE = 2.0 * math.cosh(0.5)
LANES = 128
DEPTH = 128
ZONE_TILE = 256
SHORT = pl.CostEstimate(flops=1, bytes_accessed=1, transcendentals=0)
VMEM = pl.BlockSpec(memory_space=pltpu.VMEM)
SMEM = pl.BlockSpec(memory_space=pltpu.SMEM)
F32 = jnp.float32
BF16 = jnp.bfloat16


def params():
    return pltpu.CompilerParams(vmem_limit_bytes=20 * 2**20)


def near(x):
    return pltpu.with_memory_space_constraint(x, pltpu.VMEM)


def call(kernel, name, outs, args, scratch=(), cost=None):
    return pl.pallas_call(
        kernel,
        in_specs=[VMEM] * len(args),
        out_specs=[VMEM] * len(outs),
        out_shape=[pltpu.MemorySpace.VMEM(shape, kind) for shape, kind in outs],
        scratch_shapes=list(scratch),
        compiler_params=params(),
        cost_estimate=cost,
        name=name,
    )(*[near(a) for a in args])


def coeff_kernel(
    map_hbm, owner_hbm, wp_hbm, band_hbm, area_hbm, resp_hbm, rhs_ref, plan_ref, area_ref, resp_ref,
    map_ref, owner_ref, wp_ref, band_ref, zp_ref, sems, resp_sems,
):
    hours, width, zones = resp_ref.shape
    pieces = resp_sems.shape[0]
    span = hours // pieces
    small = [
        pltpu.make_async_copy(source, target, sems.at[i])
        for i, (source, target) in enumerate(
            (
                (map_hbm, map_ref),
                (owner_hbm, owner_ref),
                (wp_hbm, wp_ref),
                (band_hbm, band_ref),
                (area_hbm, area_ref),
            )
        )
    ]
    for copy in small:
        copy.start()
    large = []
    for i in range(pieces):
        part = pl.ds(i * span, span)
        large.append(
            pltpu.make_async_copy(resp_hbm.at[part], resp_ref.at[part], resp_sems.at[i])
        )
        large[-1].start()
    for copy in small:
        copy.wait()
    place = map_ref[...]
    row, lane = place // LANES, place % LANES

    def look(i, found):
        table = jnp.broadcast_to(owner_ref[pl.ds(i, 1), :], place.shape)
        here = jnp.take_along_axis(table, lane, axis=1, mode="promise_in_bounds")
        return jnp.where(row == i, here, found)

    plan = lax.fori_loop(0, owner_ref.shape[0], look, jnp.zeros_like(place))
    for r in range(plan.shape[0]):
        plan_ref[:, r * LANES : (r + 1) * LANES] = plan[r : r + 1, :]
    designs = wp_ref.shape[0]
    onehot = (
        lax.broadcasted_iota(jnp.int32, (designs, zones), 0) == plan_ref[...]
    ).astype(F32).astype(BF16)
    rest = wp_ref[...]
    total = jnp.zeros((width, zones), F32)
    for _ in range(3):
        part = rest.astype(BF16)
        rest = rest - part.astype(F32)
        total = total + lax.dot_general(
            part, onehot, (((0,), (0,)), ((), ())), preferred_element_type=F32
        )
    zp_ref[...] = total
    extra = lax.broadcasted_iota(jnp.int32, (16, zones), 0)
    blank = jnp.zeros((DEPTH - width - 16, zones), BF16)

    def pair_step(j, carry):
        for k in range(2):
            h = 2 * j + k
            at = k * DEPTH
            coeff = resp_ref[h].astype(F32) * zp_ref[...]
            rhs_ref[j, at : at + width, :] = coeff.astype(BF16)
            middle = 0.25 * (band_ref[pl.ds(h, 1), :].astype(F32) - 3.5)
            tail = jnp.where(extra == 0, -middle, jnp.where(extra == 1, 1.0, 0.0))
            rhs_ref[j, at + width : at + width + 16, :] = tail.astype(BF16)
            rhs_ref[j, at + width + 16 : at + DEPTH, :] = blank
        return carry

    for i in range(pieces):
        large[i].wait()
        lax.fori_loop(i * span // 2, (i + 1) * span // 2, pair_step, 0, unroll=span // 2)


def coefficients(building_map, owner_ids, window_params, band_ids, floor_area, response):
    hours, width, zones = response.shape
    args = [
        building_map.reshape(-1, LANES),
        owner_ids.reshape(-1, LANES),
        window_params,
        band_ids,
        floor_area.reshape(1, zones),
        response,
    ]
    outs = [
        ((hours // 2, 2 * DEPTH, zones), BF16),
        ((1, zones), jnp.int32),
        ((1, zones), F32),
        (response.shape, BF16),
    ]
    return pl.pallas_call(
        coeff_kernel,
        in_specs=[pl.BlockSpec(memory_space=pl.ANY)] * len(args),
        out_specs=[VMEM] * len(outs),
        out_shape=[pltpu.MemorySpace.VMEM(shape, kind) for shape, kind in outs],
        scratch_shapes=[pltpu.VMEM(a.shape, a.dtype) for a in args[:4]]
        + [
            pltpu.VMEM((width, zones), F32),
            pltpu.SemaphoreType.DMA((5,)),
            pltpu.SemaphoreType.DMA((4,)),
        ],
        compiler_params=params(),
        cost_estimate=SHORT,
        name="coefficients",
    )(*[pltpu.with_memory_space_constraint(a, pltpu.HBM) for a in args])


def drivers(pair, second, fill):
    half = pair.shape[1] // 2
    lane = lax.broadcasted_iota(jnp.int32, pair.shape, 1)
    if second:
        pair = pltpu.roll(pair.astype(F32), half, 1).astype(BF16)
    rest = jnp.zeros(pair.shape, F32)
    for spot, value in enumerate(fill):
        rest = jnp.where(lane == half + spot, value, rest)
    return jnp.where(lane < half, pair, rest.astype(BF16))


def here():
    core = lax.axis_index("hour")
    return core, lax.axis_index("zone") * lax.axis_size("hour") + core


def occupancy(hour, hours_total):
    return 1.0 + 2.0 * hour.astype(F32) / (hours_total - 1)


def scan_kernel(kind, hours_total, chunks, extra, sources, priors, unroll, *refs):
    with_loss, with_slope, with_turn = "loss" in kind, "slope" in kind, "turn" in kind
    f_refs, refs = refs[:chunks], refs[chunks:]
    turn_refs, refs = [*refs[:extra], *f_refs], refs[extra:]
    rhs_ref, area_ref, refs = refs[0], refs[1], refs[2:]
    prior_refs, refs = refs[:priors], refs[priors:]
    if with_loss:
        out_ref, refs = refs[0], refs[1:]
    if with_slope:
        slope_ref, refs = refs[0], refs[1:]
    if with_turn:
        ft_ref, refs = refs[0], refs[1:]
    if with_loss:
        acc_ref = refs[0]
        acc_ref[...] = jnp.zeros_like(acc_ref)
    pairs, _, zones = rhs_ref.shape
    hours = 2 * pairs
    core, me = here()

    def rows_of(parts, at):
        parts = [part[:, at] for part in parts]
        return parts[0] if len(parts) == 1 else jnp.concatenate(parts, axis=0)

    def pair_step(j, carry):
        at = pl.ds(pl.multiple_of(j * LANES, LANES), LANES)
        pair = rows_of(f_refs, at)
        if with_turn:
            ft_ref[at, :] = rows_of(turn_refs, at).T
        rows = pair.shape[0]
        fill = (0.5,) if with_loss else (0.5, 0.25)
        pair = (pair.astype(F32) * 0.5).astype(BF16)
        none = jnp.zeros(pair.shape, BF16)
        lhs = jnp.concatenate(
            [
                jnp.concatenate([drivers(pair, False, fill), none], axis=1),
                jnp.concatenate([none, drivers(pair, True, fill)], axis=1),
            ],
            axis=0,
        )
        summed = None
        for z in range(0, zones, ZONE_TILE):
            v = jnp.dot(lhs, rhs_ref[j, :, z : z + ZONE_TILE], preferred_element_type=F32)
            if with_loss:
                a = jnp.abs(v) * (2.0 * MINUS_LOG2_E)
                q = jnp.exp2(a)
                pen = jnp.log2((q + EDGE) * q + 1.0) - a
                pen = pen * area_ref[:, z : z + ZONE_TILE]
                for c in range(0, ZONE_TILE, LANES):
                    piece = pen[:, c : c + LANES]
                    summed = piece if summed is None else summed + piece
            if with_slope:
                if with_loss:
                    slope = jnp.tanh(v + 0.25) + jnp.tanh(v - 0.25)
                else:
                    slope = jnp.tanh(v) + jnp.tanh(v - 0.5)
                slope = slope.astype(BF16)
                slope_ref[2 * j, :, z : z + ZONE_TILE] = slope[:rows]
                slope_ref[2 * j + 1, :, z : z + ZONE_TILE] = slope[rows:]
        if with_loss:
            first = core * hours + 2 * j
            acc_ref[...] += summed[:rows] * occupancy(first, hours_total) + summed[
                rows:
            ] * occupancy(first + 1, hours_total)
        return carry

    lax.fori_loop(0, pairs, pair_step, 0, unroll=unroll)

    if with_loss:
        row = jnp.sum(acc_ref[...].T, axis=0, keepdims=True)
        if not priors:
            out_ref[...] = jnp.broadcast_to(row, out_ref.shape)
        else:
            known = [ref[0:1, :] for ref in prior_refs] + [row]
            chunk = sum(part.shape[1] for part in known) // sources
            pieces = [
                part[:, first : first + chunk]
                for part in known
                for first in range(0, part.shape[1], chunk)
            ]
            occ_sum = hours * 1.0 + (
                2.0 * (core * hours * hours + hours * (hours - 1) // 2)
            ).astype(F32) / (hours_total - 1)
            weight = jnp.sum(area_ref[...]) * occ_sum
            message = jnp.zeros(out_ref.shape, F32) + weight
            index = lax.broadcasted_iota(jnp.int32, message.shape, 0)
            blank = jnp.zeros((1, LANES - chunk), F32)
            for m, piece in enumerate(pieces):
                piece = jnp.concatenate([piece, blank], axis=1)
                message = jnp.where(index == (me ^ m), piece, message)
            out_ref[...] = message


def scan(kind, rows_in, rhs, area, hours_total, sources, extra=(), priors=(), unroll=6, cost=None):
    hours, zones = 2 * rhs.shape[0], rhs.shape[2]
    rows = sum(f.shape[0] for f in rows_in)
    outs = []
    scratch = []
    if "loss" in kind:
        sublanes = -(-(sources + 1) // 8) * 8
        outs.append(((sublanes, LANES) if priors else (8, rows), F32))
        scratch.append(pltpu.VMEM((rows, LANES), F32))
    if "slope" in kind:
        outs.append(((hours, rows, zones), BF16))
    if "turn" in kind:
        outs.append(((rows_in[0].shape[1], rows + sum(f.shape[0] for f in extra)), BF16))
    return call(
        functools.partial(
            scan_kernel, kind, hours_total, len(rows_in), len(extra), sources, len(priors), unroll
        ),
        kind,
        outs,
        [*rows_in, *extra, rhs, area, *priors],
        scratch,
        cost,
    )


def gradient_kernel(
    hours_total, gain, owners, sources, messages, *refs
):
    msg_refs, refs = refs[:messages], refs[messages:]
    ft_refs, slope_refs, refs = refs[:2], refs[2:6], refs[6:]
    resp_ref, area_ref, plan_ref, out_ref, acc_ref, score_ref, e_ref = refs
    hours, width, zones = resp_ref.shape
    core, me = here()
    chunk = e_ref.shape[1] // sources
    total = [msg_ref[...] for msg_ref in msg_refs]
    while len(total) > 1:
        total = [first + second for first, second in zip(total[::2], total[1::2])]
    total = total[0]
    weight = jnp.max(total[sources : sources + 1, :])
    score = total * (SHARPNESS * math.log(2.0) / weight)
    rows = lax.broadcasted_iota(jnp.int32, score.shape, 0)
    lanes = lax.broadcasted_iota(jnp.int32, score.shape, 1)
    valid = (rows < sources) & (lanes < chunk)
    peak = jnp.max(jnp.where(valid, score, -jnp.inf))
    e = jnp.where(valid, jnp.exp(jnp.where(valid, score - peak, 0.0)), 0.0)
    exp_total = jnp.sum(e)
    score_ref[...] = e
    quarter = sources // 4
    order = [q * quarter + m for q in (0, 2, 1, 3) for m in range(quarter)]
    for spot, m in enumerate(order):
        piece = score_ref[pl.ds(me ^ m, 1), :]
        e_ref[:, spot * chunk : (spot + 1) * chunk] = piece[:, :chunk]
    acc_ref[...] = jnp.zeros_like(acc_ref)

    def hour_step(h, carry):
        occ = occupancy(core * hours + h, hours_total)
        at = pl.ds(pl.multiple_of(h * width, width), width)
        ft = jnp.concatenate([ref[at, :] for ref in ft_refs], axis=1).astype(F32)
        ft = ft * (e_ref[...] * occ)
        high = ft.astype(BF16)
        low = (ft - high.astype(F32)).astype(BF16)
        both = jnp.concatenate([high, low], axis=0)
        for z in range(0, zones, ZONE_TILE):
            at = slice(z, z + ZONE_TILE)
            kept = jnp.concatenate([ref[h, :, at] for ref in slope_refs], axis=0)
            mixed = jnp.dot(both, kept, preferred_element_type=F32)
            mixed = mixed[:width] + mixed[width:]
            acc_ref[:, at] += resp_ref[h, :, at].astype(F32) * mixed
        return carry

    lax.fori_loop(0, hours, hour_step, 0, unroll=hours // 2)

    grad = acc_ref[...] * area_ref[...]
    blocks, pad, _ = out_ref.shape
    index = lax.broadcasted_iota(jnp.int32, (blocks * pad, zones), 0)
    within = index % pad
    design = jnp.where(within < owners, (index // pad) * owners + within, -1)
    onehot = (design == plan_ref[...]).astype(F32).astype(BF16)
    sens = jnp.zeros((blocks * pad, width), F32)
    for _ in range(3):
        part = grad.astype(BF16)
        grad = grad - part.astype(F32)
        sens = sens + lax.dot_general(
            onehot, part, (((1,), (1,)), ((), ())), preferred_element_type=F32
        )
    sens = sens * (0.5 * gain / weight)
    out_ref[:, :, :width] = sens.reshape(blocks, pad, width)
    lane = lax.broadcasted_iota(jnp.int32, (blocks, pad, LANES - width), 2)
    out_ref[:, :, width:] = jnp.where(lane == 0, peak, exp_total)


def finish_kernel(scen_parts, width, parts_ref, sens_ref, objective_ref):
    parts = parts_ref[...]
    devices = parts.shape[0]
    peaks = parts[:, :, width : width + 1]
    totals = parts[:, :, width + 1 : width + 2]
    peak = jnp.max(peaks)
    scale = jnp.exp(peaks - peak)
    total = jnp.sum((scale * totals)[:, 0:1, :]) * (scen_parts / devices)
    summed = jnp.sum(parts[:, :, :width] * scale, axis=0) / total
    sens_ref[...] = summed[: sens_ref.shape[0]]
    log_total = jnp.max(jnp.log(jnp.full((8, LANES), total, F32)))
    objective_ref[0] = (peak + log_total) / SHARPNESS - 0.5


def on_device(forcing, response, window_params, building_map, owner_ids, band_ids, floor_area):
    hours, width, zones = response.shape
    hour_parts = lax.axis_size("hour")
    zone_parts = lax.axis_size("zone")
    scen_parts = lax.axis_size("scen")
    hours_total = hours * hour_parts
    core = lax.axis_index("hour")
    sources = zone_parts * hour_parts

    half = hours * width
    everyone = forcing.reshape(forcing.shape[0], hours_total * width)
    keep = lax.dynamic_slice_in_dim(everyone, core * half, half, axis=1)
    leave = lax.dynamic_slice_in_dim(everyone, (1 - core) * half, half, axis=1)
    came = lax.ppermute(leave, "hour", [(0, 1), (1, 0)])

    def swap(x, step):
        return lax.ppermute(x, "zone", [(i, i ^ step) for i in range(zone_parts)])

    came, building_map = lax.optimization_barrier((came, building_map))
    rhs, plan, area, near_response = coefficients(
        building_map, owner_ids, window_params, band_ids, floor_area, response
    )
    if zone_parts == 4:
        mine = jnp.concatenate([keep, came], axis=0)
        far0, far1, beside = swap(keep, 2), swap(came, 2), swap(mine, 1)
    else:
        me = lax.axis_index(("zone", "hour"))
        both = jnp.where(core == 0, jnp.stack([keep, came]), jnp.stack([came, keep]))
        gathered = lax.all_gather(both, "zone", axis=0, tiled=True)
        ordered = jnp.take(gathered, me ^ jnp.arange(sources), axis=0).reshape(4, -1, half)
        mine, beside, far, last = ordered
    common = (rhs, area, hours_total, sources)
    loss0, slope0 = scan("loss_slope", [mine], *common, cost=SHORT)
    if zone_parts == 4:
        far0, far1, loss0 = lax.optimization_barrier((far0, far1, loss0))
        far = jnp.concatenate([far0, far1], axis=0)
        last = swap(far, 1)
    loss2, slope2, ft0 = scan("loss_slope_turn", [far], *common, extra=[mine])
    beside, loss2 = lax.optimization_barrier((beside, loss2))
    loss1, slope1 = scan("loss_slope", [beside], *common)
    (message,) = scan("loss", [last], *common, priors=[loss0, loss1, loss2])
    message = message + lax.ppermute(message, "hour", [(0, 1), (1, 0)])
    slope3, ft1 = scan("slope_turn", [last], *common, extra=[beside])
    if zone_parts == 4:
        others = [swap(message, k) for k in (1, 2, 3)]
        *others, slope3 = lax.optimization_barrier((*others, slope3))
        messages = [message, *others]
    else:
        messages = [lax.psum(message, "zone")]

    designs = window_params.shape[0]
    devices = zone_parts * scen_parts * hour_parts
    owners = designs // devices
    pad = -(-owners // 8) * 8
    gain = math.sqrt(width * zones * zone_parts * hours_total * designs)
    (parts,) = call(
        functools.partial(gradient_kernel, hours_total, gain, owners, sources, len(messages)),
        "gradient",
        [((devices, pad, LANES), F32)],
        [*messages, ft0, ft1, slope0, slope2, slope1, slope3, near_response, area, plan],
        [
            pltpu.VMEM((width, zones), F32),
            pltpu.VMEM(message.shape, F32),
            pltpu.VMEM((1, ft0.shape[1] + ft1.shape[1]), F32),
        ],
    )
    parts = lax.all_to_all(
        parts, ("zone", "scen", "hour"), split_axis=0, concat_axis=0, tiled=True
    )
    sensitivity, objective = pl.pallas_call(
        functools.partial(finish_kernel, scen_parts, width),
        in_specs=[VMEM],
        out_specs=[VMEM, SMEM],
        out_shape=[
            jax.ShapeDtypeStruct((owners, width), F32),
            jax.ShapeDtypeStruct((1,), F32),
        ],
        compiler_params=params(),
        name="finish",
    )(near(parts))
    return (sensitivity, objective)


def solution(mesh):
    in_specs = (
        P(("groups", "zone", "scen", "hour"), None, None),
        P("hour", None, ("groups", "zone")),
        P("groups", None),
        P(("groups", "zone")),
        P("groups"),
        P("hour", ("groups", "zone")),
        P(("groups", "zone")),
    )
    out_specs = (P(("groups", "zone", "scen", "hour"), None), P("groups"))
    return jax.shard_map(
        on_device, mesh=mesh, in_specs=in_specs, out_specs=out_specs, check_vma=False
    )
```

```python
import functools
import math

import jax
import jax.numpy as jnp
from jax import lax
from jax.experimental import pallas as pl
from jax.experimental.pallas import tpu as pltpu
from jax.sharding import PartitionSpec as P

SHARPNESS = 200.0
MINUS_LOG2_E = -1.0 / math.log(2.0)
EDGE = 2.0 * math.cosh(0.5)
LANES = 128
DEPTH = 128
ZONE_TILE = 256
SHORT = pl.CostEstimate(flops=1, bytes_accessed=1, transcendentals=0)
VMEM = pl.BlockSpec(memory_space=pltpu.VMEM)
SMEM = pl.BlockSpec(memory_space=pltpu.SMEM)
F32 = jnp.float32
BF16 = jnp.bfloat16


def params():
    return pltpu.CompilerParams(vmem_limit_bytes=20 * 2**20)


def near(x):
    return pltpu.with_memory_space_constraint(x, pltpu.VMEM)


def call(kernel, name, outs, args, scratch=(), cost=None):
    return pl.pallas_call(
        kernel,
        in_specs=[VMEM] * len(args),
        out_specs=[VMEM] * len(outs),
        out_shape=[pltpu.MemorySpace.VMEM(shape, kind) for shape, kind in outs],
        scratch_shapes=list(scratch),
        compiler_params=params(),
        cost_estimate=cost,
        name=name,
    )(*[near(a) for a in args])


def open_kernel(
    hours_total, mine_ref, map_hbm, owner_hbm, wp_hbm, band_hbm, area_hbm, resp_hbm,
    rhs_ref, plan_ref, area_ref, resp_ref, loss_ref, slope_ref,
    map_ref, owner_ref, wp_ref, band_ref, zp_ref, acc_ref, sems, resp_sems,
):
    hours, width, zones = resp_ref.shape
    pieces = resp_sems.shape[0]
    span = hours // pieces
    small = [
        pltpu.make_async_copy(source, target, sems.at[i])
        for i, (source, target) in enumerate(
            (
                (map_hbm, map_ref),
                (owner_hbm, owner_ref),
                (wp_hbm, wp_ref),
                (band_hbm, band_ref),
                (area_hbm, area_ref),
            )
        )
    ]
    for copy in small:
        copy.start()
    large = []
    for i in range(pieces):
        part = pl.ds(i * span, span)
        large.append(
            pltpu.make_async_copy(resp_hbm.at[part], resp_ref.at[part], resp_sems.at[i])
        )
        large[-1].start()
    for copy in small:
        copy.wait()
    place = map_ref[...]
    row, lane = place // LANES, place % LANES

    def look(i, found):
        table = jnp.broadcast_to(owner_ref[pl.ds(i, 1), :], place.shape)
        here = jnp.take_along_axis(table, lane, axis=1, mode="promise_in_bounds")
        return jnp.where(row == i, here, found)

    plan = lax.fori_loop(0, owner_ref.shape[0], look, jnp.zeros_like(place), unroll=8)
    for r in range(plan.shape[0]):
        plan_ref[:, r * LANES : (r + 1) * LANES] = plan[r : r + 1, :]
    designs = wp_ref.shape[0]
    onehot = (
        lax.broadcasted_iota(jnp.int32, (designs, zones), 0) == plan_ref[...]
    ).astype(F32).astype(BF16)
    rest = wp_ref[...]
    exact = []
    for _ in range(3):
        exact.append(rest.astype(BF16))
        rest = rest - exact[-1].astype(F32)
    zp_ref[...] = lax.dot_general(
        jnp.concatenate(exact, axis=0),
        jnp.concatenate([onehot] * 3, axis=0),
        (((0,), (0,)), ((), ())),
        preferred_element_type=F32,
    )
    extra = lax.broadcasted_iota(jnp.int32, (16, zones), 0)
    blank = jnp.zeros((DEPTH - width - 16, zones), BF16)
    core, _ = here()
    acc_ref[...] = jnp.zeros_like(acc_ref)

    def pair_step(j, carry):
        depth = []
        for k in range(2):
            h = 2 * j + k
            coeff = (resp_ref[h].astype(F32) * zp_ref[...]).astype(BF16)
            middle = 0.25 * (band_ref[pl.ds(h, 1), :].astype(F32) - 3.5)
            tail = jnp.where(extra == 0, -middle, jnp.where(extra == 1, 1.0, 0.0))
            depth += [coeff, tail.astype(BF16), blank]
        rhs = jnp.concatenate(depth, axis=0)
        rhs_ref[j] = rhs
        pair = mine_ref[:, pl.ds(pl.multiple_of(j * LANES, LANES), LANES)]
        summed = pair_work("loss_slope", pair, lambda at: rhs[:, at], area_ref, slope_ref, j)
        acc_ref[...] += hour_weighted(summed, core, hours, hours_total, j)
        return carry

    for i in range(pieces):
        large[i].wait()
        lax.fori_loop(i * span // 2, (i + 1) * span // 2, pair_step, 0, unroll=span // 2)
    loss_ref[...] = jnp.broadcast_to(
        jnp.sum(acc_ref[...].T, axis=0, keepdims=True), loss_ref.shape
    )


def opening(
    mine, building_map, owner_ids, window_params, band_ids, floor_area, response, hours_total
):
    hours, width, zones = response.shape
    args = [
        building_map.reshape(-1, LANES),
        owner_ids.reshape(-1, LANES),
        window_params,
        band_ids,
        floor_area.reshape(1, zones),
        response,
    ]
    outs = [
        ((hours // 2, 2 * DEPTH, zones), BF16),
        ((1, zones), jnp.int32),
        ((1, zones), F32),
        (response.shape, BF16),
        ((8, mine.shape[0]), F32),
        ((hours, mine.shape[0], zones), BF16),
    ]
    return pl.pallas_call(
        functools.partial(open_kernel, hours_total),
        in_specs=[VMEM] + [pl.BlockSpec(memory_space=pl.ANY)] * len(args),
        out_specs=[VMEM] * len(outs),
        out_shape=[pltpu.MemorySpace.VMEM(shape, kind) for shape, kind in outs],
        scratch_shapes=[pltpu.VMEM(a.shape, a.dtype) for a in args[:4]]
        + [
            pltpu.VMEM((width, zones), F32),
            pltpu.VMEM((mine.shape[0], LANES), F32),
            pltpu.SemaphoreType.DMA((5,)),
            pltpu.SemaphoreType.DMA((2,)),
        ],
        compiler_params=params(),
        cost_estimate=SHORT,
        name="opening",
    )(near(mine), *[pltpu.with_memory_space_constraint(a, pltpu.HBM) for a in args])


def drivers(pair, second, fill):
    half = pair.shape[1] // 2
    lane = lax.broadcasted_iota(jnp.int32, pair.shape, 1)
    if second:
        pair = pltpu.roll(pair.astype(F32), half, 1).astype(BF16)
    rest = jnp.zeros(pair.shape, F32)
    for spot, value in enumerate(fill):
        rest = jnp.where(lane == half + spot, value, rest)
    return jnp.where(lane < half, pair, rest.astype(BF16))


def here():
    core = lax.axis_index("hour")
    return core, lax.axis_index("zone") * lax.axis_size("hour") + core


def occupancy(hour, hours_total):
    return 1.0 + 2.0 * hour.astype(F32) / (hours_total - 1)


def pair_work(kind, pair, rhs_at, area_ref, slope_ref, j):
    with_loss, with_slope = "loss" in kind, "slope" in kind
    zones = area_ref.shape[1]
    rows = pair.shape[0]
    fill = (0.5,) if with_loss else (0.5, 0.25)
    pair = (pair.astype(F32) * 0.5).astype(BF16)
    none = jnp.zeros(pair.shape, BF16)
    lhs = jnp.concatenate(
        [
            jnp.concatenate([drivers(pair, False, fill), none], axis=1),
            jnp.concatenate([none, drivers(pair, True, fill)], axis=1),
        ],
        axis=0,
    )
    summed = None
    for z in range(0, zones, ZONE_TILE):
        v = jnp.dot(lhs, rhs_at(slice(z, z + ZONE_TILE)), preferred_element_type=F32)
        if with_loss:
            a = jnp.abs(v) * (2.0 * MINUS_LOG2_E)
            q = jnp.exp2(a)
            pen = jnp.log2((q + EDGE) * q + 1.0) - a
            pen = pen * area_ref[:, z : z + ZONE_TILE]
            for c in range(0, ZONE_TILE, LANES):
                piece = pen[:, c : c + LANES]
                summed = piece if summed is None else summed + piece
        if with_slope:
            if with_loss:
                slope = jnp.tanh(v + 0.25) + jnp.tanh(v - 0.25)
            else:
                slope = jnp.tanh(v) + jnp.tanh(v - 0.5)
            slope = slope.astype(BF16)
            slope_ref[2 * j, :, z : z + ZONE_TILE] = slope[:rows]
            slope_ref[2 * j + 1, :, z : z + ZONE_TILE] = slope[rows:]
    return summed


def hour_weighted(summed, core, hours, hours_total, j):
    rows = summed.shape[0] // 2
    first = core * hours + 2 * j
    return summed[:rows] * occupancy(first, hours_total) + summed[rows:] * occupancy(
        first + 1, hours_total
    )


def scan_kernel(kind, hours_total, chunks, extra, order, priors, unroll, *refs):
    with_loss, with_slope, with_turn = "loss" in kind, "slope" in kind, "turn" in kind
    f_refs, refs = refs[:chunks], refs[chunks:]
    turn_refs, refs = [*refs[:extra], *f_refs], refs[extra:]
    rhs_ref, area_ref, refs = refs[0], refs[1], refs[2:]
    prior_refs, refs = refs[:priors], refs[priors:]
    if with_loss:
        out_ref, refs = refs[0], refs[1:]
    slope_ref = None
    if with_slope:
        slope_ref, refs = refs[0], refs[1:]
    if with_turn:
        ft_ref, refs = refs[0], refs[1:]
    if with_loss:
        acc_ref = refs[0]
        acc_ref[...] = jnp.zeros_like(acc_ref)
    pairs, _, zones = rhs_ref.shape
    hours = 2 * pairs
    core, me = here()

    def rows_of(parts, at):
        parts = [part[:, at] for part in parts]
        return parts[0] if len(parts) == 1 else jnp.concatenate(parts, axis=0)

    def pair_step(j, carry):
        at = pl.ds(pl.multiple_of(j * LANES, LANES), LANES)
        pair = rows_of(f_refs, at)
        if with_turn:
            ft_ref[at, :] = rows_of(turn_refs, at).T
        summed = pair_work(kind, pair, lambda at: rhs_ref[j, :, at], area_ref, slope_ref, j)
        if with_loss:
            acc_ref[...] += hour_weighted(summed, core, hours, hours_total, j)
        return carry

    lax.fori_loop(0, pairs, pair_step, 0, unroll=unroll)

    if with_loss:
        row = jnp.sum(acc_ref[...].T, axis=0, keepdims=True)
        if not priors:
            out_ref[...] = jnp.broadcast_to(row, out_ref.shape)
        else:
            known = [ref[0:1, :] for ref in prior_refs] + [row]
            chunk = sum(part.shape[1] for part in known) // len(order)
            pieces = [
                part[:, first : first + chunk]
                for part in known
                for first in range(0, part.shape[1], chunk)
            ]
            occ_sum = hours * 1.0 + (
                2.0 * (core * hours * hours + hours * (hours - 1) // 2)
            ).astype(F32) / (hours_total - 1)
            weight = jnp.sum(area_ref[...]) * occ_sum
            message = jnp.zeros(out_ref.shape, F32) + weight
            index = lax.broadcasted_iota(jnp.int32, message.shape, 0)
            blank = jnp.zeros((1, LANES - chunk), F32)
            for m, piece in zip(order, pieces):
                piece = jnp.concatenate([piece, blank], axis=1)
                message = jnp.where(index == (me ^ m), piece, message)
            out_ref[...] = message


def scan(kind, rows_in, rhs, area, hours_total, order, extra=(), priors=(), unroll=6, cost=None):
    hours, zones = 2 * rhs.shape[0], rhs.shape[2]
    rows = sum(f.shape[0] for f in rows_in)
    outs = []
    scratch = []
    if "loss" in kind:
        sublanes = -(-(len(order) + 1) // 8) * 8
        outs.append(((sublanes, LANES) if priors else (8, rows), F32))
        scratch.append(pltpu.VMEM((rows, LANES), F32))
    if "slope" in kind:
        outs.append(((hours, rows, zones), BF16))
    if "turn" in kind:
        outs.append(((rows_in[0].shape[1], rows + sum(f.shape[0] for f in extra)), BF16))
    return call(
        functools.partial(
            scan_kernel, kind, hours_total, len(rows_in), len(extra), order, len(priors), unroll
        ),
        kind,
        outs,
        [*rows_in, *extra, rhs, area, *priors],
        scratch,
        cost,
    )


def gradient_kernel(
    hours_total, gain, owners, order, messages, *refs
):
    msg_refs, refs = refs[:messages], refs[messages:]
    ft_refs, slope_refs, refs = refs[:2], refs[2:6], refs[6:]
    resp_ref, area_ref, plan_ref, out_ref, acc_ref, score_ref, e_ref = refs
    hours, width, zones = resp_ref.shape
    core, me = here()
    sources = len(order)
    chunk = e_ref.shape[1] // sources
    total = [msg_ref[...] for msg_ref in msg_refs]
    while len(total) > 1:
        total = [first + second for first, second in zip(total[::2], total[1::2])]
    total = total[0]
    weight = jnp.max(total[sources : sources + 1, :])
    score = total * (SHARPNESS * math.log(2.0) / weight)
    rows = lax.broadcasted_iota(jnp.int32, score.shape, 0)
    lanes = lax.broadcasted_iota(jnp.int32, score.shape, 1)
    valid = (rows < sources) & (lanes < chunk)
    peak = jnp.max(jnp.where(valid, score, -jnp.inf))
    e = jnp.where(valid, jnp.exp(jnp.where(valid, score - peak, 0.0)), 0.0)
    exp_total = jnp.sum(e)
    score_ref[...] = e
    for spot, m in enumerate(order):
        piece = score_ref[pl.ds(me ^ m, 1), :]
        e_ref[:, spot * chunk : (spot + 1) * chunk] = piece[:, :chunk]
    acc_ref[...] = jnp.zeros_like(acc_ref)

    def hour_step(h, carry):
        occ = occupancy(core * hours + h, hours_total)
        at = pl.ds(pl.multiple_of(h * width, width), width)
        ft = jnp.concatenate([ref[at, :] for ref in ft_refs], axis=1).astype(F32)
        ft = ft * (e_ref[...] * occ)
        high = ft.astype(BF16)
        low = (ft - high.astype(F32)).astype(BF16)
        both = jnp.concatenate([high, low], axis=0)
        for z in range(0, zones, ZONE_TILE):
            at = slice(z, z + ZONE_TILE)
            kept = jnp.concatenate([ref[h, :, at] for ref in slope_refs], axis=0)
            mixed = jnp.dot(both, kept, preferred_element_type=F32)
            mixed = mixed[:width] + mixed[width:]
            acc_ref[:, at] += resp_ref[h, :, at].astype(F32) * mixed
        return carry

    lax.fori_loop(0, hours, hour_step, 0, unroll=hours // 2)

    grad = acc_ref[...] * area_ref[...]
    blocks, pad, _ = out_ref.shape
    index = lax.broadcasted_iota(jnp.int32, (blocks * pad, zones), 0)
    within = index % pad
    design = jnp.where(within < owners, (index // pad) * owners + within, -1)
    onehot = (design == plan_ref[...]).astype(F32).astype(BF16)
    sens = jnp.zeros((blocks * pad, width), F32)
    for _ in range(3):
        part = grad.astype(BF16)
        grad = grad - part.astype(F32)
        sens = sens + lax.dot_general(
            onehot, part, (((1,), (1,)), ((), ())), preferred_element_type=F32
        )
    sens = sens * (0.5 * gain / weight)
    out_ref[:, :, :width] = sens.reshape(blocks, pad, width)
    lane = lax.broadcasted_iota(jnp.int32, (blocks, pad, LANES - width), 2)
    out_ref[:, :, width:] = jnp.where(lane == 0, peak, exp_total)


def finish_kernel(scen_parts, width, parts_ref, sens_ref, objective_ref):
    parts = parts_ref[...]
    devices = parts.shape[0]
    peaks = parts[:, :, width : width + 1]
    totals = parts[:, :, width + 1 : width + 2]
    peak = jnp.max(peaks)
    scale = jnp.exp(peaks - peak)
    total = jnp.sum((scale * totals)[:, 0:1, :]) * (scen_parts / devices)
    summed = jnp.sum(parts[:, :, :width] * scale, axis=0) / total
    sens_ref[...] = summed[: sens_ref.shape[0]]
    log_total = jnp.max(jnp.log(jnp.full((8, LANES), total, F32)))
    objective_ref[0] = (peak + log_total) / SHARPNESS - 0.5


def on_device(forcing, response, window_params, building_map, owner_ids, band_ids, floor_area):
    hours, width, zones = response.shape
    hour_parts = lax.axis_size("hour")
    zone_parts = lax.axis_size("zone")
    scen_parts = lax.axis_size("scen")
    hours_total = hours * hour_parts
    core = lax.axis_index("hour")
    sources = zone_parts * hour_parts

    half = hours * width
    everyone = forcing.reshape(forcing.shape[0], hours_total * width)
    keep = lax.dynamic_slice_in_dim(everyone, core * half, half, axis=1)
    leave = lax.dynamic_slice_in_dim(everyone, (1 - core) * half, half, axis=1)
    came = lax.ppermute(leave, "hour", [(0, 1), (1, 0)])

    def swap(x, step):
        return lax.ppermute(x, "zone", [(i, i ^ step) for i in range(zone_parts)])

    piece = sources // 8
    parts = [range(i, i + piece) for i in range(0, sources, piece)]
    own, near0, near1, far_a, far_b, final = (
        [*parts[0], *parts[1]], parts[2], parts[3], parts[4], parts[5], [*parts[6], *parts[7]]
    )
    worked = (*own, *far_a, *near0, *near1, *far_b, *final)
    kept = (*far_a, *near0, *near1, *far_b, *own, *final)
    if zone_parts == 4:
        mine = jnp.concatenate([keep, came], axis=0)
        far0, far1, beside = swap(keep, 2), swap(came, 2), swap(mine, 1)
    else:
        me = lax.axis_index(("zone", "hour"))
        both = jnp.where(core == 0, jnp.stack([keep, came]), jnp.stack([came, keep]))
        gathered = lax.all_gather(both, "zone", axis=0, tiled=True)
        ordered = jnp.take(gathered, me ^ jnp.arange(sources), axis=0).reshape(4, -1, half)
        mine, beside, far, last = ordered
        far0, far1 = far[: far.shape[0] // 2], far[far.shape[0] // 2 :]
    rhs, plan, area, near_response, loss0, slope0 = opening(
        mine, building_map, owner_ids, window_params, band_ids, floor_area, response, hours_total
    )
    common = (rhs, area, hours_total, worked)
    far0, loss0 = lax.optimization_barrier((far0, loss0))
    loss1, slope1 = scan("loss_slope", [far0], *common, cost=SHORT)
    if zone_parts == 4:
        far0, far1, loss1 = lax.optimization_barrier((far0, far1, loss1))
        last = swap(jnp.concatenate([far0, far1], axis=0), 1)
    loss2, slope2, ft0 = scan("loss_slope_turn", [beside, far1], *common, extra=[far0])
    (message,) = scan("loss", [last], *common, priors=[loss0, loss1, loss2])
    message = message + lax.ppermute(message, "hour", [(0, 1), (1, 0)])
    slope3, ft1 = scan("slope_turn", [last], *common, extra=[mine])
    if zone_parts == 4:
        others = [swap(message, k) for k in (1, 2, 3)]
        *others, slope3 = lax.optimization_barrier((*others, slope3))
        messages = [message, *others]
    else:
        messages = [lax.psum(message, "zone")]

    designs = window_params.shape[0]
    devices = zone_parts * scen_parts * hour_parts
    owners = designs // devices
    pad = -(-owners // 8) * 8
    gain = math.sqrt(width * zones * zone_parts * hours_total * designs)
    (parts,) = call(
        functools.partial(gradient_kernel, hours_total, gain, owners, kept, len(messages)),
        "gradient",
        [((devices, pad, LANES), F32)],
        [*messages, ft0, ft1, slope1, slope2, slope0, slope3, near_response, area, plan],
        [
            pltpu.VMEM((width, zones), F32),
            pltpu.VMEM(message.shape, F32),
            pltpu.VMEM((1, ft0.shape[1] + ft1.shape[1]), F32),
        ],
    )
    parts = lax.all_to_all(
        parts, ("zone", "scen", "hour"), split_axis=0, concat_axis=0, tiled=True
    )
    sensitivity, objective = pl.pallas_call(
        functools.partial(finish_kernel, scen_parts, width),
        in_specs=[VMEM],
        out_specs=[VMEM, SMEM],
        out_shape=[
            jax.ShapeDtypeStruct((owners, width), F32),
            jax.ShapeDtypeStruct((1,), F32),
        ],
        compiler_params=params(),
        name="finish",
    )(near(parts))
    return (sensitivity, objective)


def solution(mesh):
    in_specs = (
        P(("groups", "zone", "scen", "hour"), None, None),
        P("hour", None, ("groups", "zone")),
        P("groups", None),
        P(("groups", "zone")),
        P("groups"),
        P("hour", ("groups", "zone")),
        P(("groups", "zone")),
    )
    out_specs = (P(("groups", "zone", "scen", "hour"), None), P("groups"))
    return jax.shard_map(
        on_device, mesh=mesh, in_specs=in_specs, out_specs=out_specs, check_vma=False
    )
```

```python
import functools
import math

import jax
import jax.numpy as jnp
from jax import lax
from jax.experimental import pallas as pl
from jax.experimental.pallas import tpu as pltpu
from jax.sharding import PartitionSpec as P

SHARPNESS = 200.0
MINUS_LOG2_E = -1.0 / math.log(2.0)
EDGE = 2.0 * math.cosh(0.5)
LANES = 128
DEPTH = 128
ZONE_TILE = 256
SHORT = pl.CostEstimate(flops=1, bytes_accessed=1, transcendentals=0)
VMEM = pl.BlockSpec(memory_space=pltpu.VMEM)
SMEM = pl.BlockSpec(memory_space=pltpu.SMEM)
F32 = jnp.float32
BF16 = jnp.bfloat16


def params():
    return pltpu.CompilerParams(vmem_limit_bytes=20 * 2**20)


def near(x):
    return pltpu.with_memory_space_constraint(x, pltpu.VMEM)


def call(kernel, name, outs, args, scratch=(), cost=None):
    return pl.pallas_call(
        kernel,
        in_specs=[VMEM] * len(args),
        out_specs=[VMEM] * len(outs),
        out_shape=[pltpu.MemorySpace.VMEM(shape, kind) for shape, kind in outs],
        scratch_shapes=list(scratch),
        compiler_params=params(),
        cost_estimate=cost,
        name=name,
    )(*[near(a) for a in args])


def open_kernel(
    hours_total, mine_ref, map_hbm, owner_hbm, wp_hbm, band_hbm, area_hbm, resp_hbm,
    rhs_ref, plan_ref, area_ref, resp_ref, loss_ref, slope_ref,
    map_ref, owner_ref, wp_ref, band_ref, zp_ref, acc_ref, sems, resp_sems,
):
    hours, width, zones = resp_ref.shape
    pieces = resp_sems.shape[0]
    span = hours // pieces
    small = [
        pltpu.make_async_copy(source, target, sems.at[i])
        for i, (source, target) in enumerate(
            (
                (map_hbm, map_ref),
                (owner_hbm, owner_ref),
                (wp_hbm, wp_ref),
                (band_hbm, band_ref),
                (area_hbm, area_ref),
            )
        )
    ]
    for copy in small:
        copy.start()
    large = []
    for i in range(pieces):
        part = pl.ds(i * span, span)
        large.append(
            pltpu.make_async_copy(resp_hbm.at[part], resp_ref.at[part], resp_sems.at[i])
        )
        large[-1].start()
    for copy in small:
        copy.wait()
    place = map_ref[...]
    row, lane = place // LANES, place % LANES

    def look(i, found):
        table = jnp.broadcast_to(owner_ref[pl.ds(i, 1), :], place.shape)
        here = jnp.take_along_axis(table, lane, axis=1, mode="promise_in_bounds")
        return jnp.where(row == i, here, found)

    plan = lax.fori_loop(0, owner_ref.shape[0], look, jnp.zeros_like(place), unroll=8)
    for r in range(plan.shape[0]):
        plan_ref[:, r * LANES : (r + 1) * LANES] = plan[r : r + 1, :]
    designs = wp_ref.shape[0]
    onehot = (
        lax.broadcasted_iota(jnp.int32, (designs, zones), 0) == plan_ref[...]
    ).astype(F32).astype(BF16)
    rest = wp_ref[...]
    exact = []
    for _ in range(3):
        exact.append(rest.astype(BF16))
        rest = rest - exact[-1].astype(F32)
    zp_ref[...] = lax.dot_general(
        jnp.concatenate(exact, axis=0),
        jnp.concatenate([onehot] * 3, axis=0),
        (((0,), (0,)), ((), ())),
        preferred_element_type=F32,
    )
    extra = lax.broadcasted_iota(jnp.int32, (16, zones), 0)
    blank = jnp.zeros((DEPTH - width - 16, zones), BF16)
    core, _ = here()
    acc_ref[...] = jnp.zeros_like(acc_ref)

    def pair_step(j, carry):
        depth = []
        for k in range(2):
            h = 2 * j + k
            coeff = (resp_ref[h].astype(F32) * zp_ref[...]).astype(BF16)
            middle = 0.25 * (band_ref[pl.ds(h, 1), :].astype(F32) - 3.5)
            tail = jnp.where(extra == 0, -middle, jnp.where(extra == 1, 1.0, 0.0))
            depth += [coeff, tail.astype(BF16), blank]
        rhs = jnp.concatenate(depth, axis=0)
        rhs_ref[j] = rhs
        pair = mine_ref[:, pl.ds(pl.multiple_of(j * LANES, LANES), LANES)]
        summed = pair_work("loss_slope", pair, lambda at: rhs[:, at], area_ref, slope_ref, j)
        acc_ref[...] += hour_weighted(summed, core, hours, hours_total, j)
        return carry

    for i in range(pieces):
        large[i].wait()
        lax.fori_loop(i * span // 2, (i + 1) * span // 2, pair_step, 0, unroll=span // 2)
    loss_ref[...] = jnp.broadcast_to(
        jnp.sum(acc_ref[...].T, axis=0, keepdims=True), loss_ref.shape
    )


def opening(
    mine, building_map, owner_ids, window_params, band_ids, floor_area, response, hours_total
):
    hours, width, zones = response.shape
    args = [
        building_map.reshape(-1, LANES),
        owner_ids.reshape(-1, LANES),
        window_params,
        band_ids,
        floor_area.reshape(1, zones),
        response,
    ]
    outs = [
        ((hours // 2, 2 * DEPTH, zones), BF16),
        ((1, zones), jnp.int32),
        ((1, zones), F32),
        (response.shape, BF16),
        ((8, mine.shape[0]), F32),
        ((hours, mine.shape[0], zones), BF16),
    ]
    return pl.pallas_call(
        functools.partial(open_kernel, hours_total),
        in_specs=[VMEM] + [pl.BlockSpec(memory_space=pl.ANY)] * len(args),
        out_specs=[VMEM] * len(outs),
        out_shape=[pltpu.MemorySpace.VMEM(shape, kind) for shape, kind in outs],
        scratch_shapes=[pltpu.VMEM(a.shape, a.dtype) for a in args[:4]]
        + [
            pltpu.VMEM((width, zones), F32),
            pltpu.VMEM((mine.shape[0], LANES), F32),
            pltpu.SemaphoreType.DMA((5,)),
            pltpu.SemaphoreType.DMA((2,)),
        ],
        compiler_params=params(),
        cost_estimate=SHORT,
        name="opening",
    )(near(mine), *[pltpu.with_memory_space_constraint(a, pltpu.HBM) for a in args])


def drivers(pair, second, fill):
    half = pair.shape[1] // 2
    lane = lax.broadcasted_iota(jnp.int32, pair.shape, 1)
    if second:
        pair = pltpu.roll(pair.astype(F32), half, 1).astype(BF16)
    rest = jnp.zeros(pair.shape, F32)
    for spot, value in enumerate(fill):
        rest = jnp.where(lane == half + spot, value, rest)
    return jnp.where(lane < half, pair, rest.astype(BF16))


def here():
    core = lax.axis_index("hour")
    return core, lax.axis_index("zone") * lax.axis_size("hour") + core


def occupancy(hour, hours_total):
    return 1.0 + 2.0 * hour.astype(F32) / (hours_total - 1)


def pair_work(kind, pair, rhs_at, area_ref, slope_ref, j):
    with_loss, with_slope = "loss" in kind, "slope" in kind
    zones = area_ref.shape[1]
    rows = pair.shape[0]
    fill = (0.5,) if with_loss else (0.5, 0.25)
    pair = (pair.astype(F32) * 0.5).astype(BF16)
    none = jnp.zeros(pair.shape, BF16)
    lhs = jnp.concatenate(
        [
            jnp.concatenate([drivers(pair, False, fill), none], axis=1),
            jnp.concatenate([none, drivers(pair, True, fill)], axis=1),
        ],
        axis=0,
    )
    summed = None
    for z in range(0, zones, ZONE_TILE):
        v = jnp.dot(lhs, rhs_at(slice(z, z + ZONE_TILE)), preferred_element_type=F32)
        if with_loss:
            a = jnp.abs(v) * (2.0 * MINUS_LOG2_E)
            q = jnp.exp2(a)
            pen = jnp.log2((q + EDGE) * q + 1.0) - a
            pen = pen * area_ref[:, z : z + ZONE_TILE]
            for c in range(0, ZONE_TILE, LANES):
                piece = pen[:, c : c + LANES]
                summed = piece if summed is None else summed + piece
        if with_slope:
            if with_loss:
                slope = jnp.tanh(v + 0.25) + jnp.tanh(v - 0.25)
            else:
                slope = jnp.tanh(v) + jnp.tanh(v - 0.5)
            slope = slope.astype(BF16)
            slope_ref[2 * j, :, z : z + ZONE_TILE] = slope[:rows]
            slope_ref[2 * j + 1, :, z : z + ZONE_TILE] = slope[rows:]
    return summed


def hour_weighted(summed, core, hours, hours_total, j):
    rows = summed.shape[0] // 2
    first = core * hours + 2 * j
    return summed[:rows] * occupancy(first, hours_total) + summed[rows:] * occupancy(
        first + 1, hours_total
    )


def scan_kernel(kind, hours_total, chunks, extra, order, priors, unroll, *refs):
    with_loss, with_slope, with_turn = "loss" in kind, "slope" in kind, "turn" in kind
    f_refs, refs = refs[:chunks], refs[chunks:]
    turn_refs, refs = [*refs[:extra], *f_refs], refs[extra:]
    rhs_ref, area_ref, refs = refs[0], refs[1], refs[2:]
    prior_refs, refs = refs[:priors], refs[priors:]
    if with_loss:
        out_ref, refs = refs[0], refs[1:]
    slope_ref = None
    if with_slope:
        slope_ref, refs = refs[0], refs[1:]
    if with_turn:
        ft_ref, refs = refs[0], refs[1:]
    if with_loss:
        acc_ref = refs[0]
        acc_ref[...] = jnp.zeros_like(acc_ref)
    pairs, _, zones = rhs_ref.shape
    hours = 2 * pairs
    core, me = here()

    def rows_of(parts, at):
        parts = [part[:, at] for part in parts]
        return parts[0] if len(parts) == 1 else jnp.concatenate(parts, axis=0)

    def pair_step(j, carry):
        at = pl.ds(pl.multiple_of(j * LANES, LANES), LANES)
        pair = rows_of(f_refs, at)
        if with_turn:
            ft_ref[at, :] = rows_of(turn_refs, at).T
        summed = pair_work(kind, pair, lambda at: rhs_ref[j, :, at], area_ref, slope_ref, j)
        if with_loss:
            acc_ref[...] += hour_weighted(summed, core, hours, hours_total, j)
        return carry

    lax.fori_loop(0, pairs, pair_step, 0, unroll=unroll)

    if with_loss:
        row = jnp.sum(acc_ref[...].T, axis=0, keepdims=True)
        if not priors:
            out_ref[...] = jnp.broadcast_to(row, out_ref.shape)
        else:
            known = [ref[0:1, :] for ref in prior_refs] + [row]
            chunk = sum(part.shape[1] for part in known) // len(order)
            pieces = [
                part[:, first : first + chunk]
                for part in known
                for first in range(0, part.shape[1], chunk)
            ]
            occ_sum = hours * 1.0 + (
                2.0 * (core * hours * hours + hours * (hours - 1) // 2)
            ).astype(F32) / (hours_total - 1)
            weight = jnp.sum(area_ref[...]) * occ_sum
            message = jnp.zeros(out_ref.shape, F32) + weight
            index = lax.broadcasted_iota(jnp.int32, message.shape, 0)
            blank = jnp.zeros((1, LANES - chunk), F32)
            for m, piece in zip(order, pieces):
                piece = jnp.concatenate([piece, blank], axis=1)
                message = jnp.where(index == (me ^ m), piece, message)
            out_ref[...] = message


def scan(kind, rows_in, rhs, area, hours_total, order, extra=(), priors=(), unroll=6, cost=None):
    hours, zones = 2 * rhs.shape[0], rhs.shape[2]
    rows = sum(f.shape[0] for f in rows_in)
    outs = []
    scratch = []
    if "loss" in kind:
        sublanes = -(-(len(order) + 1) // 8) * 8
        outs.append(((sublanes, LANES) if priors else (8, rows), F32))
        scratch.append(pltpu.VMEM((rows, LANES), F32))
    if "slope" in kind:
        outs.append(((hours, rows, zones), BF16))
    if "turn" in kind:
        outs.append(((rows_in[0].shape[1], rows + sum(f.shape[0] for f in extra)), BF16))
    return call(
        functools.partial(
            scan_kernel, kind, hours_total, len(rows_in), len(extra), order, len(priors), unroll
        ),
        kind,
        outs,
        [*rows_in, *extra, rhs, area, *priors],
        scratch,
        cost,
    )


def gradient_kernel(
    hours_total, gain, owners, order, messages, *refs
):
    msg_refs, refs = refs[:messages], refs[messages:]
    ft_refs, slope_refs, refs = refs[:2], refs[2:6], refs[6:]
    resp_ref, area_ref, plan_ref, out_ref, acc_ref, score_ref, e_ref = refs
    hours, width, zones = resp_ref.shape
    core, me = here()
    sources = len(order)
    chunk = e_ref.shape[1] // sources
    total = [msg_ref[...] for msg_ref in msg_refs]
    while len(total) > 1:
        total = [first + second for first, second in zip(total[::2], total[1::2])]
    total = total[0]
    weight = jnp.max(total[sources : sources + 1, :])
    score = total * (SHARPNESS * math.log(2.0) / weight)
    rows = lax.broadcasted_iota(jnp.int32, score.shape, 0)
    lanes = lax.broadcasted_iota(jnp.int32, score.shape, 1)
    valid = (rows < sources) & (lanes < chunk)
    peak = jnp.max(jnp.where(valid, score, -jnp.inf))
    e = jnp.where(valid, jnp.exp(jnp.where(valid, score - peak, 0.0)), 0.0)
    exp_total = jnp.sum(e)
    score_ref[...] = e
    for spot, m in enumerate(order):
        piece = score_ref[pl.ds(me ^ m, 1), :]
        e_ref[:, spot * chunk : (spot + 1) * chunk] = piece[:, :chunk]
    acc_ref[...] = jnp.zeros_like(acc_ref)

    def hour_step(h, carry):
        occ = occupancy(core * hours + h, hours_total)
        at = pl.ds(pl.multiple_of(h * width, width), width)
        ft = jnp.concatenate([ref[at, :] for ref in ft_refs], axis=1).astype(F32)
        ft = ft * (e_ref[...] * occ)
        high = ft.astype(BF16)
        low = (ft - high.astype(F32)).astype(BF16)
        both = jnp.concatenate([high, low], axis=0)
        for z in range(0, zones, ZONE_TILE):
            at = slice(z, z + ZONE_TILE)
            kept = jnp.concatenate([ref[h, :, at] for ref in slope_refs], axis=0)
            mixed = jnp.dot(both, kept, preferred_element_type=F32)
            mixed = mixed[:width] + mixed[width:]
            acc_ref[:, at] += resp_ref[h, :, at].astype(F32) * mixed
        return carry

    lax.fori_loop(0, hours, hour_step, 0, unroll=hours // 2)

    grad = acc_ref[...] * area_ref[...]
    blocks, pad, _ = out_ref.shape
    index = lax.broadcasted_iota(jnp.int32, (blocks * pad, zones), 0)
    within = index % pad
    design = jnp.where(within < owners, (index // pad) * owners + within, -1)
    onehot = (design == plan_ref[...]).astype(F32).astype(BF16)
    sens = jnp.zeros((blocks * pad, width), F32)
    for _ in range(3):
        part = grad.astype(BF16)
        grad = grad - part.astype(F32)
        sens = sens + lax.dot_general(
            onehot, part, (((1,), (1,)), ((), ())), preferred_element_type=F32
        )
    sens = sens * (0.5 * gain / weight)
    out_ref[:, :, :width] = sens.reshape(blocks, pad, width)
    lane = lax.broadcasted_iota(jnp.int32, (blocks, pad, LANES - width), 2)
    out_ref[:, :, width:] = jnp.where(lane == 0, peak, exp_total)


def finish_kernel(scen_parts, width, parts_ref, sens_ref, objective_ref):
    parts = parts_ref[...]
    devices = parts.shape[0]
    peaks = parts[:, :, width : width + 1]
    totals = parts[:, :, width + 1 : width + 2]
    peak = jnp.max(peaks)
    scale = jnp.exp(peaks - peak)
    total = jnp.sum((scale * totals)[:, 0:1, :]) * (scen_parts / devices)
    summed = jnp.sum(parts[:, :, :width] * scale, axis=0) / total
    sens_ref[...] = summed[: sens_ref.shape[0]]
    log_total = jnp.max(jnp.log(jnp.full((8, LANES), total, F32)))
    objective_ref[0] = (peak + log_total) / SHARPNESS - 0.5


def on_device(forcing, response, window_params, building_map, owner_ids, band_ids, floor_area):
    hours, width, zones = response.shape
    hour_parts = lax.axis_size("hour")
    zone_parts = lax.axis_size("zone")
    scen_parts = lax.axis_size("scen")
    hours_total = hours * hour_parts
    core = lax.axis_index("hour")
    sources = zone_parts * hour_parts

    half = hours * width
    everyone = forcing.reshape(forcing.shape[0], hours_total * width)
    keep = lax.dynamic_slice_in_dim(everyone, core * half, half, axis=1)
    leave = lax.dynamic_slice_in_dim(everyone, (1 - core) * half, half, axis=1)
    came = lax.ppermute(leave, "hour", [(0, 1), (1, 0)])

    def swap(x, step):
        return lax.ppermute(x, "zone", [(i, i ^ step) for i in range(zone_parts)])

    piece = sources // 8
    parts = [range(i, i + piece) for i in range(0, sources, piece)]
    own, near0, near1, far_a, far_b, final = (
        [*parts[0], *parts[1]], parts[2], parts[3], parts[4], parts[5], [*parts[6], *parts[7]]
    )
    worked = (*own, *far_a, *near0, *near1, *far_b, *final)
    kept = (*far_a, *near0, *near1, *far_b, *own, *final)
    if zone_parts == 4:
        mine = jnp.concatenate([keep, came], axis=0)
        far0, far1, beside = swap(keep, 2), swap(came, 2), swap(mine, 1)
    else:
        me = lax.axis_index(("zone", "hour"))
        both = jnp.where(core == 0, jnp.stack([keep, came]), jnp.stack([came, keep]))
        gathered = lax.all_gather(both, "zone", axis=0, tiled=True)
        ordered = jnp.take(gathered, me ^ jnp.arange(sources), axis=0).reshape(4, -1, half)
        mine, beside, far, last = ordered
        far0, far1 = far[: far.shape[0] // 2], far[far.shape[0] // 2 :]
    rhs, plan, area, near_response, loss0, slope0 = opening(
        mine, building_map, owner_ids, window_params, band_ids, floor_area, response, hours_total
    )
    common = (rhs, area, hours_total, worked)
    far0, loss0 = lax.optimization_barrier((far0, loss0))
    loss1, slope1 = scan("loss_slope", [far0], *common, cost=SHORT)
    if zone_parts == 4:
        far0, far1, loss1 = lax.optimization_barrier((far0, far1, loss1))
        last = swap(jnp.concatenate([far0, far1], axis=0), 1)
    loss2, slope2, ft0 = scan("loss_slope_turn", [beside, far1], *common, extra=[far0])
    (message,) = scan("loss", [last], *common, priors=[loss0, loss1, loss2])
    message = message + lax.ppermute(message, "hour", [(0, 1), (1, 0)])
    slope3, ft1 = scan("slope_turn", [last], *common, extra=[mine])
    if zone_parts == 4:
        others = [swap(message, k) for k in (3, 2, 1)]
        *others, slope3 = lax.optimization_barrier((*others, slope3))
        others = others[::-1]
        messages = [message, *others]
    else:
        messages = [lax.psum(message, "zone")]

    designs = window_params.shape[0]
    devices = zone_parts * scen_parts * hour_parts
    owners = designs // devices
    pad = -(-owners // 8) * 8
    gain = math.sqrt(width * zones * zone_parts * hours_total * designs)
    (parts,) = call(
        functools.partial(gradient_kernel, hours_total, gain, owners, kept, len(messages)),
        "gradient",
        [((devices, pad, LANES), F32)],
        [*messages, ft0, ft1, slope1, slope2, slope0, slope3, near_response, area, plan],
        [
            pltpu.VMEM((width, zones), F32),
            pltpu.VMEM(message.shape, F32),
            pltpu.VMEM((1, ft0.shape[1] + ft1.shape[1]), F32),
        ],
    )
    parts = lax.all_to_all(
        parts, ("zone", "scen", "hour"), split_axis=0, concat_axis=0, tiled=True
    )
    sensitivity, objective = pl.pallas_call(
        functools.partial(finish_kernel, scen_parts, width),
        in_specs=[VMEM],
        out_specs=[VMEM, SMEM],
        out_shape=[
            jax.ShapeDtypeStruct((owners, width), F32),
            jax.ShapeDtypeStruct((1,), F32),
        ],
        compiler_params=params(),
        name="finish",
    )(near(parts))
    return (sensitivity, objective)


def solution(mesh):
    in_specs = (
        P(("groups", "zone", "scen", "hour"), None, None),
        P("hour", None, ("groups", "zone")),
        P("groups", None),
        P(("groups", "zone")),
        P("groups"),
        P("hour", ("groups", "zone")),
        P(("groups", "zone")),
    )
    out_specs = (P(("groups", "zone", "scen", "hour"), None), P("groups"))
    return jax.shard_map(
        on_device, mesh=mesh, in_specs=in_specs, out_specs=out_specs, check_vma=False
    )
```

```python
import functools
import math

import jax
import jax.numpy as jnp
from jax import lax
from jax.experimental import pallas as pl
from jax.experimental.pallas import tpu as pltpu
from jax.sharding import PartitionSpec as P

SHARPNESS = 200.0
MINUS_LOG2_E = -1.0 / math.log(2.0)
EDGE = 2.0 * math.cosh(0.5)
LANES = 128
DEPTH = 128
ZONE_TILE = 256
SHORT = pl.CostEstimate(flops=1, bytes_accessed=1, transcendentals=0)
VMEM = pl.BlockSpec(memory_space=pltpu.VMEM)
SMEM = pl.BlockSpec(memory_space=pltpu.SMEM)
F32 = jnp.float32
BF16 = jnp.bfloat16


def params():
    return pltpu.CompilerParams(vmem_limit_bytes=20 * 2**20)


def near(x):
    return pltpu.with_memory_space_constraint(x, pltpu.VMEM)


def call(kernel, name, outs, args, scratch=(), cost=None):
    return pl.pallas_call(
        kernel,
        in_specs=[VMEM] * len(args),
        out_specs=[VMEM] * len(outs),
        out_shape=[pltpu.MemorySpace.VMEM(shape, kind) for shape, kind in outs],
        scratch_shapes=list(scratch),
        compiler_params=params(),
        cost_estimate=cost,
        name=name,
    )(*[near(a) for a in args])


def open_kernel(
    hours_total, mine_ref, map_hbm, owner_hbm, wp_hbm, band_hbm, area_hbm, resp_hbm,
    rhs_ref, plan_ref, area_ref, resp_ref, loss_ref, slope_ref,
    map_ref, owner_ref, wp_ref, band_ref, zp_ref, acc_ref, sems, resp_sems,
):
    hours, width, zones = resp_ref.shape
    pieces = resp_sems.shape[0]
    span = hours // pieces
    small = [
        pltpu.make_async_copy(source, target, sems.at[i])
        for i, (source, target) in enumerate(
            (
                (map_hbm, map_ref),
                (owner_hbm, owner_ref),
                (wp_hbm, wp_ref),
                (band_hbm, band_ref),
                (area_hbm, area_ref),
            )
        )
    ]
    for copy in small:
        copy.start()
    large = []
    for i in range(pieces):
        part = pl.ds(i * span, span)
        large.append(
            pltpu.make_async_copy(resp_hbm.at[part], resp_ref.at[part], resp_sems.at[i])
        )
        large[-1].start()
    for copy in small:
        copy.wait()
    place = map_ref[...]
    row, lane = place // LANES, place % LANES

    def look(i, found):
        table = jnp.broadcast_to(owner_ref[pl.ds(i, 1), :], place.shape)
        here = jnp.take_along_axis(table, lane, axis=1, mode="promise_in_bounds")
        return jnp.where(row == i, here, found)

    plan = lax.fori_loop(0, owner_ref.shape[0], look, jnp.zeros_like(place), unroll=8)
    for r in range(plan.shape[0]):
        plan_ref[:, r * LANES : (r + 1) * LANES] = plan[r : r + 1, :]
    designs = wp_ref.shape[0]
    onehot = (
        lax.broadcasted_iota(jnp.int32, (designs, zones), 0) == plan_ref[...]
    ).astype(F32).astype(BF16)
    rest = wp_ref[...]
    exact = []
    for _ in range(3):
        exact.append(rest.astype(BF16))
        rest = rest - exact[-1].astype(F32)
    zp_ref[...] = lax.dot_general(
        jnp.concatenate(exact, axis=0),
        jnp.concatenate([onehot] * 3, axis=0),
        (((0,), (0,)), ((), ())),
        preferred_element_type=F32,
    )
    extra = lax.broadcasted_iota(jnp.int32, (16, zones), 0)
    blank = jnp.zeros((DEPTH - width - 16, zones), BF16)
    core, _ = here()
    acc_ref[...] = jnp.zeros_like(acc_ref)

    def pair_step(j, carry):
        depth = []
        for k in range(2):
            h = 2 * j + k
            coeff = (resp_ref[h].astype(F32) * zp_ref[...]).astype(BF16)
            middle = 0.25 * (band_ref[pl.ds(h, 1), :].astype(F32) - 3.5)
            tail = jnp.where(extra == 0, -middle, jnp.where(extra == 1, 1.0, 0.0))
            depth += [coeff, tail.astype(BF16), blank]
        rhs = jnp.concatenate(depth, axis=0)
        rhs_ref[j] = rhs
        pair = mine_ref[:, pl.ds(pl.multiple_of(j * LANES, LANES), LANES)]
        summed = pair_work("loss_slope", pair, lambda at: rhs[:, at], area_ref, slope_ref, j)
        acc_ref[...] += hour_weighted(summed, core, hours, hours_total, j)
        return carry

    for i in range(pieces):
        large[i].wait()
        lax.fori_loop(i * span // 2, (i + 1) * span // 2, pair_step, 0, unroll=span // 2)
    loss_ref[...] = jnp.broadcast_to(
        jnp.sum(acc_ref[...].T, axis=0, keepdims=True), loss_ref.shape
    )


def opening(
    mine, building_map, owner_ids, window_params, band_ids, floor_area, response, hours_total
):
    hours, width, zones = response.shape
    args = [
        building_map.reshape(-1, LANES),
        owner_ids.reshape(-1, LANES),
        window_params,
        band_ids,
        floor_area.reshape(1, zones),
        response,
    ]
    outs = [
        ((hours // 2, 2 * DEPTH, zones), BF16),
        ((1, zones), jnp.int32),
        ((1, zones), F32),
        (response.shape, BF16),
        ((8, mine.shape[0]), F32),
        ((hours, mine.shape[0], zones), BF16),
    ]
    return pl.pallas_call(
        functools.partial(open_kernel, hours_total),
        in_specs=[VMEM] + [pl.BlockSpec(memory_space=pl.ANY)] * len(args),
        out_specs=[VMEM] * len(outs),
        out_shape=[pltpu.MemorySpace.VMEM(shape, kind) for shape, kind in outs],
        scratch_shapes=[pltpu.VMEM(a.shape, a.dtype) for a in args[:4]]
        + [
            pltpu.VMEM((width, zones), F32),
            pltpu.VMEM((mine.shape[0], LANES), F32),
            pltpu.SemaphoreType.DMA((5,)),
            pltpu.SemaphoreType.DMA((2,)),
        ],
        compiler_params=params(),
        cost_estimate=SHORT,
        name="opening",
    )(near(mine), *[pltpu.with_memory_space_constraint(a, pltpu.HBM) for a in args])


def drivers(pair, second, fill):
    half = pair.shape[1] // 2
    lane = lax.broadcasted_iota(jnp.int32, pair.shape, 1)
    if second:
        pair = pltpu.roll(pair.astype(F32), half, 1).astype(BF16)
    rest = jnp.zeros(pair.shape, F32)
    for spot, value in enumerate(fill):
        rest = jnp.where(lane == half + spot, value, rest)
    return jnp.where(lane < half, pair, rest.astype(BF16))


def here():
    core = lax.axis_index("hour")
    return core, lax.axis_index("zone") * lax.axis_size("hour") + core


def occupancy(hour, hours_total):
    return 1.0 + 2.0 * hour.astype(F32) / (hours_total - 1)


def pair_work(kind, pair, rhs_at, area_ref, slope_ref, j):
    with_loss, with_slope = "loss" in kind, "slope" in kind
    zones = area_ref.shape[1]
    rows = pair.shape[0]
    fill = (0.5,) if with_loss else (0.5, 0.25)
    pair = (pair.astype(F32) * 0.5).astype(BF16)
    none = jnp.zeros(pair.shape, BF16)
    lhs = jnp.concatenate(
        [
            jnp.concatenate([drivers(pair, False, fill), none], axis=1),
            jnp.concatenate([none, drivers(pair, True, fill)], axis=1),
        ],
        axis=0,
    )
    summed = None
    for z in range(0, zones, ZONE_TILE):
        v = jnp.dot(lhs, rhs_at(slice(z, z + ZONE_TILE)), preferred_element_type=F32)
        if with_loss:
            a = jnp.abs(v) * (2.0 * MINUS_LOG2_E)
            q = jnp.exp2(a)
            pen = jnp.log2((q + EDGE) * q + 1.0) - a
            pen = pen * area_ref[:, z : z + ZONE_TILE]
            for c in range(0, ZONE_TILE, LANES):
                piece = pen[:, c : c + LANES]
                summed = piece if summed is None else summed + piece
        if with_slope:
            if with_loss:
                slope = jnp.tanh(v + 0.25) + jnp.tanh(v - 0.25)
            else:
                slope = jnp.tanh(v) + jnp.tanh(v - 0.5)
            slope = slope.astype(BF16)
            slope_ref[2 * j, :, z : z + ZONE_TILE] = slope[:rows]
            slope_ref[2 * j + 1, :, z : z + ZONE_TILE] = slope[rows:]
    return summed


def hour_weighted(summed, core, hours, hours_total, j):
    rows = summed.shape[0] // 2
    first = core * hours + 2 * j
    return summed[:rows] * occupancy(first, hours_total) + summed[rows:] * occupancy(
        first + 1, hours_total
    )


def scan_kernel(kind, hours_total, chunks, extra, order, priors, unroll, *refs):
    with_loss, with_slope, with_turn = "loss" in kind, "slope" in kind, "turn" in kind
    f_refs, refs = refs[:chunks], refs[chunks:]
    turn_refs, refs = [*refs[:extra], *f_refs], refs[extra:]
    rhs_ref, area_ref, refs = refs[0], refs[1], refs[2:]
    prior_refs, refs = refs[:priors], refs[priors:]
    if with_loss:
        out_ref, refs = refs[0], refs[1:]
    slope_ref = None
    if with_slope:
        slope_ref, refs = refs[0], refs[1:]
    if with_turn:
        ft_ref, refs = refs[0], refs[1:]
    if with_loss:
        acc_ref = refs[0]
        acc_ref[...] = jnp.zeros_like(acc_ref)
    pairs, _, zones = rhs_ref.shape
    hours = 2 * pairs
    core, me = here()

    def rows_of(parts, at):
        parts = [part[:, at] for part in parts]
        return parts[0] if len(parts) == 1 else jnp.concatenate(parts, axis=0)

    def pair_step(j, carry):
        at = pl.ds(pl.multiple_of(j * LANES, LANES), LANES)
        pair = rows_of(f_refs, at)
        if with_turn:
            ft_ref[at, :] = rows_of(turn_refs, at).T
        summed = pair_work(kind, pair, lambda at: rhs_ref[j, :, at], area_ref, slope_ref, j)
        if with_loss:
            acc_ref[...] += hour_weighted(summed, core, hours, hours_total, j)
        return carry

    lax.fori_loop(0, pairs, pair_step, 0, unroll=unroll)

    if with_loss:
        row = jnp.sum(acc_ref[...].T, axis=0, keepdims=True)
        if not priors:
            out_ref[...] = jnp.broadcast_to(row, out_ref.shape)
        else:
            known = [ref[0:1, :] for ref in prior_refs] + [row]
            chunk = sum(part.shape[1] for part in known) // len(order)
            pieces = [
                part[:, first : first + chunk]
                for part in known
                for first in range(0, part.shape[1], chunk)
            ]
            occ_sum = hours * 1.0 + (
                2.0 * (core * hours * hours + hours * (hours - 1) // 2)
            ).astype(F32) / (hours_total - 1)
            weight = jnp.sum(area_ref[...]) * occ_sum
            message = jnp.zeros(out_ref.shape, F32) + weight
            index = lax.broadcasted_iota(jnp.int32, message.shape, 0)
            blank = jnp.zeros((1, LANES - chunk), F32)
            for m, piece in zip(order, pieces):
                piece = jnp.concatenate([piece, blank], axis=1)
                message = jnp.where(index == (me ^ m), piece, message)
            out_ref[...] = message


def scan(kind, rows_in, rhs, area, hours_total, order, extra=(), priors=(), unroll=12, cost=None):
    hours, zones = 2 * rhs.shape[0], rhs.shape[2]
    rows = sum(f.shape[0] for f in rows_in)
    outs = []
    scratch = []
    if "loss" in kind:
        sublanes = -(-(len(order) + 1) // 8) * 8
        outs.append(((sublanes, LANES) if priors else (8, rows), F32))
        scratch.append(pltpu.VMEM((rows, LANES), F32))
    if "slope" in kind:
        outs.append(((hours, rows, zones), BF16))
    if "turn" in kind:
        outs.append(((rows_in[0].shape[1], rows + sum(f.shape[0] for f in extra)), BF16))
    return call(
        functools.partial(
            scan_kernel, kind, hours_total, len(rows_in), len(extra), order, len(priors), unroll
        ),
        kind,
        outs,
        [*rows_in, *extra, rhs, area, *priors],
        scratch,
        cost,
    )


def gradient_kernel(
    hours_total, gain, order, messages, *refs
):
    msg_refs, refs = refs[:messages], refs[messages:]
    ft_refs, slope_refs, refs = refs[:2], refs[2:6], refs[6:]
    resp_ref, area_ref, plan_ref, out_ref, acc_ref, score_ref, e_ref = refs
    hours, width, zones = resp_ref.shape
    core, me = here()
    sources = len(order)
    chunk = e_ref.shape[1] // sources
    total = [msg_ref[...] for msg_ref in msg_refs]
    while len(total) > 1:
        total = [first + second for first, second in zip(total[::2], total[1::2])]
    total = total[0]
    weight = jnp.max(total[sources : sources + 1, :])
    score = total * (SHARPNESS * math.log(2.0) / weight)
    rows = lax.broadcasted_iota(jnp.int32, score.shape, 0)
    lanes = lax.broadcasted_iota(jnp.int32, score.shape, 1)
    valid = (rows < sources) & (lanes < chunk)
    peak = jnp.max(jnp.where(valid, score, -jnp.inf))
    e = jnp.where(valid, jnp.exp(jnp.where(valid, score - peak, 0.0)), 0.0)
    exp_total = jnp.sum(e)
    score_ref[...] = e
    for spot, m in enumerate(order):
        piece = score_ref[pl.ds(me ^ m, 1), :]
        e_ref[:, spot * chunk : (spot + 1) * chunk] = piece[:, :chunk]
    acc_ref[...] = jnp.zeros_like(acc_ref)

    def hour_step(h, carry):
        occ = occupancy(core * hours + h, hours_total)
        at = pl.ds(pl.multiple_of(h * width, width), width)
        ft = jnp.concatenate([ref[at, :] for ref in ft_refs], axis=1).astype(F32)
        ft = ft * (e_ref[...] * occ)
        high = ft.astype(BF16)
        low = (ft - high.astype(F32)).astype(BF16)
        both = jnp.concatenate([high, low], axis=0)
        for z in range(0, zones, ZONE_TILE):
            at = slice(z, z + ZONE_TILE)
            kept = jnp.concatenate([ref[h, :, at] for ref in slope_refs], axis=0)
            mixed = jnp.dot(both, kept, preferred_element_type=F32)
            mixed = mixed[:width] + mixed[width:]
            acc_ref[:, at] += resp_ref[h, :, at].astype(F32) * mixed
        return carry

    lax.fori_loop(0, hours, hour_step, 0, unroll=hours // 2)

    grad = acc_ref[...] * area_ref[...]
    blocks, owners, _ = out_ref.shape
    index = lax.broadcasted_iota(jnp.int32, (blocks * owners, zones), 0)
    onehot = (index == plan_ref[...]).astype(F32).astype(BF16)
    sens = jnp.zeros((blocks * owners, width), F32)
    for _ in range(3):
        part = grad.astype(BF16)
        grad = grad - part.astype(F32)
        sens = sens + lax.dot_general(
            onehot, part, (((1,), (1,)), ((), ())), preferred_element_type=F32
        )
    sens = sens * (0.5 * gain / weight)
    for k in range(blocks):
        out_ref[k, :, :width] = sens[k * owners : (k + 1) * owners]
    lane = lax.broadcasted_iota(jnp.int32, (blocks, owners, LANES - width), 2)
    out_ref[:, :, width:] = jnp.where(lane == 0, peak, exp_total)


def finish_kernel(scen_parts, width, parts_ref, sens_ref, objective_ref):
    parts = parts_ref[...]
    devices = parts.shape[0]
    peaks = parts[:, :, width : width + 1]
    totals = parts[:, :, width + 1 : width + 2]
    peak = jnp.max(peaks)
    scale = jnp.exp(peaks - peak)
    total = jnp.sum((scale * totals)[:, 0:1, :]) * (scen_parts / devices)
    summed = jnp.sum(parts[:, :, :width] * scale, axis=0) / total
    sens_ref[...] = summed
    log_total = jnp.max(jnp.log(jnp.full((8, LANES), total, F32)))
    objective_ref[0] = (peak + log_total) / SHARPNESS - 0.5


def on_device(forcing, response, window_params, building_map, owner_ids, band_ids, floor_area):
    hours, width, zones = response.shape
    hour_parts = lax.axis_size("hour")
    zone_parts = lax.axis_size("zone")
    scen_parts = lax.axis_size("scen")
    hours_total = hours * hour_parts
    core = lax.axis_index("hour")
    sources = zone_parts * hour_parts

    half = hours * width
    everyone = forcing.reshape(forcing.shape[0], hours_total * width)
    keep = lax.dynamic_slice_in_dim(everyone, core * half, half, axis=1)
    leave = lax.dynamic_slice_in_dim(everyone, (1 - core) * half, half, axis=1)
    came = lax.ppermute(leave, "hour", [(0, 1), (1, 0)])

    def swap(x, step):
        return lax.ppermute(x, "zone", [(i, i ^ step) for i in range(zone_parts)])

    piece = sources // 8
    parts = [range(i, i + piece) for i in range(0, sources, piece)]
    own, near0, near1, far_a, far_b, final = (
        [*parts[0], *parts[1]], parts[2], parts[3], parts[4], parts[5], [*parts[6], *parts[7]]
    )
    worked = (*own, *far_a, *near0, *near1, *far_b, *final)
    kept = (*far_a, *near0, *near1, *far_b, *own, *final)
    if zone_parts == 4:
        mine = jnp.concatenate([keep, came], axis=0)
        far0, far1, beside = swap(keep, 2), swap(came, 2), swap(mine, 1)
    else:
        me = lax.axis_index(("zone", "hour"))
        both = jnp.where(core == 0, jnp.stack([keep, came]), jnp.stack([came, keep]))
        gathered = lax.all_gather(both, "zone", axis=0, tiled=True)
        ordered = jnp.take(gathered, me ^ jnp.arange(sources), axis=0).reshape(4, -1, half)
        mine, beside, far, last = ordered
        far0, far1 = far[: far.shape[0] // 2], far[far.shape[0] // 2 :]
    rhs, plan, area, near_response, loss0, slope0 = opening(
        mine, building_map, owner_ids, window_params, band_ids, floor_area, response, hours_total
    )
    common = (rhs, area, hours_total, worked)
    far0, loss0 = lax.optimization_barrier((far0, loss0))
    loss1, slope1 = scan("loss_slope", [far0], *common, cost=SHORT)
    if zone_parts == 4:
        far0, far1, loss1 = lax.optimization_barrier((far0, far1, loss1))
        last = swap(jnp.concatenate([far0, far1], axis=0), 1)
    loss2, slope2, ft0 = scan("loss_slope_turn", [beside, far1], *common, extra=[far0])
    (message,) = scan("loss", [last], *common, priors=[loss0, loss1, loss2])
    message = message + lax.ppermute(message, "hour", [(0, 1), (1, 0)])
    slope3, ft1 = scan("slope_turn", [last], *common, extra=[mine])
    if zone_parts == 4:
        others = [swap(message, k) for k in (3, 2, 1)]
        *others, slope3 = lax.optimization_barrier((*others, slope3))
        others = others[::-1]
        messages = [message, *others]
    else:
        messages = [lax.psum(message, "zone")]

    designs = window_params.shape[0]
    devices = zone_parts * scen_parts * hour_parts
    owners = designs // devices
    gain = math.sqrt(width * zones * zone_parts * hours_total * designs)
    (parts,) = call(
        functools.partial(gradient_kernel, hours_total, gain, kept, len(messages)),
        "gradient",
        [((devices, owners, LANES), F32)],
        [*messages, ft0, ft1, slope1, slope2, slope0, slope3, near_response, area, plan],
        [
            pltpu.VMEM((width, zones), F32),
            pltpu.VMEM(message.shape, F32),
            pltpu.VMEM((1, ft0.shape[1] + ft1.shape[1]), F32),
        ],
    )
    parts = lax.all_to_all(
        parts, ("zone", "scen", "hour"), split_axis=0, concat_axis=0, tiled=True
    )
    sensitivity, objective = pl.pallas_call(
        functools.partial(finish_kernel, scen_parts, width),
        in_specs=[VMEM],
        out_specs=[VMEM, SMEM],
        out_shape=[
            jax.ShapeDtypeStruct((owners, width), F32),
            jax.ShapeDtypeStruct((1,), F32),
        ],
        compiler_params=params(),
        name="finish",
    )(near(parts))
    return (sensitivity, objective)


def solution(mesh):
    in_specs = (
        P(("groups", "zone", "scen", "hour"), None, None),
        P("hour", None, ("groups", "zone")),
        P("groups", None),
        P(("groups", "zone")),
        P("groups"),
        P("hour", ("groups", "zone")),
        P(("groups", "zone")),
    )
    out_specs = (P(("groups", "zone", "scen", "hour"), None), P("groups"))
    return jax.shard_map(
        on_device, mesh=mesh, in_specs=in_specs, out_specs=out_specs, check_vma=False
    )
```

```python
import functools
import math

import jax
import jax.numpy as jnp
from jax import lax
from jax.experimental import pallas as pl
from jax.experimental.pallas import tpu as pltpu
from jax.sharding import PartitionSpec as P

SHARPNESS = 200.0
MINUS_LOG2_E = -1.0 / math.log(2.0)
EDGE = 2.0 * math.cosh(0.5)
LANES = 128
DEPTH = 128
ZONE_TILE = 256
SHORT = pl.CostEstimate(flops=1, bytes_accessed=1, transcendentals=0)
VMEM = pl.BlockSpec(memory_space=pltpu.VMEM)
SMEM = pl.BlockSpec(memory_space=pltpu.SMEM)
F32 = jnp.float32
BF16 = jnp.bfloat16


def params():
    return pltpu.CompilerParams(vmem_limit_bytes=20 * 2**20)


def near(x):
    return pltpu.with_memory_space_constraint(x, pltpu.VMEM)


def call(kernel, name, outs, args, scratch=(), cost=None):
    return pl.pallas_call(
        kernel,
        in_specs=[VMEM] * len(args),
        out_specs=[VMEM] * len(outs),
        out_shape=[pltpu.MemorySpace.VMEM(shape, kind) for shape, kind in outs],
        scratch_shapes=list(scratch),
        compiler_params=params(),
        cost_estimate=cost,
        name=name,
    )(*[near(a) for a in args])


def open_kernel(
    hours_total, mine_ref, map_hbm, owner_hbm, wp_hbm, band_hbm, area_hbm, resp_hbm,
    rhs_ref, plan_ref, area_ref, resp_ref, loss_ref, slope_ref,
    map_ref, owner_ref, wp_ref, band_ref, zp_ref, acc_ref, sems, resp_sems,
):
    hours, width, zones = resp_ref.shape
    pieces = resp_sems.shape[0]
    span = hours // pieces
    small = [
        pltpu.make_async_copy(source, target, sems.at[i])
        for i, (source, target) in enumerate(
            (
                (map_hbm, map_ref),
                (owner_hbm, owner_ref),
                (wp_hbm, wp_ref),
                (band_hbm, band_ref),
                (area_hbm, area_ref),
            )
        )
    ]
    for copy in small:
        copy.start()
    large = []
    for i in range(pieces):
        part = pl.ds(i * span, span)
        large.append(
            pltpu.make_async_copy(resp_hbm.at[part], resp_ref.at[part], resp_sems.at[i])
        )
        large[-1].start()
    for copy in small:
        copy.wait()
    place = map_ref[...]
    row, lane = place // LANES, place % LANES

    def look(i, found):
        table = jnp.broadcast_to(owner_ref[pl.ds(i, 1), :], place.shape)
        here = jnp.take_along_axis(table, lane, axis=1, mode="promise_in_bounds")
        return jnp.where(row == i, here, found)

    plan = lax.fori_loop(0, owner_ref.shape[0], look, jnp.zeros_like(place), unroll=8)
    for r in range(plan.shape[0]):
        plan_ref[:, r * LANES : (r + 1) * LANES] = plan[r : r + 1, :]
    designs = wp_ref.shape[0]
    onehot = (
        lax.broadcasted_iota(jnp.int32, (designs, zones), 0) == plan_ref[...]
    ).astype(F32).astype(BF16)
    rest = wp_ref[...]
    exact = []
    for _ in range(3):
        exact.append(rest.astype(BF16))
        rest = rest - exact[-1].astype(F32)
    zp_ref[...] = lax.dot_general(
        jnp.concatenate(exact, axis=0),
        jnp.concatenate([onehot] * 3, axis=0),
        (((0,), (0,)), ((), ())),
        preferred_element_type=F32,
    )
    extra = lax.broadcasted_iota(jnp.int32, (16, zones), 0)
    blank = jnp.zeros((DEPTH - width - 16, zones), BF16)
    core, _ = here()
    acc_ref[...] = jnp.zeros_like(acc_ref)

    def pair_step(j, carry):
        depth = []
        for k in range(2):
            h = 2 * j + k
            coeff = (resp_ref[h].astype(F32) * zp_ref[...]).astype(BF16)
            middle = 0.25 * (band_ref[pl.ds(h, 1), :].astype(F32) - 3.5)
            tail = jnp.where(extra == 0, -middle, jnp.where(extra == 1, 1.0, 0.0))
            depth += [coeff, tail.astype(BF16), blank]
        rhs = jnp.concatenate(depth, axis=0)
        rhs_ref[j] = rhs
        pair = mine_ref[:, pl.ds(pl.multiple_of(j * LANES, LANES), LANES)]
        summed = pair_work("loss_slope", pair, lambda at: rhs[:, at], area_ref, slope_ref, j)
        acc_ref[...] += hour_weighted(summed, core, hours, hours_total, j)
        return carry

    for i in range(pieces):
        large[i].wait()
        lax.fori_loop(i * span // 2, (i + 1) * span // 2, pair_step, 0, unroll=span // 2)
    loss_ref[...] = jnp.broadcast_to(
        jnp.sum(acc_ref[...].T, axis=0, keepdims=True), loss_ref.shape
    )


def opening(
    mine, building_map, owner_ids, window_params, band_ids, floor_area, response, hours_total
):
    hours, width, zones = response.shape
    args = [
        building_map.reshape(-1, LANES),
        owner_ids.reshape(-1, LANES),
        window_params,
        band_ids,
        floor_area.reshape(1, zones),
        response,
    ]
    outs = [
        ((hours // 2, 2 * DEPTH, zones), BF16),
        ((1, zones), jnp.int32),
        ((1, zones), F32),
        (response.shape, BF16),
        ((8, mine.shape[0]), F32),
        ((hours, mine.shape[0], zones), BF16),
    ]
    return pl.pallas_call(
        functools.partial(open_kernel, hours_total),
        in_specs=[VMEM] + [pl.BlockSpec(memory_space=pl.ANY)] * len(args),
        out_specs=[VMEM] * len(outs),
        out_shape=[pltpu.MemorySpace.VMEM(shape, kind) for shape, kind in outs],
        scratch_shapes=[pltpu.VMEM(a.shape, a.dtype) for a in args[:4]]
        + [
            pltpu.VMEM((width, zones), F32),
            pltpu.VMEM((mine.shape[0], LANES), F32),
            pltpu.SemaphoreType.DMA((5,)),
            pltpu.SemaphoreType.DMA((2,)),
        ],
        compiler_params=params(),
        cost_estimate=SHORT,
        name="opening",
    )(near(mine), *[pltpu.with_memory_space_constraint(a, pltpu.HBM) for a in args])


def drivers(pair, second, fill):
    half = pair.shape[1] // 2
    lane = lax.broadcasted_iota(jnp.int32, pair.shape, 1)
    if second:
        pair = pltpu.roll(pair.astype(F32), half, 1).astype(BF16)
    rest = jnp.zeros(pair.shape, F32)
    for spot, value in enumerate(fill):
        rest = jnp.where(lane == half + spot, value, rest)
    return jnp.where(lane < half, pair, rest.astype(BF16))


def here():
    core = lax.axis_index("hour")
    return core, lax.axis_index("zone") * lax.axis_size("hour") + core


def occupancy(hour, hours_total):
    return 1.0 + 2.0 * hour.astype(F32) / (hours_total - 1)


def pair_work(kind, pair, rhs_at, area_ref, slope_ref, j):
    with_loss, with_slope = "loss" in kind, "slope" in kind
    zones = area_ref.shape[1]
    rows = pair.shape[0]
    fill = (0.5,) if with_loss else (0.5, 0.25)
    pair = (pair.astype(F32) * 0.5).astype(BF16)
    none = jnp.zeros(pair.shape, BF16)
    lhs = jnp.concatenate(
        [
            jnp.concatenate([drivers(pair, False, fill), none], axis=1),
            jnp.concatenate([none, drivers(pair, True, fill)], axis=1),
        ],
        axis=0,
    )
    summed = None
    for z in range(0, zones, ZONE_TILE):
        v = jnp.dot(lhs, rhs_at(slice(z, z + ZONE_TILE)), preferred_element_type=F32)
        if with_loss:
            a = jnp.abs(v) * (2.0 * MINUS_LOG2_E)
            q = jnp.exp2(a)
            pen = jnp.log2((q + EDGE) * q + 1.0) - a
            pen = pen * area_ref[:, z : z + ZONE_TILE]
            for c in range(0, ZONE_TILE, LANES):
                piece = pen[:, c : c + LANES]
                summed = piece if summed is None else summed + piece
        if with_slope:
            if with_loss:
                slope = jnp.tanh(v + 0.25) + jnp.tanh(v - 0.25)
            else:
                slope = jnp.tanh(v) + jnp.tanh(v - 0.5)
            slope = slope.astype(BF16)
            slope_ref[2 * j, :, z : z + ZONE_TILE] = slope[:rows]
            slope_ref[2 * j + 1, :, z : z + ZONE_TILE] = slope[rows:]
    return summed


def hour_weighted(summed, core, hours, hours_total, j):
    rows = summed.shape[0] // 2
    first = core * hours + 2 * j
    return summed[:rows] * occupancy(first, hours_total) + summed[rows:] * occupancy(
        first + 1, hours_total
    )


def scan_kernel(kind, hours_total, chunks, extra, order, priors, unroll, *refs):
    with_loss, with_slope, with_turn = "loss" in kind, "slope" in kind, "turn" in kind
    f_refs, refs = refs[:chunks], refs[chunks:]
    turn_refs, refs = [*refs[:extra], *f_refs], refs[extra:]
    rhs_ref, area_ref, refs = refs[0], refs[1], refs[2:]
    prior_refs, refs = refs[:priors], refs[priors:]
    if with_loss:
        out_ref, refs = refs[0], refs[1:]
    slope_ref = None
    if with_slope:
        slope_ref, refs = refs[0], refs[1:]
    if with_turn:
        ft_ref, refs = refs[0], refs[1:]
    if with_loss:
        acc_ref = refs[0]
        acc_ref[...] = jnp.zeros_like(acc_ref)
    pairs, _, zones = rhs_ref.shape
    hours = 2 * pairs
    core, me = here()

    def rows_of(parts, at):
        parts = [part[:, at] for part in parts]
        return parts[0] if len(parts) == 1 else jnp.concatenate(parts, axis=0)

    def pair_step(j, carry):
        at = pl.ds(pl.multiple_of(j * LANES, LANES), LANES)
        pair = rows_of(f_refs, at)
        if with_turn:
            ft_ref[at, :] = rows_of(turn_refs, at).T
        summed = pair_work(kind, pair, lambda at: rhs_ref[j, :, at], area_ref, slope_ref, j)
        if with_loss:
            acc_ref[...] += hour_weighted(summed, core, hours, hours_total, j)
        return carry

    lax.fori_loop(0, pairs, pair_step, 0, unroll=unroll)

    if with_loss:
        row = jnp.sum(acc_ref[...].T, axis=0, keepdims=True)
        if not priors:
            out_ref[...] = jnp.broadcast_to(row, out_ref.shape)
        else:
            known = [ref[0:1, :] for ref in prior_refs] + [row]
            chunk = sum(part.shape[1] for part in known) // len(order)
            pieces = [
                part[:, first : first + chunk]
                for part in known
                for first in range(0, part.shape[1], chunk)
            ]
            occ_sum = hours * 1.0 + (
                2.0 * (core * hours * hours + hours * (hours - 1) // 2)
            ).astype(F32) / (hours_total - 1)
            weight = jnp.sum(area_ref[...]) * occ_sum
            message = jnp.zeros(out_ref.shape, F32) + weight
            index = lax.broadcasted_iota(jnp.int32, message.shape, 0)
            blank = jnp.zeros((1, LANES - chunk), F32) + weight
            for m, piece in zip(order, pieces):
                piece = jnp.concatenate([piece, blank], axis=1)
                message = jnp.where(index == (me ^ m), piece, message)
            out_ref[...] = message


def scan(kind, rows_in, rhs, area, hours_total, order, extra=(), priors=(), unroll=12, cost=None):
    hours, zones = 2 * rhs.shape[0], rhs.shape[2]
    rows = sum(f.shape[0] for f in rows_in)
    outs = []
    scratch = []
    if "loss" in kind:
        sublanes = -(-len(order) // 8) * 8
        outs.append(((sublanes, LANES) if priors else (8, rows), F32))
        scratch.append(pltpu.VMEM((rows, LANES), F32))
    if "slope" in kind:
        outs.append(((hours, rows, zones), BF16))
    if "turn" in kind:
        outs.append(((rows_in[0].shape[1], rows + sum(f.shape[0] for f in extra)), BF16))
    return call(
        functools.partial(
            scan_kernel, kind, hours_total, len(rows_in), len(extra), order, len(priors), unroll
        ),
        kind,
        outs,
        [*rows_in, *extra, rhs, area, *priors],
        scratch,
        cost,
    )


def gradient_kernel(
    hours_total, gain, order, messages, *refs
):
    msg_refs, refs = refs[:messages], refs[messages:]
    ft_refs, slope_refs, refs = refs[:2], refs[2:6], refs[6:]
    resp_ref, area_ref, plan_ref, out_ref, acc_ref, score_ref, e_ref = refs
    hours, width, zones = resp_ref.shape
    core, me = here()
    sources = len(order)
    chunk = e_ref.shape[1] // sources
    total = [msg_ref[...] for msg_ref in msg_refs]
    while len(total) > 1:
        total = [first + second for first, second in zip(total[::2], total[1::2])]
    total = total[0]
    weight = jnp.max(total[0:1, chunk : chunk + 1])
    score = total * (SHARPNESS * math.log(2.0) / weight)
    rows = lax.broadcasted_iota(jnp.int32, score.shape, 0)
    lanes = lax.broadcasted_iota(jnp.int32, score.shape, 1)
    valid = (rows < sources) & (lanes < chunk)
    peak = jnp.max(jnp.where(valid, score, -jnp.inf))
    e = jnp.where(valid, jnp.exp(jnp.where(valid, score - peak, 0.0)), 0.0)
    exp_total = jnp.sum(e)
    score_ref[...] = e
    for spot, m in enumerate(order):
        piece = score_ref[pl.ds(me ^ m, 1), :]
        e_ref[:, spot * chunk : (spot + 1) * chunk] = piece[:, :chunk]
    acc_ref[...] = jnp.zeros_like(acc_ref)

    def hour_step(h, carry):
        occ = occupancy(core * hours + h, hours_total)
        at = pl.ds(pl.multiple_of(h * width, width), width)
        ft = jnp.concatenate([ref[at, :] for ref in ft_refs], axis=1).astype(F32)
        ft = ft * (e_ref[...] * occ)
        high = ft.astype(BF16)
        low = (ft - high.astype(F32)).astype(BF16)
        both = jnp.concatenate([high, low], axis=0)
        for z in range(0, zones, ZONE_TILE):
            at = slice(z, z + ZONE_TILE)
            kept = jnp.concatenate([ref[h, :, at] for ref in slope_refs], axis=0)
            mixed = jnp.dot(both, kept, preferred_element_type=F32)
            mixed = mixed[:width] + mixed[width:]
            acc_ref[:, at] += resp_ref[h, :, at].astype(F32) * mixed
        return carry

    lax.fori_loop(0, hours, hour_step, 0, unroll=hours // 2)

    grad = acc_ref[...] * area_ref[...]
    blocks, owners, _ = out_ref.shape
    index = lax.broadcasted_iota(jnp.int32, (blocks * owners, zones), 0)
    onehot = (index == plan_ref[...]).astype(F32).astype(BF16)
    sens = jnp.zeros((blocks * owners, width), F32)
    for _ in range(3):
        part = grad.astype(BF16)
        grad = grad - part.astype(F32)
        sens = sens + lax.dot_general(
            onehot, part, (((1,), (1,)), ((), ())), preferred_element_type=F32
        )
    sens = sens * (0.5 * gain / weight)
    for k in range(blocks):
        out_ref[k, :, :width] = sens[k * owners : (k + 1) * owners]
    lane = lax.broadcasted_iota(jnp.int32, (blocks, owners, LANES - width), 2)
    out_ref[:, :, width:] = jnp.where(lane == 0, peak, exp_total)


def finish_kernel(scen_parts, width, parts_ref, sens_ref, objective_ref):
    parts = parts_ref[...]
    devices = parts.shape[0]
    peaks = parts[:, :, width : width + 1]
    totals = parts[:, :, width + 1 : width + 2]
    peak = jnp.max(peaks)
    scale = jnp.exp(peaks - peak)
    total = jnp.sum((scale * totals)[:, 0:1, :]) * (scen_parts / devices)
    summed = jnp.sum(parts[:, :, :width] * scale, axis=0) / total
    sens_ref[...] = summed
    log_total = jnp.max(jnp.log(jnp.full((8, LANES), total, F32)))
    objective_ref[0] = (peak + log_total) / SHARPNESS - 0.5


def on_device(forcing, response, window_params, building_map, owner_ids, band_ids, floor_area):
    hours, width, zones = response.shape
    hour_parts = lax.axis_size("hour")
    zone_parts = lax.axis_size("zone")
    scen_parts = lax.axis_size("scen")
    hours_total = hours * hour_parts
    core = lax.axis_index("hour")
    sources = zone_parts * hour_parts

    half = hours * width
    everyone = forcing.reshape(forcing.shape[0], hours_total * width)
    keep = lax.dynamic_slice_in_dim(everyone, core * half, half, axis=1)
    leave = lax.dynamic_slice_in_dim(everyone, (1 - core) * half, half, axis=1)
    came = lax.ppermute(leave, "hour", [(0, 1), (1, 0)])

    def swap(x, step):
        return lax.ppermute(x, "zone", [(i, i ^ step) for i in range(zone_parts)])

    piece = sources // 8
    parts = [range(i, i + piece) for i in range(0, sources, piece)]
    own, near0, near1, far_a, far_b, final = (
        [*parts[0], *parts[1]], parts[2], parts[3], parts[4], parts[5], [*parts[6], *parts[7]]
    )
    worked = (*own, *far_a, *near0, *near1, *far_b, *final)
    kept = (*far_a, *near0, *near1, *far_b, *own, *final)
    if zone_parts == 4:
        mine = jnp.concatenate([keep, came], axis=0)
        far0, far1, beside = swap(keep, 2), swap(came, 2), swap(mine, 1)
    else:
        me = lax.axis_index(("zone", "hour"))
        both = jnp.where(core == 0, jnp.stack([keep, came]), jnp.stack([came, keep]))
        gathered = lax.all_gather(both, "zone", axis=0, tiled=True)
        ordered = jnp.take(gathered, me ^ jnp.arange(sources), axis=0).reshape(4, -1, half)
        mine, beside, far, last = ordered
        far0, far1 = far[: far.shape[0] // 2], far[far.shape[0] // 2 :]
    rhs, plan, area, near_response, loss0, slope0 = opening(
        mine, building_map, owner_ids, window_params, band_ids, floor_area, response, hours_total
    )
    common = (rhs, area, hours_total, worked)
    far0, loss0 = lax.optimization_barrier((far0, loss0))
    loss1, slope1 = scan("loss_slope", [far0], *common, cost=SHORT)
    if zone_parts == 4:
        far0, far1, loss1 = lax.optimization_barrier((far0, far1, loss1))
        last = swap(jnp.concatenate([far0, far1], axis=0), 1)
    loss2, slope2, ft0 = scan("loss_slope_turn", [beside, far1], *common, extra=[far0])
    (message,) = scan("loss", [last], *common, priors=[loss0, loss1, loss2])
    message = message + lax.ppermute(message, "hour", [(0, 1), (1, 0)])
    slope3, ft1 = scan("slope_turn", [last], *common, extra=[mine])
    if zone_parts == 4:
        others = [swap(message, k) for k in (3, 2, 1)]
        *others, slope3 = lax.optimization_barrier((*others, slope3))
        others = others[::-1]
        messages = [message, *others]
    else:
        messages = [lax.psum(message, "zone")]

    designs = window_params.shape[0]
    devices = zone_parts * scen_parts * hour_parts
    owners = designs // devices
    gain = math.sqrt(width * zones * zone_parts * hours_total * designs)
    (parts,) = call(
        functools.partial(gradient_kernel, hours_total, gain, kept, len(messages)),
        "gradient",
        [((devices, owners, LANES), F32)],
        [*messages, ft0, ft1, slope1, slope2, slope0, slope3, near_response, area, plan],
        [
            pltpu.VMEM((width, zones), F32),
            pltpu.VMEM(message.shape, F32),
            pltpu.VMEM((1, ft0.shape[1] + ft1.shape[1]), F32),
        ],
    )
    parts = lax.all_to_all(
        parts, ("zone", "scen", "hour"), split_axis=0, concat_axis=0, tiled=True
    )
    sensitivity, objective = pl.pallas_call(
        functools.partial(finish_kernel, scen_parts, width),
        in_specs=[VMEM],
        out_specs=[VMEM, SMEM],
        out_shape=[
            jax.ShapeDtypeStruct((owners, width), F32),
            jax.ShapeDtypeStruct((1,), F32),
        ],
        compiler_params=params(),
        name="finish",
    )(near(parts))
    return (sensitivity, objective)


def solution(mesh):
    in_specs = (
        P(("groups", "zone", "scen", "hour"), None, None),
        P("hour", None, ("groups", "zone")),
        P("groups", None),
        P(("groups", "zone")),
        P("groups"),
        P("hour", ("groups", "zone")),
        P(("groups", "zone")),
    )
    out_specs = (P(("groups", "zone", "scen", "hour"), None), P("groups"))
    return jax.shard_map(
        on_device, mesh=mesh, in_specs=in_specs, out_specs=out_specs, check_vma=False
    )
```
